1024 devices in a mesh: bl: 16 (over z), row: 8 (over x, y_hi), col: 8 (over y_lo, core).
Axes of the slice: x: 4, y: 8 (y_hi: 2, y_lo: 4; y = y_hi * 4 + y_lo), z: 16, core: 2. Of those that a mesh axis runs over, the one named last changes fastest.
Arguments:
- visibilities: bfloat16 [32768, 2, 1024], P(('bl', 'row', 'col')), may hold values from -6 to 6
- offsets: bfloat16 [32768, 2, 64], P(('bl', 'row', 'col')), may hold values from -6 to 6
- frequencies: float32 [16], replicated, may hold values from 0.8 to 1.2
- taper_curve: float32 [32], replicated, may hold values from 0.2 to 1
- owner_index: int32 [32768, 1], P(('bl', 'row', 'col')), may hold values from 0 to 63; in each aligned block of 32 rows (0 to 31, 32 to 63, ...) at most 2 rows name the same one
- tile_index: int32 [32768], P(('bl', 'row', 'col')), may hold values from 0 to 255
Outputs:
- dirty_rows: float32 [8, 128, 2, 16384], P('row', ('bl', 'col'))
The draws below stay inside these ranges and needn't reach their ends.
Inputs may be any that keep to these rules, and one draw needn't show every extreme that they name: `owner_index`: owner index is pencil row times 8 plus pencil column; among the 32 blocks of one device no owner is named more than 2 times, a bound that some block reaches.
All inputs are finite; a program needn't handle non-finite values.
Results may differ from the reference program's by a relative error of at most 0.0036.
Values may be sent and summed in bfloat16 or wider, within the bound.
A program may use at most 64 MiB of HBM per device.

```python
import math
import jax
import jax.numpy as jnp
import numpy as np
from jax import lax

SUB = 32
TIMES = 64
CHANS = 16
GC = 16384
GR = 1024
BLK_DEV = 32
BLOCKS = 32768
VIS = 1024
CAP = 2
TILES_OWN = 256
N_ROW = 8
N_COL = 8


def place_ends(entries, stream_key, least, largest):
    longest = entries.shape.index(max(entries.shape))
    spots = []
    for shift in (0, 1):
        where = [jax.random.randint(jax.random.fold_in(stream_key, axis), (), 0, length) for axis, length in enumerate(entries.shape)]
        where[longest] = (where[longest] + shift) % entries.shape[longest]
        spots.append(tuple(where))
    return entries.at[spots[0]].set(least).at[spots[1]].set(largest)


def levels(own_key, shape, cuts, least, top_value):
    gain, own = 1.0, jax.random.fold_in(own_key, 6)
    for position, blocks in cuts:
        heights = jnp.exp(jax.random.uniform(jax.random.fold_in(own, position), (blocks,), jnp.float32, least / len(cuts), top_value / len(cuts)))
        gain = gain * jnp.repeat(heights, shape[position] // blocks).reshape([-1 if axis == position else 1 for axis in range(len(shape))])
    return gain


def shared_out(own_key, own, number, rows, amount, top, bound, skew):
    ranking = jax.random.permutation(own_key, amount)
    crowded, usual = load_shares(amount, rows * top, bound, skew, True), load_shares(amount, rows * top, bound, skew, False)
    places = jnp.arange(amount)

    def named(lengths, rotation):
        used = int((lengths > 0).sum())
        fixed = max(1, used // 4)
        moved = fixed + (places - fixed + rotation * (used - fixed)) % max(1, amount - fixed)
        return jnp.zeros((amount,), jnp.int32).at[ranking[jnp.where(places < fixed, places, moved)]].set(jnp.asarray(lengths, jnp.int32))

    lengths = jnp.where(number % 4 == 0, named(crowded, number // 4), named(usual, number - number // 4 - 1))
    mixed = jax.random.permutation(jax.random.fold_in(own, 3), amount)
    source_of, sink = mixed[0:amount // 2 * 2:2], mixed[1:amount // 2 * 2:2]
    margin = jnp.minimum(lengths[source_of] - 1, bound - lengths[sink]) // 2
    margin = jnp.where((source_of == ranking[0]) | (sink == ranking[0]) | (lengths[sink] == 0), 0, jnp.maximum(margin, 0))
    moved = jax.random.randint(jax.random.fold_in(own, 4), (amount // 2,), 0, 1 << 20) % (margin + 1)
    lengths = lengths.at[source_of].add(-moved).at[sink].add(moved)
    labels = jnp.searchsorted(jnp.cumsum(lengths), jnp.arange(rows * top), side="right").astype(jnp.int32)
    listing = labels.reshape(top, rows).T
    listing = listing[jax.random.permutation(jax.random.fold_in(own, 1), rows)]
    rotation = jax.random.randint(jax.random.fold_in(own, 2), (rows, 1), 0, top)
    return jnp.take_along_axis(listing, (jnp.arange(top)[None, :] + rotation) % top, axis=1)


def load_shares(amount, total, reach, skew, full):
    weights = [(1 << 20) // math.isqrt(grade ** skew) + 1 for grade in range(1, amount + 1)]
    largest = reach if full else min(reach, max(-(-total // amount), total * weights[0] // sum(weights)))
    least = 1 if total - largest >= amount - 1 else 0
    counts, rest = [largest] + [least] * (amount - 1), total - largest - least * (amount - 1)
    while rest > 0:
        candidates = [i for i in range(1, amount) if counts[i] < largest] or [i for i in range(1, amount) if counts[i] < reach]
        pool, budget = sum([weights[i] for i in candidates]), rest
        for i in candidates:
            extra = min(reach - counts[i], max(1, budget * weights[i] // pool), rest)
            counts[i] = counts[i] + extra
            rest = rest - extra
    return np.array(counts)


def scatter_about(stream_key, extent, scale, limit, cuts=(), held_as=jnp.bfloat16):
    result = jax.random.normal(stream_key, extent, jnp.float32) * scale
    if len(cuts) > 0:
        result = levels(stream_key, extent, cuts, -0.22, 0.18) * result
    return jnp.clip(result, min=-limit, max=limit).astype(held_as)


def setup_inputs(seed: int = 0) -> dict:
    seeds = jax.random.split(jax.random.key(seed), 7)
    visibilities = scatter_about(seeds[0], (BLOCKS, 2, VIS), 1.0, 6.0, ((0, 1024),))
    offsets = jnp.clip(jax.random.uniform(seeds[1], (BLOCKS, 2, TIMES), jnp.float32, -6.0, 6.0) * levels(seeds[1], (BLOCKS, 2, TIMES), ((0, 1024),), -0.4, 0.0), -6.0, 6.0).astype(jnp.bfloat16)
    frequencies = jnp.clip(jax.random.uniform(seeds[2], (CHANS,), jnp.float32, 0.8, 1.2), 0.8, 1.2)
    taper_curve = jnp.clip(jnp.exp(jax.random.uniform(seeds[3], (SUB,), jnp.float32, math.log(0.2), math.log(1.0))), 0.2, 1.0)
    owner_index_keys = jax.random.split(jax.random.fold_in(seeds[4], 1), BLOCKS // BLK_DEV)
    owner_index_turns = jax.random.permutation(jax.random.fold_in(seeds[4], 3), BLOCKS // BLK_DEV)
    owner_index = jax.vmap(lambda own, number: shared_out(jax.random.fold_in(seeds[4], 2), own, number, BLK_DEV, N_ROW * N_COL, 1, CAP, 2))(owner_index_keys, owner_index_turns).reshape((BLOCKS, 1))
    tile_index = place_ends(jax.random.randint(seeds[5], (BLOCKS,), 0, TILES_OWN), jax.random.fold_in(seeds[5], 1), 0, TILES_OWN - 1).astype(jnp.int32)
    return {"visibilities": visibilities, "offsets": offsets, "frequencies": frequencies, "taper_curve": taper_curve, "owner_index": owner_index, "tile_index": tile_index}


def dft_tables(length):
    indices = jnp.arange(length, dtype=jnp.int32)
    product = indices[:, None] * indices[None, :] % length
    angles = 2.0 * math.pi / length * product.astype(jnp.float32)
    return (jnp.cos(angles), jnp.sin(angles))

def make_subgrids(visibilities, offsets, frequencies, taper_curve):
    block_count = visibilities.shape[0]
    time_count = offsets.shape[2]
    chan_count = frequencies.shape[0]
    sub_size = taper_curve.shape[0]
    shifted = offsets.astype(jnp.float32)
    scaled_u = (shifted[:, 0, :, None] * frequencies[None, None, :]).reshape(block_count, time_count * chan_count)
    scaled_v = (shifted[:, 1, :, None] * frequencies[None, None, :]).reshape(block_count, time_count * chan_count)
    pixels = jnp.arange(sub_size, dtype=jnp.float32) - float(sub_size // 2)
    phase_rows = 2.0 * math.pi / sub_size * scaled_u[:, :, None] * pixels[None, None, :]
    phase_cols = 2.0 * math.pi / sub_size * scaled_v[:, :, None] * pixels[None, None, :]
    vis_real = visibilities[:, 0, :, None].astype(jnp.float32)
    vis_imag = visibilities[:, 1, :, None].astype(jnp.float32)
    cos_rows = jnp.cos(phase_rows)
    sin_rows = jnp.sin(phase_rows)
    left_side = jnp.concatenate([vis_real * cos_rows - vis_imag * sin_rows, vis_real * sin_rows + vis_imag * cos_rows], axis=2).astype(jnp.bfloat16)
    right_side = jnp.concatenate([jnp.cos(phase_cols), jnp.sin(phase_cols)], axis=2).astype(jnp.bfloat16)
    left_side = lax.optimization_barrier(left_side).astype(jnp.float32)
    right_side = lax.optimization_barrier(right_side).astype(jnp.float32)
    product = jnp.einsum('nkl,nkm->nlm', left_side, right_side, precision=lax.Precision.HIGHEST)
    real_part = product[:, :sub_size, :sub_size] - product[:, sub_size:, sub_size:]
    imag_part = product[:, :sub_size, sub_size:] + product[:, sub_size:, :sub_size]
    weights = taper_curve[:, None] * taper_curve[None, :] / math.sqrt(time_count * chan_count)
    real_part = real_part * weights[None]
    imag_part = imag_part * weights[None]
    cos_table, sin_table = dft_tables(sub_size)
    highest = lax.Precision.HIGHEST
    first_real = jnp.einsum('pj,njm->npm', cos_table, real_part, precision=highest) + jnp.einsum('pj,njm->npm', sin_table, imag_part, precision=highest)
    first_imag = jnp.einsum('pj,njm->npm', cos_table, imag_part, precision=highest) - jnp.einsum('pj,njm->npm', sin_table, real_part, precision=highest)
    final_real = jnp.einsum('npm,qm->npq', first_real, cos_table, precision=highest) + jnp.einsum('npm,qm->npq', first_imag, sin_table, precision=highest)
    final_imag = jnp.einsum('npm,qm->npq', first_imag, cos_table, precision=highest) - jnp.einsum('npm,qm->npq', first_real, sin_table, precision=highest)
    stacked = jnp.stack([final_real, final_imag], axis=2) / float(sub_size)
    return stacked.reshape(block_count, sub_size * 2 * sub_size)

def reference(visibilities, offsets, frequencies, taper_curve, owner_index, tile_index):
    group_count = visibilities.shape[0] // BLK_DEV
    tiles_down = GR // N_ROW // SUB
    tiles_across = GC // N_COL // SUB
    grid_across = GC // SUB
    total_tiles = GR // SUB * grid_across

    def accumulate(carry, packet):
        vis_group, off_group, own_group, til_group = packet
        subgrids = make_subgrids(vis_group, off_group, frequencies, taper_curve)
        pencil_row = own_group[:, 0] // N_COL
        pencil_col = own_group[:, 0] % N_COL
        global_row = pencil_row * tiles_down + til_group // tiles_across
        global_col = pencil_col * tiles_across + til_group % tiles_across
        placed = (global_row * grid_across + global_col).astype(jnp.int32)
        return (carry.at[placed].add(subgrids), None)
    packets = (visibilities.reshape(group_count, BLK_DEV, 2, VIS), offsets.reshape(group_count, BLK_DEV, 2, TIMES), owner_index.reshape(group_count, BLK_DEV, 1), tile_index.reshape(group_count, BLK_DEV))
    initial = jnp.zeros((total_tiles, SUB * 2 * SUB), jnp.float32)
    tiles_sum, _ = lax.scan(accumulate, initial, packets)
    grid = tiles_sum.reshape(GR // SUB, grid_across, SUB, 2, SUB).transpose(0, 2, 3, 1, 4).reshape(GR, 2, GC)
    complex_grid = grid[:, 0, :] + 1j * grid[:, 1, :]
    transformed = jnp.fft.ifft(complex_grid, axis=-1, norm='ortho')
    dirty_rows = jnp.stack([jnp.real(transformed), jnp.imag(transformed)], axis=1).astype(jnp.float32)
    return dirty_rows.reshape(N_ROW, GR // N_ROW, 2, GC)
```

```python
import math

import jax
import jax.numpy as jnp
import numpy as np
from jax import lax
from jax.experimental import pallas as pl
from jax.experimental.pallas import tpu as pltpu
from jax.sharding import PartitionSpec as P

MESH = pl.DeviceIdType.MESH
SUB = 32
GC = 16384
TILES = GC // SUB
GROUP = 64
F32 = jnp.float32
BF16 = jnp.bfloat16


def split_np(table):
    high = table.astype(BF16)
    low = (table - high.astype(np.float64)).astype(BF16)
    return np.stack([high, low])


def make_tables():
    index = np.arange(SUB)
    angle = 2.0 * np.pi * (index[:, None] * index[None, :] % SUB) / SUB
    cos, sin = np.cos(angle), np.sin(angle)
    rows = np.zeros((2, 4, SUB, 4, 2, SUB))
    for b in range(4):
        rows[0, b, :, b, 0], rows[0, b, :, b, 1] = cos, sin
        rows[1, b, :, b, 0], rows[1, b, :, b, 1] = -sin, cos
    rows = rows.reshape(256, 256)
    from_real = np.block([[cos, -sin], [sin, cos]])
    from_imag = np.block([[sin, cos], [-cos, sin]])
    cols = np.zeros((2, 2, 256, 128))
    for half in range(2):
        cols[half, 0, :, half * 64 : half * 64 + 64] = np.tile(from_real, (4, 1))
        cols[half, 1, :, half * 64 : half * 64 + 64] = np.tile(from_imag, (4, 1))
    cols = cols.reshape(4, 256, 128)
    wide = np.arange(TILES)
    wide_angle = 2.0 * np.pi * (wide[:, None] * wide[None, :] % TILES) / TILES
    wide_table = np.concatenate([np.cos(wide_angle), np.sin(wide_angle)], axis=1)
    twist_angle = 2.0 * np.pi * (index[:, None] * wide[None, :]) / GC
    twist = (np.stack([np.cos(twist_angle), np.sin(twist_angle)]) / 128.0).astype(np.float32)
    last = np.block([[cos, -sin], [sin, cos]])
    return split_np(rows), split_np(cols), split_np(wide_table), twist, split_np(last)


def dot(a, b):
    return lax.dot_general(a, b, (((1,), (0,)), ((), ())), preferred_element_type=F32)


def dot_t(a, b):
    return lax.dot_general(a, b, (((1,), (1,)), ((), ())), preferred_element_type=F32)


def split(x):
    high = x.astype(BF16)
    return high, (x - high.astype(F32)).astype(BF16)


def cmul(ar, ai, br, bi):
    return ar * br - ai * bi, ar * bi + ai * br


def phasors(off_ref, freq_ref, z_ref):
    spread = (
        lax.broadcasted_iota(jnp.int32, (64, 1024), 1) // 16
        == lax.broadcasted_iota(jnp.int32, (64, 1024), 0)
    ).astype(F32).astype(BF16)
    scaled = dot(off_ref[...], spread) * freq_ref[...]
    theta = scaled * (2.0 * math.pi / SUB)
    square = theta * theta
    cos, sin = jnp.full_like(square, 1.0 / math.factorial(14)), jnp.full_like(
        square, 1.0 / math.factorial(15)
    )
    for order in range(6, -1, -1):
        sign = 1.0 if order % 2 == 0 else -1.0
        if order == 6:
            cos, sin = -cos, -sin
        cos = cos * square + sign / math.factorial(2 * order)
        sin = sin * square + sign / math.factorial(2 * order + 1)
    real, imag = cos, sin * theta
    for e in range(5):
        z_ref[e, 0], z_ref[e, 1] = real, imag
        if e < 4:
            real, imag = real * real - imag * imag, 2.0 * real * imag


def powers(base_r, base_i, z8, z16):
    parts = [
        cmul(base_r, base_i, z16[0], -z16[1]),
        cmul(base_r, base_i, z8[0], -z8[1]),
        (base_r, base_i),
        cmul(base_r, base_i, z8[0], z8[1]),
    ]
    real = jnp.concatenate([part[0] for part in parts], axis=0)
    imag = jnp.concatenate([part[1] for part in parts], axis=0)
    return jnp.concatenate([real, imag], axis=0).astype(BF16)


def block_sides(block, slot, vis_ref, z_ref, left_ref, right_ref):
    chunk = 256
    sub = lax.broadcasted_iota(jnp.int32, (8, chunk), 0)
    rows = pl.ds(pl.multiple_of(slot * 64, 64), 64)
    for start in range(0, 1024, chunk):
        lanes = pl.ds(start, chunk)
        for side in range(2):
            row = pl.ds(2 * block + side, 1)

            def z(e):
                return [jnp.broadcast_to(z_ref[e, part, row, lanes], (8, chunk)) for part in (0, 1)]

            base_r, base_i = jnp.where(sub & 1, z(0)[0], 1.0), jnp.where(sub & 1, z(0)[1], 0.0)
            for e in (1, 2):
                bit = (sub & (1 << e)) != 0
                zr, zi = z(e)
                base_r, base_i = cmul(
                    base_r, base_i, jnp.where(bit, zr, 1.0), jnp.where(bit, zi, 0.0)
                )
            if side == 0:
                vis = vis_ref[block, :, lanes].astype(F32)
                base_r, base_i = cmul(base_r, base_i, vis[0:1], vis[1:2])
            target = left_ref if side == 0 else right_ref
            target[rows, lanes] = powers(base_r, base_i, z(3), z(4))


def subgrids(vis_ref, w_ref, rows_ref, cols_ref, z_ref, left_ref, right_ref, sub_ref):
    def pair(gp, _):
        def one(slot, _):
            block_sides(gp * 8 + slot, slot, vis_ref, z_ref, left_ref, right_ref)
            return 0

        lax.fori_loop(0, 8, one, 0)
        total = jnp.zeros((128, 128), F32)
        for half in range(2):
            four = slice(half * 256, half * 256 + 256)
            image = dot_t(left_ref[four], right_ref[four]) * w_ref[...]
            high, low = split(image)
            first = dot(rows_ref[0], high) + dot(rows_ref[0], low) + dot(rows_ref[1], high)
            high, low = split(first)
            for part in range(2):
                use = slice(part * 128, part * 128 + 128)
                k = 2 * half + part
                total += dot(high[use], cols_ref[0, k]) + dot(low[use], cols_ref[0, k])
                total += dot(high[use], cols_ref[1, k])
        for b in range(4):
            sub_ref[pl.ds(gp * 4 + b, SUB, stride=16), :] = total[b * 32 : b * 32 + 32]
        return 0

    lax.fori_loop(0, 4, pair, 0)


def column_transform(grid, wide_ref, twist_ref, last_ref):
    high, low = split(grid)
    wide = dot(high, wide_ref[0]) + dot(low, wide_ref[0]) + dot(high, wide_ref[1])
    real = wide[:SUB, :TILES] - wide[SUB:, TILES:]
    imag = wide[SUB:, :TILES] + wide[:SUB, TILES:]
    real, imag = cmul(real, imag, twist_ref[0], twist_ref[1])
    high, low = split(jnp.concatenate([real, imag], axis=0))
    return dot(last_ref[0], high) + dot(last_ref[0], low) + dot(last_ref[1], high)


def kernel(
    vis_ref,
    off_ref,
    freq_ref,
    w_ref,
    place_ref,
    rows_ref,
    cols_ref,
    wide_hbm,
    twist_ref,
    last_ref,
    out_ref,
    z_ref,
    left_ref,
    right_ref,
    sub_ref,
    send_ref,
    got_ref,
    places_ref,
    data_ref,
    onehot_ref,
    masked_ref,
    own_ref,
    xsend_ref,
    xgot_ref,
    zsend_ref,
    zgot_ref,
    wide_ref,
    local_sem,
    psend_sem,
    pgot_sem,
    ssend_sem,
    sgot_sem,
    xsend_sem,
    xgot_sem,
    zsend_sem,
    zgot_sem,
):
    bl, row, col = lax.axis_index("bl"), lax.axis_index("row"), lax.axis_index("col")
    high_z, low_z = bl // 4, bl % 4
    x, y_hi = row // 2, row % 2
    me = y_hi * 32 + low_z * 8 + col

    def member(slot):
        return (high_z * 4 + slot % 32 // 8, x * 2 + slot // 32, slot % 8)

    def along_x(step):
        return (bl, (x + step) % 4 * 2 + y_hi, col)

    def along_z(step):
        return ((high_z + step) % 4 * 4 + low_z, row, col)

    barrier = pltpu.get_barrier_semaphore()

    def greet(step, _):
        pl.semaphore_signal(
            barrier, inc=1, device_id=member((me + step) % GROUP), device_id_type=MESH
        )
        return 0

    lax.fori_loop(1, GROUP, greet, 0)
    for step in range(1, 4):
        pl.semaphore_signal(barrier, inc=1, device_id=along_x(step), device_id_type=MESH)
        pl.semaphore_signal(barrier, inc=1, device_id=along_z(step), device_id_type=MESH)
    wide_copy = pltpu.make_async_copy(wide_hbm, wide_ref, local_sem)
    wide_copy.start()

    phasors(off_ref, freq_ref, z_ref)
    pl.semaphore_wait(barrier, GROUP - 1 + 6)

    def place_copy(step):
        return pltpu.make_async_remote_copy(
            src_ref=place_ref,
            dst_ref=places_ref.at[me],
            send_sem=psend_sem.at[step],
            recv_sem=pgot_sem.at[me],
            device_id=member((me + step) % GROUP),
            device_id_type=MESH,
        )

    def sub_copy(step):
        slot = (me + step) % GROUP
        return pltpu.make_async_remote_copy(
            src_ref=send_ref.at[slot % 32],
            dst_ref=got_ref.at[me],
            send_sem=ssend_sem.at[step],
            recv_sem=sgot_sem.at[me],
            device_id=member(slot),
            device_id_type=MESH,
        )

    def start(copy):
        def body(step, _):
            copy(step).start()
            return 0

        lax.fori_loop(1, GROUP, body, 0)

    def finish_sends(copy):
        def body(step, _):
            copy(step).wait_send()
            return 0

        lax.fori_loop(1, GROUP, body, 0)

    def finish_gets(buffer, sem):
        def body(step, _):
            slot = (me + step) % GROUP
            pltpu.make_async_copy(buffer.at[slot], buffer.at[slot], sem.at[slot]).wait()
            return 0

        lax.fori_loop(1, GROUP, body, 0)

    start(place_copy)
    places_ref[me] = place_ref[...]
    subgrids(vis_ref, w_ref, rows_ref, cols_ref, z_ref, left_ref, right_ref, sub_ref)
    send_ref[...] = sub_ref[...].astype(BF16).reshape(SUB, 16, 128)
    start(sub_copy)
    got_ref[me] = send_ref[me % 32]

    finish_gets(places_ref, pgot_sem)
    diagonal = (
        lax.broadcasted_iota(jnp.int32, (8, 128), 1) // 16
        == lax.broadcasted_iota(jnp.int32, (8, 128), 0)
    )
    tile_rows = []
    for k in range(16):
        pieces = places_ref[pl.ds(k // 2 * 8, 8), k % 2, :]
        place = jnp.sum(jnp.where(diagonal, pieces, 0), axis=0, keepdims=True)
        tile_rows.append(place // TILES)
        onehot_ref[:, pl.ds(k * 128, 128)] = (
            (lax.broadcasted_iota(jnp.int32, (TILES, 128), 0) == place % TILES)
            .astype(F32)
            .astype(BF16)
        )
    tile_row = jnp.concatenate(tile_rows, axis=1)

    finish_gets(got_ref, sgot_sem)
    for k in range(8):
        turned = got_ref[pl.ds(k * 8, 8)].reshape(128, 128).astype(F32).T.astype(BF16)
        data_ref[:, pl.ds(k * 256, 128)] = turned[:64]
        data_ref[:, pl.ds(k * 256 + 128, 128)] = turned[64:]

    def x_copy(turn, step):
        return pltpu.make_async_remote_copy(
            src_ref=xsend_ref.at[turn, step - 1],
            dst_ref=xgot_ref.at[turn, step - 1],
            send_sem=xsend_sem.at[turn, step - 1],
            recv_sem=xgot_sem.at[turn, step - 1],
            device_id=along_x(step),
            device_id_type=MESH,
        )

    def z_copy(turn):
        return pltpu.make_async_remote_copy(
            src_ref=zsend_ref.at[turn],
            dst_ref=zgot_ref.at[turn],
            send_sem=zsend_sem.at[turn],
            recv_sem=zgot_sem.at[turn],
            device_id=along_z((2, 1, 3)[turn]),
            device_id_type=MESH,
        )

    for turn in range(4):
        td = (high_z + (2, 1, 3, 0)[turn]) % 4
        for step in range(4):
            wanted = ((x + step) % 4 * 2 + y_hi) * 4 + td
            masked_ref[pl.ds(step * 64, 64), :] = jnp.where(
                tile_row == wanted, data_ref[...].astype(F32), 0.0
            ).astype(BF16)
        placed = dot_t(masked_ref[...], onehot_ref[...])
        own_ref[turn] = placed[:64]
        for step in (2, 1, 3):
            xsend_ref[turn, step - 1] = placed[step * 64 : step * 64 + 64].astype(BF16)
            x_copy(turn, step).start()

    for turn in range(4):
        total = own_ref[turn]
        for step in range(1, 4):
            x_copy(turn, step).wait_recv()
            total += xgot_ref[turn, step - 1].astype(F32)
        if turn < 3:
            zsend_ref[turn] = total.astype(BF16)
            z_copy(turn).start()
        else:
            own_ref[turn] = total

    finish_sends(place_copy)
    finish_sends(sub_copy)
    for turn in range(4):
        for step in range(1, 4):
            x_copy(turn, step).wait_send()
    wide_copy.wait()
    grid = own_ref[3]
    for turn in range(3):
        z_copy(turn).wait_recv()
        grid += zgot_ref[turn].astype(F32)
    out_ref[...] = column_transform(grid, wide_ref, twist_ref, last_ref)
    for turn in range(3):
        z_copy(turn).wait_send()


def on_device(visibilities, offsets, frequencies, taper_curve, owner_index, tile_index):
    rows, cols, wide, twist, last = make_tables()
    mask = np.kron(np.eye(4), np.ones((64, 64))).astype(np.float32) / 1024.0
    taper = jnp.tile(taper_curve, 8)
    weights = taper[:, None] * taper[None, :] * mask
    owner = owner_index[:, 0]
    place = (owner // 8 * 4 + tile_index // 64) * TILES + owner % 8 * 64 + tile_index % 64
    place = place.reshape(4, 2, 4).transpose(1, 0, 2).reshape(2, 1, 16)
    place = jnp.broadcast_to(place, (2, 8, 16)).reshape(2, 128)
    vmem = pl.BlockSpec(memory_space=pltpu.VMEM)
    result = pl.pallas_call(
        kernel,
        out_shape=jax.ShapeDtypeStruct((64, TILES), F32),
        in_specs=[vmem] * 7 + [pl.BlockSpec(memory_space=pl.ANY)] + [vmem] * 2,
        out_specs=vmem,
        scratch_shapes=[
            pltpu.VMEM((5, 2, 64, 1024), F32),
            pltpu.VMEM((512, 1024), BF16),
            pltpu.VMEM((512, 1024), BF16),
            pltpu.VMEM((512, 128), F32),
            pltpu.VMEM((SUB, 16, 128), BF16),
            pltpu.VMEM((GROUP, 16, 128), BF16),
            pltpu.VMEM((GROUP, 2, 128), jnp.int32),
            pltpu.VMEM((64, 2048), BF16),
            pltpu.VMEM((TILES, 2048), BF16),
            pltpu.VMEM((256, 2048), BF16),
            pltpu.VMEM((4, 64, TILES), F32),
            pltpu.VMEM((4, 3, 64, TILES), BF16),
            pltpu.VMEM((4, 3, 64, TILES), BF16),
            pltpu.VMEM((3, 64, TILES), BF16),
            pltpu.VMEM((3, 64, TILES), BF16),
            pltpu.VMEM((2, TILES, 2 * TILES), BF16),
            pltpu.SemaphoreType.DMA,
            pltpu.SemaphoreType.DMA((GROUP,)),
            pltpu.SemaphoreType.DMA((GROUP,)),
            pltpu.SemaphoreType.DMA((GROUP,)),
            pltpu.SemaphoreType.DMA((GROUP,)),
            pltpu.SemaphoreType.DMA((4, 3)),
            pltpu.SemaphoreType.DMA((4, 3)),
            pltpu.SemaphoreType.DMA((3,)),
            pltpu.SemaphoreType.DMA((3,)),
        ],
        compiler_params=pltpu.CompilerParams(
            collective_id=0, has_side_effects=True, vmem_limit_bytes=40 * 1024 * 1024
        ),
    )(
        visibilities,
        offsets.reshape(64, 64),
        jnp.tile(frequencies, 64).reshape(1, 1024),
        weights,
        place,
        jnp.asarray(rows),
        jnp.asarray(cols),
        jnp.asarray(wide),
        jnp.asarray(twist),
        jnp.asarray(last),
    )
    return result.reshape(1, 1, 2, GC)


def solution(mesh):
    in_specs = (
        P(("bl", "row", "col"), None, None),
        P(("bl", "row", "col"), None, None),
        P(),
        P(),
        P(("bl", "row", "col"), None),
        P(("bl", "row", "col")),
    )
    out_specs = P("row", ("bl", "col"), None, None)
    return jax.shard_map(
        on_device, mesh=mesh, in_specs=in_specs, out_specs=out_specs, check_vma=False
    )
```

```python
import math

import jax
import jax.numpy as jnp
import numpy as np
from jax import lax
from jax.experimental import pallas as pl
from jax.experimental.pallas import tpu as pltpu
from jax.sharding import PartitionSpec as P

MESH = pl.DeviceIdType.MESH
SUB = 32
GC = 16384
TILES = GC // SUB
GROUP = 64
F32 = jnp.float32
BF16 = jnp.bfloat16


def split_np(table):
    high = table.astype(BF16)
    low = (table - high.astype(np.float64)).astype(BF16)
    return np.stack([high, low])


def by_lanes(table):
    rows, lanes = table.shape[-2:]
    pieces = table.reshape(table.shape[:-1] + (lanes // 128, 128))
    return np.ascontiguousarray(np.moveaxis(pieces, -2, -3))


def joined(ref, *index):
    return jnp.concatenate([ref[(*index, k)] for k in range(ref.shape[-3])], axis=1)


def make_tables():
    index = np.arange(SUB)
    angle = 2.0 * np.pi * (index[:, None] * index[None, :] % SUB) / SUB
    cos, sin = np.cos(angle), np.sin(angle)
    order = pixel_order()
    cos_in, sin_in = cos[:, order], sin[:, order]
    rows = np.zeros((2, 4, SUB, 4, 2, SUB))
    for b in range(4):
        rows[0, b, :, b, 0], rows[0, b, :, b, 1] = cos_in, sin_in
        rows[1, b, :, b, 0], rows[1, b, :, b, 1] = sin_in, -cos_in
    rows = split_np(rows.reshape(2, 128, 256))
    cos_in, sin_in = cos[order], sin[order]
    cols = np.block([[cos_in, -sin_in, -sin_in, -cos_in], [sin_in, cos_in, cos_in, -sin_in]])
    cols = split_np(np.tile(cols, (2, 1)))
    cols = np.concatenate([cols[0], cols[0], cols[1]])
    wide = np.arange(TILES)
    wide_angle = 2.0 * np.pi * (wide[:, None] * wide[None, :] % TILES) / TILES
    wide_table = np.concatenate([np.cos(wide_angle), np.sin(wide_angle)], axis=1)
    twist_angle = 2.0 * np.pi * (index[:, None] * wide[None, :]) / GC
    twist = (np.stack([np.cos(twist_angle), np.sin(twist_angle)]) / 128.0).astype(np.float32)
    last = np.block([[cos, -sin], [sin, cos]])
    return (
        by_lanes(rows),
        cols,
        by_lanes(split_np(wide_table)),
        twist,
        split_np(last),
    )


def dot(a, b):
    return lax.dot_general(a, b, (((1,), (0,)), ((), ())), preferred_element_type=F32)


def dot_t(a, b):
    return lax.dot_general(a, b, (((1,), (1,)), ((), ())), preferred_element_type=F32)


def split(x):
    high = x.astype(BF16)
    return high, (x - high.astype(F32)).astype(BF16)


def cmul(ar, ai, br, bi):
    return ar * br - ai * bi, ar * bi + ai * br


def three(x, rows):
    high = x.astype(BF16).astype(F32)
    middle = (x - high).astype(BF16).astype(F32)
    low = x - high - middle
    place = lax.broadcasted_iota(jnp.int32, (rows, x.shape[1]), 0)
    parts = jnp.where(place == 0, high, jnp.where(place == 1, middle, jnp.where(place == 2, low, 0.0)))
    return parts.astype(BF16)


def matches(shape, left, right):
    row, lane = lax.broadcasted_iota(jnp.int32, shape, 0), lax.broadcasted_iota(jnp.int32, shape, 1)
    return (left(row) == right(lane)).astype(F32).astype(BF16)


def pixel(k):
    slot = k % SUB
    return 16 + jnp.where(slot < 16, slot, jnp.where(slot == 16, -16, 16 - slot))


def weights(taper_ref, w_ref):
    parts = three(taper_ref[...], 16)
    along = dot(parts, matches((SUB, 128), lambda i: i, pixel))
    down = dot_t(matches((64, SUB), pixel, lambda k: k), parts)
    along, down = jnp.sum(along, axis=0, keepdims=True), jnp.sum(down, axis=1, keepdims=True)
    lane = lax.broadcasted_iota(jnp.int32, (64, 128), 1) // 64
    for half in range(2):
        w_ref[half] = jnp.where(lane == half, down * along * (1.0 / 1024.0), 0.0)


def places(owner_ref, tile_ref, place_ref):
    row = lax.broadcasted_iota(jnp.int32, (16, SUB), 0)
    parts = jnp.where(row == 0, owner_ref[...], jnp.where(row == 1, tile_ref[...], 0))
    order = matches(
        (SUB, 256), lambda i: i, lambda k: k % 16 // 4 * 8 + k // 128 * 4 + k % 4
    )
    both = dot(parts.astype(F32).astype(BF16), order).astype(jnp.int32)
    owner, tile = both[0:1], both[1:2]
    place_ref[...] = (owner // 8 * 4 + tile // 64) * TILES + owner % 8 * 64 + tile % 64


def phasors(off_ref, freq_ref, base_ref, far_ref):
    spread = matches((64, 1024), lambda i: i, lambda k: k // 16)
    repeat = matches((16, 1024), lambda i: i, lambda k: k % 16)
    freq = jnp.sum(dot(three(freq_ref[...], 16), repeat), axis=0, keepdims=True)
    scaled = dot(off_ref[...], spread) * freq
    theta = scaled * (2.0 * math.pi / SUB)
    square = theta * theta
    cos = jnp.full_like(square, -1.0 / math.factorial(14))
    sin = jnp.full_like(square, -1.0 / math.factorial(15))
    for order in range(6, -1, -1):
        sign = 1.0 if order % 2 == 0 else -1.0
        cos = cos * square + sign / math.factorial(2 * order)
        sin = sin * square + sign / math.factorial(2 * order + 1)
    z = [(jnp.ones_like(cos), jnp.zeros_like(cos)), (cos, sin * theta)]
    for p in range(2, 8):
        z.append(cmul(*z[p // 2], *z[p - p // 2]))
    for p in range(8):
        for part in range(2):
            for k in range(8):
                base_ref[part, k, pl.ds(p * 65, 64)] = z[p][part][:, k * 128 : k * 128 + 128]
    z8 = cmul(*z[4], *z[4])
    for e, value in enumerate((z8, cmul(*z8, *z8))):
        for part in range(2):
            far_ref[e, part] = value[part]


def pixel_order():
    slot = np.arange(SUB)
    return 16 + np.where(slot < 16, slot, np.where(slot == 16, -16, 16 - slot))


def block_sides(block, slot, vis_ref, base_ref, far_ref, left_ref, right_ref):
    chunk = 256
    first = lax.broadcasted_iota(jnp.int32, (8, chunk), 0) == 0
    for start in range(0, 1024, chunk):
        lanes = pl.ds(start, chunk)
        for side, target in enumerate((left_ref, right_ref)):
            row = 2 * block + side
            low = [
                jnp.concatenate(
                    [
                        base_ref[part, start // 128 + k, pl.ds(row, 8, stride=65), :]
                        for k in range(chunk // 128)
                    ],
                    axis=1,
                )
                for part in (0, 1)
            ]
            far = [
                [jnp.broadcast_to(far_ref[e, part, pl.ds(row, 1), lanes], (8, chunk)) for part in (0, 1)]
                for e in (0, 1)
            ]
            near = (low, cmul(*low, *far[0]))
            if side == 0:
                vis = vis_ref[block, :, lanes].astype(F32)
                vr, vi = (jnp.broadcast_to(vis[k : k + 1], (8, chunk)) for k in (0, 1))
                products = [(vr * c, vi * s, vr * s, vi * c) for c, s in near]
                plus = [(a - b, d + e) for a, b, d, e in products]
                minus = [(a + b, e - d) for a, b, d, e in products]
                last = cmul(vr, vi, far[1][0], -far[1][1])
            else:
                plus, minus = near, [(c, -s) for c, s in near]
                last = (far[1][0], -far[1][1])
            minus[0] = tuple(jnp.where(first, x, y) for x, y in zip(last, minus[0]))
            for part in range(2):
                for k, pieces in enumerate((plus, minus)):
                    rows = pl.ds(slot * 64 + part * 32 + k * 16, 16)
                    target[rows, lanes] = jnp.concatenate(
                        [piece[part] for piece in pieces], axis=0
                    ).astype(BF16)


def subgrids(vis_ref, w_ref, rows_ref, cols_ref, base_ref, far_ref, side_refs, image_ref, sub_ref):
    def sides(four, which):
        for b in range(4):
            block_sides(four * 4 + b, b, vis_ref, base_ref, far_ref, *side_refs[which])

    def image(four, which):
        left_ref, right_ref = side_refs[which]
        product = dot_t(left_ref[...], right_ref[...])
        for b in range(4):
            block = product[b * 64 : b * 64 + 64, b // 2 * 128 : b // 2 * 128 + 128] * w_ref[b % 2]
            high, low = split(block)
            rows = pl.ds(four * 256 + b * 64, 64)
            image_ref[rows, 0:128], image_ref[rows, 128:256] = high, low

    sides(0, 0)

    def pair(gp, _):
        sides(2 * gp + 1, 1)
        image(2 * gp, 0)
        sides(jnp.minimum(2 * gp + 2, 7), 0)
        image(2 * gp + 1, 1)
        return 0

    lax.fori_loop(0, 4, pair, 0)
    lower = lax.broadcasted_iota(jnp.int32, (256, 128), 1) < 64
    for half in range(2):
        image = image_ref[half * 1024 : half * 1024 + 1024]
        turned = dot(image, cols_ref[pl.ds(0, 256)]) + dot(image[:, :128], cols_ref[pl.ds(256, 128)])
        straight, crossed = [], []
        for k in range(2):
            even, odd = turned[k * 512 : k * 512 + 256], turned[k * 512 + 256 : k * 512 + 512]
            straight.append(jnp.where(lower, even, pltpu.roll(odd, 64, 1)))
            crossed.append(jnp.where(lower, pltpu.roll(even, 64, 1), odd))
        total = 0.0
        for part, pieces in enumerate((straight, crossed)):
            high, low = split(jnp.concatenate(pieces, axis=1))
            rows_high, rows_low = joined(rows_ref, 0, part), joined(rows_ref, 1, part)
            total += dot(rows_high, high) + dot(rows_high, low) + dot(rows_low, high)
        for k in range(2):
            for b in range(4):
                sub_ref[pl.ds((half * 2 + k) * 4 + b, SUB, stride=17), :] = total[
                    b * 32 : b * 32 + 32, k * 128 : k * 128 + 128
                ]


def column_transform(grid, wide_ref, twist_ref, last_ref):
    high, low = split(grid)
    wide_high, wide_low = joined(wide_ref, 0), joined(wide_ref, 1)
    wide = dot(high, wide_high) + dot(low, wide_high) + dot(high, wide_low)
    real = wide[:SUB, :TILES] - wide[SUB:, TILES:]
    imag = wide[SUB:, :TILES] + wide[:SUB, TILES:]
    real, imag = cmul(real, imag, twist_ref[0], twist_ref[1])
    high, low = split(jnp.concatenate([real, imag], axis=0))
    return dot(last_ref[0], high) + dot(last_ref[0], low) + dot(last_ref[1], high)


def kernel(
    vis_hbm,
    off_hbm,
    freq_hbm,
    taper_hbm,
    owner_hbm,
    tile_hbm,
    rows_hbm,
    cols_hbm,
    wide_hbm,
    twist_hbm,
    last_hbm,
    out_ref,
    vis_ref,
    off_ref,
    freq_ref,
    taper_ref,
    owner_ref,
    tile_ref,
    rows_ref,
    cols_ref,
    wide_ref,
    twist_ref,
    last_ref,
    w_ref,
    place_ref,
    base_ref,
    far_ref,
    left_a_ref,
    right_a_ref,
    left_b_ref,
    right_b_ref,
    image_ref,
    sub_ref,
    send_ref,
    got_ref,
    places_ref,
    data_ref,
    onehot_ref,
    masked_ref,
    own_ref,
    xsend_ref,
    xgot_ref,
    zsend_ref,
    zgot_ref,
    local_sem,
    psend_sem,
    pgot_sem,
    ssend_sem,
    sgot_sem,
    xsend_sem,
    xgot_sem,
    zsend_sem,
    zgot_sem,
):
    bl, row, col = lax.axis_index("bl"), lax.axis_index("row"), lax.axis_index("col")
    high_z, low_z = bl // 4, bl % 4
    x, y_hi = row // 2, row % 2
    me = y_hi * 32 + low_z * 8 + col

    def member(slot):
        return (high_z * 4 + slot % 32 // 8, x * 2 + slot // 32, slot % 8)

    def along_x(step):
        return (bl, (x + step) % 4 * 2 + y_hi, col)

    def along_z(step):
        return ((high_z + step) % 4 * 4 + low_z, row, col)

    loads = [
        pltpu.make_async_copy(source, target, local_sem.at[k])
        for k, (source, target) in enumerate(
            (
                (off_hbm, off_ref),
                (freq_hbm, freq_ref),
                (taper_hbm, taper_ref),
                (owner_hbm, owner_ref),
                (tile_hbm, tile_ref),
                (vis_hbm, vis_ref),
                (rows_hbm, rows_ref),
                (cols_hbm, cols_ref),
                (twist_hbm, twist_ref),
                (last_hbm, last_ref),
                (wide_hbm, wide_ref),
            )
        )
    ]
    for load in loads:
        load.start()
    barrier = pltpu.get_barrier_semaphore()

    def greet(step, _):
        pl.semaphore_signal(
            barrier, inc=1, device_id=member((me + step) % GROUP), device_id_type=MESH
        )
        return 0

    lax.fori_loop(1, GROUP, greet, 0)
    for step in range(1, 4):
        pl.semaphore_signal(barrier, inc=1, device_id=along_x(step), device_id_type=MESH)
        pl.semaphore_signal(barrier, inc=1, device_id=along_z(step), device_id_type=MESH)
    for load in loads[:5]:
        load.wait()
    places(owner_ref, tile_ref, place_ref)
    phasors(off_ref, freq_ref, base_ref, far_ref)
    weights(taper_ref, w_ref)
    pl.semaphore_wait(barrier, GROUP - 1 + 6)

    def place_copy(step):
        return pltpu.make_async_remote_copy(
            src_ref=place_ref,
            dst_ref=places_ref.at[me],
            send_sem=psend_sem.at[step],
            recv_sem=pgot_sem.at[me],
            device_id=member((me + step) % GROUP),
            device_id_type=MESH,
        )

    def sub_copy(step):
        slot = (me + step) % GROUP
        return pltpu.make_async_remote_copy(
            src_ref=send_ref.at[slot % 32],
            dst_ref=got_ref.at[me],
            send_sem=ssend_sem.at[step],
            recv_sem=sgot_sem.at[me],
            device_id=member(slot),
            device_id_type=MESH,
        )

    def start(copy):
        def body(step, _):
            copy(step).start()
            return 0

        lax.fori_loop(1, GROUP, body, 0)

    def finish_sends(copy):
        def body(step, _):
            copy(step).wait_send()
            return 0

        lax.fori_loop(1, GROUP, body, 0)

    def finish_gets(buffer, sem):
        def body(step, _):
            slot = (me + step) % GROUP
            pltpu.make_async_copy(buffer.at[slot], buffer.at[slot], sem.at[slot]).wait()
            return 0

        lax.fori_loop(1, GROUP, body, 0)

    start(place_copy)
    places_ref[me] = place_ref[...]
    for load in loads[5:8]:
        load.wait()
    side_refs = ((left_a_ref, right_a_ref), (left_b_ref, right_b_ref))
    subgrids(vis_ref, w_ref, rows_ref, cols_ref, base_ref, far_ref, side_refs, image_ref, sub_ref)
    for p in range(SUB):
        send_ref[p] = sub_ref[p * 17 : p * 17 + 16].astype(BF16)
    start(sub_copy)
    got_ref[me] = send_ref[me % 32]

    finish_gets(places_ref, pgot_sem)
    diagonal = (
        lax.broadcasted_iota(jnp.int32, (8, 128), 1) // 16
        == lax.broadcasted_iota(jnp.int32, (8, 128), 0)
    )
    tile_rows = []
    for k in range(16):
        pieces = places_ref[pl.ds(k // 2 * 8, 8), 0, pl.ds(k % 2 * 128, 128)]
        place = jnp.sum(jnp.where(diagonal, pieces, 0), axis=0, keepdims=True)
        tile_rows.append(place // TILES)
        onehot_ref[:, pl.ds(k * 128, 128)] = (
            (lax.broadcasted_iota(jnp.int32, (TILES, 128), 0) == place % TILES)
            .astype(F32)
            .astype(BF16)
        )
    tile_row = jnp.concatenate(tile_rows, axis=1)

    finish_gets(got_ref, sgot_sem)
    for k in range(8):
        turned = got_ref[pl.ds(k * 8, 8)].reshape(128, 128).astype(F32).T.astype(BF16)
        data_ref[:, pl.ds(k * 256, 128)] = turned[:64]
        data_ref[:, pl.ds(k * 256 + 128, 128)] = turned[64:]

    def x_copy(turn, step):
        return pltpu.make_async_remote_copy(
            src_ref=xsend_ref.at[turn, step - 1],
            dst_ref=xgot_ref.at[turn, step - 1],
            send_sem=xsend_sem.at[turn, step - 1],
            recv_sem=xgot_sem.at[turn, step - 1],
            device_id=along_x(step),
            device_id_type=MESH,
        )

    def z_copy(turn):
        return pltpu.make_async_remote_copy(
            src_ref=zsend_ref.at[turn],
            dst_ref=zgot_ref.at[turn],
            send_sem=zsend_sem.at[turn],
            recv_sem=zgot_sem.at[turn],
            device_id=along_z((2, 1, 3)[turn]),
            device_id_type=MESH,
        )

    for turn in range(4):
        td = (high_z + (2, 1, 3, 0)[turn]) % 4
        for step in range(4):
            wanted = ((x + step) % 4 * 2 + y_hi) * 4 + td
            masked_ref[pl.ds(step * 64, 64), :] = jnp.where(
                tile_row == wanted, data_ref[...].astype(F32), 0.0
            ).astype(BF16)
        placed = dot_t(masked_ref[...], onehot_ref[...])
        own_ref[turn] = placed[:64]
        for step in (2, 1, 3):
            xsend_ref[turn, step - 1] = placed[step * 64 : step * 64 + 64].astype(BF16)
            x_copy(turn, step).start()

    for turn in range(4):
        total = own_ref[turn]
        for step in range(1, 4):
            x_copy(turn, step).wait_recv()
            total += xgot_ref[turn, step - 1].astype(F32)
        if turn < 3:
            zsend_ref[turn] = total.astype(BF16)
            z_copy(turn).start()
        else:
            own_ref[turn] = total

    finish_sends(place_copy)
    finish_sends(sub_copy)
    for turn in range(4):
        for step in range(1, 4):
            x_copy(turn, step).wait_send()
    for load in loads[8:]:
        load.wait()
    grid = own_ref[3]
    for turn in range(3):
        z_copy(turn).wait_recv()
        grid += zgot_ref[turn].astype(F32)
    out_ref[...] = column_transform(grid, wide_ref, twist_ref, last_ref)
    for turn in range(3):
        z_copy(turn).wait_send()


def on_device(visibilities, offsets, frequencies, taper_curve, owner_index, tile_index):
    rows, cols, wide, twist, last = (jnp.asarray(table) for table in make_tables())
    operands = (
        visibilities,
        offsets.reshape(64, 64),
        frequencies.reshape(1, 16),
        taper_curve.reshape(1, SUB),
        owner_index.reshape(1, 32),
        tile_index.reshape(1, 32),
        rows,
        cols,
        wide,
        twist,
        last,
    )
    result = pl.pallas_call(
        kernel,
        out_shape=jax.ShapeDtypeStruct((64, TILES), F32),
        in_specs=[pl.BlockSpec(memory_space=pl.ANY)] * len(operands),
        out_specs=pl.BlockSpec(memory_space=pltpu.VMEM),
        scratch_shapes=[pltpu.VMEM(operand.shape, operand.dtype) for operand in operands]
        + [
            pltpu.VMEM((2, 64, 128), F32),
            pltpu.VMEM((1, 256), jnp.int32),
            pltpu.VMEM((2, 8, 520, 128), F32),
            pltpu.VMEM((2, 2, 64, 1024), F32),
            pltpu.VMEM((256, 1024), BF16),
            pltpu.VMEM((256, 1024), BF16),
            pltpu.VMEM((256, 1024), BF16),
            pltpu.VMEM((256, 1024), BF16),
            pltpu.VMEM((2048, 256), BF16),
            pltpu.VMEM((17 * SUB, 128), F32),
            pltpu.VMEM((SUB, 16, 128), BF16),
            pltpu.VMEM((GROUP, 16, 128), BF16),
            pltpu.VMEM((GROUP, 1, 256), jnp.int32),
            pltpu.VMEM((64, 2048), BF16),
            pltpu.VMEM((TILES, 2048), BF16),
            pltpu.VMEM((256, 2048), BF16),
            pltpu.VMEM((4, 64, TILES), F32),
            pltpu.VMEM((4, 3, 64, TILES), BF16),
            pltpu.VMEM((4, 3, 64, TILES), BF16),
            pltpu.VMEM((3, 64, TILES), BF16),
            pltpu.VMEM((3, 64, TILES), BF16),
            pltpu.SemaphoreType.DMA((len(operands),)),
            pltpu.SemaphoreType.DMA((GROUP,)),
            pltpu.SemaphoreType.DMA((GROUP,)),
            pltpu.SemaphoreType.DMA((GROUP,)),
            pltpu.SemaphoreType.DMA((GROUP,)),
            pltpu.SemaphoreType.DMA((4, 3)),
            pltpu.SemaphoreType.DMA((4, 3)),
            pltpu.SemaphoreType.DMA((3,)),
            pltpu.SemaphoreType.DMA((3,)),
        ],
        compiler_params=pltpu.CompilerParams(
            collective_id=0, has_side_effects=True, vmem_limit_bytes=60 * 1024 * 1024
        ),
    )(*operands)
    return result.reshape(1, 1, 2, GC)


def solution(mesh):
    in_specs = (
        P(("bl", "row", "col"), None, None),
        P(("bl", "row", "col"), None, None),
        P(),
        P(),
        P(("bl", "row", "col"), None),
        P(("bl", "row", "col")),
    )
    out_specs = P("row", ("bl", "col"), None, None)
    return jax.shard_map(
        on_device, mesh=mesh, in_specs=in_specs, out_specs=out_specs, check_vma=False
    )
```

```python
import math

import jax
import jax.numpy as jnp
import numpy as np
from jax import lax
from jax.experimental import pallas as pl
from jax.experimental.pallas import tpu as pltpu
from jax.sharding import PartitionSpec as P

MESH = pl.DeviceIdType.MESH
SUB = 32
GC = 16384
TILES = GC // SUB
F32 = jnp.float32
BF16 = jnp.bfloat16


def split_np(table):
    high = table.astype(BF16)
    low = (table - high.astype(np.float64)).astype(BF16)
    return np.stack([high, low])


def by_lanes(table):
    rows, lanes = table.shape[-2:]
    pieces = table.reshape(table.shape[:-1] + (lanes // 128, 128))
    return np.ascontiguousarray(np.moveaxis(pieces, -2, -3))


def joined(ref, *index):
    return jnp.concatenate([ref[(*index, k)] for k in range(ref.shape[-3])], axis=1)


def make_tables():
    index = np.arange(SUB)
    angle = 2.0 * np.pi * (index[:, None] * index[None, :] % SUB) / SUB
    cos, sin = np.cos(angle), np.sin(angle)
    order = pixel_order()
    cos_in, sin_in = cos[:, order], sin[:, order]
    rows = np.zeros((2, 4, SUB, 4, 2, SUB))
    for b in range(4):
        rows[0, b, :, b, 0], rows[0, b, :, b, 1] = cos_in, sin_in
        rows[1, b, :, b, 0], rows[1, b, :, b, 1] = sin_in, -cos_in
    rows = split_np(rows.reshape(2, 128, 256))
    cos_in, sin_in = cos[order], sin[order]
    straight = np.stack([[cos_in, -sin_in], [sin_in, cos_in]])
    crossed = np.stack([[-sin_in, -cos_in], [cos_in, -sin_in]])
    cols = np.stack([straight, crossed], axis=1)
    cols = cols.reshape(2, 2, 2, SUB, 8, 4).transpose(0, 3, 1, 4, 2, 5).reshape(64, 128)
    cols = split_np(np.tile(cols, (2, 1)))
    cols = np.concatenate([cols[0], cols[0], cols[1]])
    wide = np.arange(TILES)
    wide_angle = 2.0 * np.pi * (wide[:, None] * wide[None, :] % TILES) / TILES
    wide_table = np.concatenate([np.cos(wide_angle), np.sin(wide_angle)], axis=1)
    twist_angle = 2.0 * np.pi * (index[:, None] * wide[None, :]) / GC
    twist = (np.stack([np.cos(twist_angle), np.sin(twist_angle)]) / 128.0).astype(np.float32)
    last = np.block([[cos, -sin], [sin, cos]])
    return (
        by_lanes(rows),
        cols,
        by_lanes(split_np(wide_table)),
        twist,
        split_np(last),
    )


def dot(a, b):
    return lax.dot_general(a, b, (((1,), (0,)), ((), ())), preferred_element_type=F32)


def dot_t(a, b):
    return lax.dot_general(a, b, (((1,), (1,)), ((), ())), preferred_element_type=F32)


def split(x):
    high = x.astype(BF16)
    return high, (x - high.astype(F32)).astype(BF16)


def cmul(ar, ai, br, bi):
    return ar * br - ai * bi, ar * bi + ai * br


def three(x, rows):
    high = x.astype(BF16).astype(F32)
    middle = (x - high).astype(BF16).astype(F32)
    low = x - high - middle
    place = lax.broadcasted_iota(jnp.int32, (rows, x.shape[1]), 0)
    parts = jnp.where(place == 0, high, jnp.where(place == 1, middle, jnp.where(place == 2, low, 0.0)))
    return parts.astype(BF16)


def matches(shape, left, right):
    row, lane = lax.broadcasted_iota(jnp.int32, shape, 0), lax.broadcasted_iota(jnp.int32, shape, 1)
    return (left(row) == right(lane)).astype(F32).astype(BF16)


def pixel(k):
    slot = k % SUB
    return 16 + jnp.where(slot < 16, slot, jnp.where(slot == 16, -16, 16 - slot))


def weights(taper_ref, w_ref):
    parts = three(taper_ref[...], 16)
    along = dot(parts, matches((SUB, 128), lambda i: i, pixel))
    down = dot_t(matches((64, SUB), pixel, lambda k: k), parts)
    along, down = jnp.sum(along, axis=0, keepdims=True), jnp.sum(down, axis=1, keepdims=True)
    lane = lax.broadcasted_iota(jnp.int32, (64, 128), 1) // 64
    for half in range(2):
        w_ref[half] = jnp.where(lane == half, down * along * (1.0 / 1024.0), 0.0)


def place_order(lane):
    slot = lane % SUB
    return slot // 16 * 16 + slot // 4 % 2 * 8 + slot // 8 % 2 * 4 + slot % 4


def places(owner_ref, tile_ref, place_ref):
    row = lax.broadcasted_iota(jnp.int32, (16, SUB), 0)
    parts = jnp.where(row == 0, owner_ref[...], jnp.where(row == 1, tile_ref[...], 0))
    order = matches((SUB, 128), lambda i: i, place_order)
    both = dot(parts.astype(F32).astype(BF16), order).astype(jnp.int32)
    owner, tile = both[0:1], both[1:2]
    place_ref[...] = (owner // 8 * 4 + tile // 64) * TILES + owner % 8 * 64 + tile % 64


def phasors(off_ref, freq_ref, base_ref, far_ref):
    spread = matches((64, 1024), lambda i: i, lambda k: k // 16)
    repeat = matches((16, 1024), lambda i: i, lambda k: k % 16)
    freq = jnp.sum(dot(three(freq_ref[...], 16), repeat), axis=0, keepdims=True)
    scaled = dot(off_ref[...], spread) * freq
    theta = scaled * (2.0 * math.pi / SUB)
    square = theta * theta
    cos = jnp.full_like(square, -1.0 / math.factorial(14))
    sin = jnp.full_like(square, -1.0 / math.factorial(15))
    for order in range(6, -1, -1):
        sign = 1.0 if order % 2 == 0 else -1.0
        cos = cos * square + sign / math.factorial(2 * order)
        sin = sin * square + sign / math.factorial(2 * order + 1)
    z = [(jnp.ones_like(cos), jnp.zeros_like(cos)), (cos, sin * theta)]
    for p in range(2, 8):
        z.append(cmul(*z[p // 2], *z[p - p // 2]))
    for p in range(8):
        for part in range(2):
            for k in range(8):
                base_ref[part, k, pl.ds(p * 65, 64)] = z[p][part][:, k * 128 : k * 128 + 128]
    z8 = cmul(*z[4], *z[4])
    for e, value in enumerate((z8, cmul(*z8, *z8))):
        for part in range(2):
            far_ref[e, part] = value[part]


def pixel_order():
    slot = np.arange(SUB)
    return 16 + np.where(slot < 16, slot, np.where(slot == 16, -16, 16 - slot))


def block_sides(block, slot, vis_ref, base_ref, far_ref, left_ref, right_ref):
    chunk = 256
    first = lax.broadcasted_iota(jnp.int32, (8, chunk), 0) == 0
    for start in range(0, 1024, chunk):
        lanes = pl.ds(start, chunk)
        for side, target in enumerate((left_ref, right_ref)):
            row = 2 * block + side
            low = [
                jnp.concatenate(
                    [
                        base_ref[part, start // 128 + k, pl.ds(row, 8, stride=65), :]
                        for k in range(chunk // 128)
                    ],
                    axis=1,
                )
                for part in (0, 1)
            ]
            far = [
                [jnp.broadcast_to(far_ref[e, part, pl.ds(row, 1), lanes], (8, chunk)) for part in (0, 1)]
                for e in (0, 1)
            ]
            near = (low, cmul(*low, *far[0]))
            if side == 0:
                vis = vis_ref[block, :, lanes].astype(F32)
                vr, vi = (jnp.broadcast_to(vis[k : k + 1], (8, chunk)) for k in (0, 1))
                products = [(vr * c, vi * s, vr * s, vi * c) for c, s in near]
                plus = [(a - b, d + e) for a, b, d, e in products]
                minus = [(a + b, e - d) for a, b, d, e in products]
                last = cmul(vr, vi, far[1][0], -far[1][1])
            else:
                plus, minus = near, [(c, -s) for c, s in near]
                last = (far[1][0], -far[1][1])
            minus[0] = tuple(jnp.where(first, x, y) for x, y in zip(last, minus[0]))
            for part in range(2):
                for k, pieces in enumerate((plus, minus)):
                    rows = pl.ds(slot * 64 + part * 32 + k * 16, 16)
                    target[rows, lanes] = jnp.concatenate(
                        [piece[part] for piece in pieces], axis=0
                    ).astype(BF16)


def sides(four, which, vis_ref, base_ref, far_ref, side_refs):
    for b in range(4):
        block_sides(four * 4 + b, b, vis_ref, base_ref, far_ref, *side_refs[which])


def images(half, vis_ref, w_ref, base_ref, far_ref, side_refs, image_ref):
    def image(four, which):
        left_ref, right_ref = side_refs[which]
        product = dot_t(left_ref[...], right_ref[...])
        for b in range(4):
            block = product[b * 64 : b * 64 + 64, b // 2 * 128 : b // 2 * 128 + 128] * w_ref[b % 2]
            high, low = split(block)
            rows = pl.ds((four - 4 * half) * 256 + b * 64, 64)
            image_ref[rows, 0:128], image_ref[rows, 128:256] = high, low

    def pair(gp, _):
        sides(2 * gp + 1, 1, vis_ref, base_ref, far_ref, side_refs)
        image(2 * gp, 0)
        sides(jnp.minimum(2 * gp + 2, 7), 0, vis_ref, base_ref, far_ref, side_refs)
        image(2 * gp + 1, 1)
        return 0

    lax.fori_loop(2 * half, 2 * half + 2, pair, 0)


def subgrids(image_ref, rows_ref, cols_ref, out_ref):
    lane = lax.broadcasted_iota(jnp.int32, (256, 128), 1)
    lower = lane < 64
    image = image_ref[...]
    turned = dot(image, cols_ref[pl.ds(0, 256)]) + dot(image[:, :128], cols_ref[pl.ds(256, 128)])
    straight, crossed = [], []
    for k in range(2):
        even, odd = turned[k * 512 : k * 512 + 256], turned[k * 512 + 256 : k * 512 + 512]
        straight.append(jnp.where(lower, even, pltpu.roll(odd, 64, 1)))
        crossed.append(jnp.where(lower, pltpu.roll(even, 64, 1), odd))
    total = 0.0
    for part, pieces in enumerate((straight, crossed)):
        high, low = split(jnp.concatenate(pieces, axis=1))
        rows_high, rows_low = joined(rows_ref, 0, part), joined(rows_ref, 1, part)
        total += dot(rows_high, high) + dot(rows_high, low) + dot(rows_low, high)
    pieces = [
        total[b * 32 : b * 32 + 32, k * 128 : k * 128 + 128] for k in range(2) for b in range(4)
    ]
    group = lane[:32] // 8 % 8
    for bit in (1, 2, 4):
        clear = group & bit == 0
        for t in range(8):
            if t & bit == 0:
                x, y = pieces[t], pieces[t | bit]
                pieces[t] = jnp.where(clear, x, pltpu.roll(y, bit * 8, 1))
                pieces[t | bit] = jnp.where(clear, pltpu.roll(x, 128 - bit * 8, 1), y)
    for h in range(4):
        for l in range(4):
            both = [pieces[h * 2 + y][l * 8 : l * 8 + 8] for y in range(2)]
            out_ref[h * 4 + l] = jnp.concatenate(both, axis=0).astype(BF16)


def column_transform(grid, wide_ref, twist_ref, last_ref):
    high, low = split(grid)
    wide_high, wide_low = joined(wide_ref, 0), joined(wide_ref, 1)
    wide = dot(high, wide_high) + dot(low, wide_high) + dot(high, wide_low)
    real = wide[:SUB, :TILES] - wide[SUB:, TILES:]
    imag = wide[SUB:, :TILES] + wide[:SUB, TILES:]
    real, imag = cmul(real, imag, twist_ref[0], twist_ref[1])
    high, low = split(jnp.concatenate([real, imag], axis=0))
    return dot(last_ref[0], high) + dot(last_ref[0], low) + dot(last_ref[1], high)


def kernel(
    vis_hbm,
    off_hbm,
    freq_hbm,
    taper_hbm,
    owner_hbm,
    tile_hbm,
    rows_hbm,
    cols_hbm,
    wide_hbm,
    twist_hbm,
    last_hbm,
    out_ref,
    vis_ref,
    off_ref,
    freq_ref,
    taper_ref,
    owner_ref,
    tile_ref,
    rows_ref,
    cols_ref,
    wide_ref,
    twist_ref,
    last_ref,
    w_ref,
    place_ref,
    base_ref,
    far_ref,
    left_a_ref,
    right_a_ref,
    left_b_ref,
    right_b_ref,
    image_ref,
    zplace_ref,
    yplace_ref,
    zsend_ref,
    zgot_ref,
    turn_ref,
    ysend_ref,
    ygot_ref,
    onehot_ref,
    masked_ref,
    xsend_ref,
    xgot_ref,
    lsend_ref,
    lgot_ref,
    local_sem,
    zplace_send,
    zplace_recv,
    yplace_send,
    yplace_recv,
    z_send,
    z_recv,
    y_send,
    y_recv,
    x_send,
    x_recv,
    l_send,
    l_recv,
):
    loads = [
        pltpu.make_async_copy(source, target, local_sem.at[k])
        for k, (source, target) in enumerate(
            (
                (off_hbm, off_ref),
                (freq_hbm, freq_ref),
                (taper_hbm, taper_ref),
                (owner_hbm, owner_ref),
                (tile_hbm, tile_ref),
                (vis_hbm, vis_ref),
                (rows_hbm, rows_ref),
                (cols_hbm, cols_ref),
                (twist_hbm, twist_ref),
                (last_hbm, last_ref),
                (wide_hbm, wide_ref),
            )
        )
    ]
    for load in loads:
        load.start()

    bl, row, col = lax.axis_index("bl"), lax.axis_index("row"), lax.axis_index("col")
    high_z, low_z = bl // 4, bl % 4
    x, y_hi = row // 2, row % 2
    me = y_hi * 8 + col

    def along_z(slot):
        return (slot, row, col)

    def along_y(slot):
        return (bl, x * 2 + slot // 8, slot % 8)

    def along_x(step):
        return (bl, (x + step) % 4 * 2 + y_hi, col)

    def final(step):
        return ((high_z + step % 4) % 4 * 4 + low_z, x * 2 + (y_hi + step // 4) % 2, col)

    barrier = pltpu.get_barrier_semaphore()

    def greet(device):
        pl.semaphore_signal(barrier, inc=1, device_id=device, device_id_type=MESH)

    def greet_lines(step, _):
        greet(along_z((bl + step) % 16))
        greet(along_y((me + step) % 16))
        return 0

    lax.fori_loop(1, 16, greet_lines, 0)
    for step in range(1, 4):
        greet(along_x(step))
        greet(final(4 + step))

    for load in loads[:5]:
        load.wait()
    places(owner_ref, tile_ref, place_ref)
    phasors(off_ref, freq_ref, base_ref, far_ref)
    weights(taper_ref, w_ref)
    pl.semaphore_wait(barrier, 36)

    def remote(source, target, send_sem, recv_sem, device):
        return pltpu.make_async_remote_copy(
            src_ref=source,
            dst_ref=target,
            send_sem=send_sem,
            recv_sem=recv_sem,
            device_id=device,
            device_id_type=MESH,
        )

    def zplace_copy(slot):
        return remote(
            place_ref, zplace_ref.at[bl], zplace_send.at[slot], zplace_recv.at[bl], along_z(slot)
        )

    def yplace_copy(slot):
        return remote(
            zplace_ref, yplace_ref.at[me], yplace_send.at[slot], yplace_recv.at[me], along_y(slot)
        )

    def z_copy(half):
        return lambda slot: remote(
            zsend_ref.at[half, slot],
            zgot_ref.at[half, bl],
            z_send.at[half, slot],
            z_recv.at[half, bl],
            along_z(slot),
        )

    def y_copy(half):
        return lambda slot: remote(
            ysend_ref.at[half, slot],
            ygot_ref.at[half, me],
            y_send.at[half, slot],
            y_recv.at[half, me],
            along_y(slot),
        )

    def others(mine, act):
        def body(step, _):
            act((mine + step) % 16)
            return 0

        lax.fori_loop(1, 16, body, 0)

    def arrive(mine, buffer, sem):
        def wait(slot):
            pltpu.make_async_copy(buffer.at[slot], buffer.at[slot], sem.at[slot]).wait()

        others(mine, wait)

    others(bl, lambda slot: zplace_copy(slot).start())
    zplace_ref[bl] = place_ref[...]
    for load in loads[5:8]:
        load.wait()
    side_refs = ((left_a_ref, right_a_ref), (left_b_ref, right_b_ref))
    sides(0, 0, vis_ref, base_ref, far_ref, side_refs)
    for half in range(2):
        images(half, vis_ref, w_ref, base_ref, far_ref, side_refs, image_ref)
        subgrids(image_ref, rows_ref, cols_ref, zsend_ref.at[half])
        others(bl, lambda slot: z_copy(half)(slot).start())
        zgot_ref[half, bl] = zsend_ref[half, bl]
        if half == 0:
            arrive(bl, zplace_ref, zplace_recv)
            others(me, lambda slot: yplace_copy(slot).start())
            yplace_ref[me] = zplace_ref[...]

    def turn(half):
        arrive(bl, zgot_ref.at[half], z_recv.at[half])
        for slot in range(16):
            turn_ref[pl.ds(slot * 17, 16)] = zgot_ref[half, slot].astype(F32)
        for slot in range(16):
            ysend_ref[half, slot] = turn_ref[pl.ds(slot, 16, stride=17)].astype(BF16)
        others(me, lambda slot: y_copy(half)(slot).start())
        ygot_ref[half, me] = ysend_ref[half, me]

    turn(0)
    arrive(me, yplace_ref, yplace_recv)
    place = yplace_ref[...].reshape(256, 128).astype(F32).T[:SUB].astype(jnp.int32)
    wanted = (place // TILES - x * 8 + 32) % 32
    column = place % TILES
    tiles = lax.broadcasted_iota(jnp.int32, (TILES, 256), 0)
    for n in range(SUB):
        onehot_ref[n // 16, :, pl.ds(n % 16 * 256, 256)] = (
            (tiles == column[n : n + 1]).astype(F32).astype(BF16)
        )
    turn(1)

    placed = 0.0
    for half in range(2):
        arrive(me, ygot_ref.at[half], y_recv.at[half])
        data = ygot_ref[half].reshape(256, 128).astype(F32).T
        for j in range(16):
            values = data[j * 8 : j * 8 + 8]
            row_of = wanted[half * 16 + j : half * 16 + j + 1]
            for k in range(16):
                pieces = [jnp.where(row_of == 2 * k + e, values, 0.0) for e in range(2)]
                masked_ref[half, pl.ds(k * 16, 16), pl.ds(j * 256, 256)] = jnp.concatenate(
                    pieces, axis=0
                ).astype(BF16)
        placed += dot_t(masked_ref[half], onehot_ref[half])

    def x_copy(step):
        return remote(
            xsend_ref.at[step - 1],
            xgot_ref.at[step - 1],
            x_send.at[step - 1],
            x_recv.at[step - 1],
            along_x(step),
        )

    for step in (2, 1, 3):
        xsend_ref[step - 1] = placed[step * 64 : step * 64 + 64].astype(BF16)
        x_copy(step).start()
    total = placed[:64]
    for step in (1, 3, 2):
        x_copy(step).wait_recv()
        total += xgot_ref[step - 1].astype(F32)

    mine = high_z * 2 + y_hi

    def l_copy(step):
        target = (y_hi + step // 4) % 2 * 4 + (high_z + step % 4) % 4
        return remote(
            lsend_ref.at[target], lgot_ref.at[mine], l_send.at[step], l_recv.at[mine], final(step)
        )

    for m in range(8):
        piece = total[m * 8 : m * 8 + 8]
        lsend_ref[m] = jnp.concatenate([piece[:, :256], piece[:, 256:]], axis=0).astype(BF16)
    for step in (2, 6, 1, 3, 5, 7, 4):
        l_copy(step).start()
    lgot_ref[mine] = lsend_ref[y_hi * 4 + high_z]

    others(bl, lambda slot: zplace_copy(slot).wait_send())
    others(me, lambda slot: yplace_copy(slot).wait_send())
    for half in range(2):
        others(bl, lambda slot: z_copy(half)(slot).wait_send())
        others(me, lambda slot: y_copy(half)(slot).wait_send())
    for step in range(1, 4):
        x_copy(step).wait_send()
    for load in loads[8:]:
        load.wait()

    for step in range(1, 8):
        source = (high_z + step % 4) % 4 * 2 + (y_hi + step // 4) % 2
        pltpu.make_async_copy(lgot_ref.at[source], lgot_ref.at[source], l_recv.at[source]).wait()
    upper = lax.broadcasted_iota(jnp.int32, (8, TILES), 0) < 4
    real, imag = [], []
    for h in range(4):
        even, odd = (
            jnp.concatenate([piece[:8], piece[8:]], axis=1)
            for piece in (lgot_ref[2 * h].astype(F32), lgot_ref[2 * h + 1].astype(F32))
        )
        real.append(jnp.where(upper, even, pltpu.roll(odd, 4, 0)))
        imag.append(jnp.where(upper, pltpu.roll(even, 4, 0), odd))
    grid = jnp.concatenate(real + imag, axis=0)
    result = column_transform(grid, wide_ref, twist_ref, last_ref)
    for part in range(2):
        for k in range(4):
            out_ref[pl.ds(k * 2 + part, SUB, stride=8), :] = result[
                part * 32 : part * 32 + 32, k * 128 : k * 128 + 128
            ]
    for step in range(1, 8):
        l_copy(step).wait_send()


def on_device(visibilities, offsets, frequencies, taper_curve, owner_index, tile_index):
    rows, cols, wide, twist, last = (jnp.asarray(table) for table in make_tables())
    operands = (
        visibilities,
        offsets.reshape(64, 64),
        frequencies.reshape(1, 16),
        taper_curve.reshape(1, SUB),
        owner_index.reshape(1, 32),
        tile_index.reshape(1, 32),
        rows,
        cols,
        wide,
        twist,
        last,
    )
    result = pl.pallas_call(
        kernel,
        out_shape=jax.ShapeDtypeStruct((256, 128), F32),
        in_specs=[pl.BlockSpec(memory_space=pl.ANY)] * len(operands),
        out_specs=pl.BlockSpec(memory_space=pltpu.VMEM),
        scratch_shapes=[pltpu.VMEM(operand.shape, operand.dtype) for operand in operands]
        + [
            pltpu.VMEM((2, 64, 128), F32),
            pltpu.VMEM((1, 128), jnp.int32),
            pltpu.VMEM((2, 8, 520, 128), F32),
            pltpu.VMEM((2, 2, 64, 1024), F32),
            pltpu.VMEM((256, 1024), BF16),
            pltpu.VMEM((256, 1024), BF16),
            pltpu.VMEM((256, 1024), BF16),
            pltpu.VMEM((256, 1024), BF16),
            pltpu.VMEM((1024, 256), BF16),
            pltpu.VMEM((16, 1, 128), jnp.int32),
            pltpu.VMEM((16, 16, 1, 128), jnp.int32),
            pltpu.VMEM((2, 16, 16, 128), BF16),
            pltpu.VMEM((2, 16, 16, 128), BF16),
            pltpu.VMEM((16 * 17, 128), F32),
            pltpu.VMEM((2, 16, 16, 128), BF16),
            pltpu.VMEM((2, 16, 16, 128), BF16),
            pltpu.VMEM((2, TILES, 4096), BF16),
            pltpu.VMEM((2, 256, 4096), BF16),
            pltpu.VMEM((3, 64, TILES), BF16),
            pltpu.VMEM((3, 64, TILES), BF16),
            pltpu.VMEM((8, 16, 256), BF16),
            pltpu.VMEM((8, 16, 256), BF16),
            pltpu.SemaphoreType.DMA((len(operands),)),
        ]
        + [pltpu.SemaphoreType.DMA((16,))] * 4
        + [pltpu.SemaphoreType.DMA((2, 16))] * 4
        + [pltpu.SemaphoreType.DMA((3,))] * 2
        + [pltpu.SemaphoreType.DMA((8,))] * 2,
        compiler_params=pltpu.CompilerParams(
            collective_id=0, has_side_effects=True, vmem_limit_bytes=60 * 1024 * 1024
        ),
    )(*operands)
    return result.reshape(128, 2, 128).transpose(1, 0, 2).reshape(1, 1, 2, GC)


def solution(mesh):
    in_specs = (
        P(("bl", "row", "col"), None, None),
        P(("bl", "row", "col"), None, None),
        P(),
        P(),
        P(("bl", "row", "col"), None),
        P(("bl", "row", "col")),
    )
    out_specs = P("row", ("bl", "col"), None, None)
    return jax.shard_map(
        on_device, mesh=mesh, in_specs=in_specs, out_specs=out_specs, check_vma=False
    )
```

```python
import math

import jax
import jax.numpy as jnp
import numpy as np
from jax import lax
from jax.experimental import pallas as pl
from jax.experimental.pallas import tpu as pltpu
from jax.sharding import PartitionSpec as P

MESH = pl.DeviceIdType.MESH
SUB = 32
GC = 16384
TILES = GC // SUB
F32 = jnp.float32
BF16 = jnp.bfloat16


def split_np(table):
    high = table.astype(BF16)
    low = (table - high.astype(np.float64)).astype(BF16)
    return np.stack([high, low])


def by_lanes(table):
    rows, lanes = table.shape[-2:]
    pieces = table.reshape(table.shape[:-1] + (lanes // 128, 128))
    return np.ascontiguousarray(np.moveaxis(pieces, -2, -3))


def joined(ref, *index):
    return jnp.concatenate([ref[(*index, k)] for k in range(ref.shape[-3])], axis=1)


def make_tables():
    index = np.arange(SUB)
    angle = 2.0 * np.pi * (index[:, None] * index[None, :] % SUB) / SUB
    cos, sin = np.cos(angle), np.sin(angle)
    order = pixel_order()
    cos_in, sin_in = cos[:, order], sin[:, order]
    rows = np.zeros((2, 4, SUB, 4, 2, SUB))
    for b in range(4):
        rows[0, b, :, b, 0], rows[0, b, :, b, 1] = cos_in, sin_in
        rows[1, b, :, b, 0], rows[1, b, :, b, 1] = sin_in, -cos_in
    rows = split_np(rows.reshape(2, 128, 256))
    cos_in, sin_in = cos[order], sin[order]
    straight = np.stack([[cos_in, -sin_in], [sin_in, cos_in]])
    crossed = np.stack([[-sin_in, -cos_in], [cos_in, -sin_in]])
    cols = np.stack([straight, crossed], axis=1)
    cols = cols.reshape(2, 2, 2, SUB, 8, 4).transpose(0, 3, 1, 4, 2, 5).reshape(64, 128)
    cols = split_np(np.tile(cols, (2, 1)))
    cols = np.concatenate([cols[0], cols[0], cols[1]])
    wide = np.arange(TILES)
    wide_angle = 2.0 * np.pi * (wide[:, None] * wide[None, :] % TILES) / TILES
    wide_table = np.concatenate([np.cos(wide_angle), np.sin(wide_angle)], axis=1)
    twist_angle = 2.0 * np.pi * (index[:, None] * wide[None, :]) / GC
    twist = (np.stack([np.cos(twist_angle), np.sin(twist_angle)]) / 128.0).astype(np.float32)
    last = np.block([[cos, -sin], [sin, cos]])
    return (
        by_lanes(rows),
        cols,
        by_lanes(split_np(wide_table)),
        twist,
        split_np(last),
    )


def dot(a, b):
    return lax.dot_general(a, b, (((1,), (0,)), ((), ())), preferred_element_type=F32)


def dot_t(a, b):
    return lax.dot_general(a, b, (((1,), (1,)), ((), ())), preferred_element_type=F32)


def split(x):
    high = x.astype(BF16)
    return high, (x - high.astype(F32)).astype(BF16)


def cmul(ar, ai, br, bi):
    return ar * br - ai * bi, ar * bi + ai * br


def three(x, rows):
    high = x.astype(BF16).astype(F32)
    middle = (x - high).astype(BF16).astype(F32)
    low = x - high - middle
    place = lax.broadcasted_iota(jnp.int32, (rows, x.shape[1]), 0)
    parts = jnp.where(place == 0, high, jnp.where(place == 1, middle, jnp.where(place == 2, low, 0.0)))
    return parts.astype(BF16)


def matches(shape, left, right):
    row, lane = lax.broadcasted_iota(jnp.int32, shape, 0), lax.broadcasted_iota(jnp.int32, shape, 1)
    return (left(row) == right(lane)).astype(F32).astype(BF16)


def pixel(k):
    slot = k % SUB
    return 16 + jnp.where(slot < 16, slot, jnp.where(slot == 16, -16, 16 - slot))


def weights(taper_ref, w_ref):
    parts = three(taper_ref[...], 16)
    along = dot(parts, matches((SUB, 128), lambda i: i, pixel))
    down = dot_t(matches((64, SUB), pixel, lambda k: k), parts)
    along, down = jnp.sum(along, axis=0, keepdims=True), jnp.sum(down, axis=1, keepdims=True)
    lane = lax.broadcasted_iota(jnp.int32, (64, 128), 1) // 64
    for half in range(2):
        w_ref[half] = jnp.where(lane == half, down * along * (1.0 / 1024.0), 0.0)


def place_order(lane):
    slot = lane % SUB
    return slot // 16 * 16 + slot // 4 % 2 * 8 + slot // 8 % 2 * 4 + slot % 4


def places(owner_ref, tile_ref, place_ref):
    row = lax.broadcasted_iota(jnp.int32, (16, SUB), 0)
    parts = jnp.where(row == 0, owner_ref[...], jnp.where(row == 1, tile_ref[...], 0))
    order = matches((SUB, 128), lambda i: i, place_order)
    both = dot(parts.astype(F32).astype(BF16), order).astype(jnp.int32)
    owner, tile = both[0:1], both[1:2]
    place_ref[...] = (owner // 8 * 4 + tile // 64) * TILES + owner % 8 * 64 + tile % 64


def phasors(off_ref, freq_ref, base_ref, far_ref):
    spread = matches((64, 1024), lambda i: i, lambda k: k // 16)
    repeat = matches((16, 1024), lambda i: i, lambda k: k % 16)
    freq = jnp.sum(dot(three(freq_ref[...], 16), repeat), axis=0, keepdims=True)
    scaled = dot(off_ref[...], spread) * freq
    theta = scaled * (2.0 * math.pi / SUB)
    square = theta * theta
    cos = jnp.full_like(square, -1.0 / math.factorial(14))
    sin = jnp.full_like(square, -1.0 / math.factorial(15))
    for order in range(6, -1, -1):
        sign = 1.0 if order % 2 == 0 else -1.0
        cos = cos * square + sign / math.factorial(2 * order)
        sin = sin * square + sign / math.factorial(2 * order + 1)
    z = [(jnp.ones_like(cos), jnp.zeros_like(cos)), (cos, sin * theta)]
    for p in range(2, 8):
        z.append(cmul(*z[p // 2], *z[p - p // 2]))
    for p in range(8):
        for part in range(2):
            for k in range(8):
                base_ref[part, k, pl.ds(p * 65, 64)] = z[p][part][:, k * 128 : k * 128 + 128]
    z8 = cmul(*z[4], *z[4])
    for e, value in enumerate((z8, cmul(*z8, *z8))):
        for part in range(2):
            far_ref[e, part] = value[part]


def pixel_order():
    slot = np.arange(SUB)
    return 16 + np.where(slot < 16, slot, np.where(slot == 16, -16, 16 - slot))


def block_sides(block, slot, vis_ref, base_ref, far_ref, left_ref, right_ref):
    chunk = 256
    first = lax.broadcasted_iota(jnp.int32, (8, chunk), 0) == 0
    for start in range(0, 1024, chunk):
        lanes = pl.ds(start, chunk)
        for side, target in enumerate((left_ref, right_ref)):
            row = 2 * block + side
            low = [
                jnp.concatenate(
                    [
                        base_ref[part, start // 128 + k, pl.ds(row, 8, stride=65), :]
                        for k in range(chunk // 128)
                    ],
                    axis=1,
                )
                for part in (0, 1)
            ]
            far = [
                [jnp.broadcast_to(far_ref[e, part, pl.ds(row, 1), lanes], (8, chunk)) for part in (0, 1)]
                for e in (0, 1)
            ]
            near = (low, cmul(*low, *far[0]))
            if side == 0:
                vis = vis_ref[block, :, lanes].astype(F32)
                vr, vi = (jnp.broadcast_to(vis[k : k + 1], (8, chunk)) for k in (0, 1))
                products = [(vr * c, vi * s, vr * s, vi * c) for c, s in near]
                plus = [(a - b, d + e) for a, b, d, e in products]
                minus = [(a + b, e - d) for a, b, d, e in products]
                last = cmul(vr, vi, far[1][0], -far[1][1])
            else:
                plus, minus = near, [(c, -s) for c, s in near]
                last = (far[1][0], -far[1][1])
            minus[0] = tuple(jnp.where(first, x, y) for x, y in zip(last, minus[0]))
            for part in range(2):
                for k, pieces in enumerate((plus, minus)):
                    rows = pl.ds(slot * 64 + part * 32 + k * 16, 16)
                    target[rows, lanes] = jnp.concatenate(
                        [piece[part] for piece in pieces], axis=0
                    ).astype(BF16)


def sides(four, which, vis_ref, base_ref, far_ref, side_refs):
    for b in range(4):
        block_sides(four * 4 + b, b, vis_ref, base_ref, far_ref, *side_refs[which])


def images(half, vis_ref, w_ref, base_ref, far_ref, side_refs, image_ref):
    def image(four, which):
        left_ref, right_ref = side_refs[which]
        product = dot_t(left_ref[...], right_ref[...])
        for b in range(4):
            block = product[b * 64 : b * 64 + 64, b // 2 * 128 : b // 2 * 128 + 128] * w_ref[b % 2]
            high, low = split(block)
            rows = pl.ds((four - 4 * half) * 256 + b * 64, 64)
            image_ref[rows, 0:128], image_ref[rows, 128:256] = high, low

    def pair(gp, _):
        sides(2 * gp + 1, 1, vis_ref, base_ref, far_ref, side_refs)
        image(2 * gp, 0)
        sides(jnp.minimum(2 * gp + 2, 7), 0, vis_ref, base_ref, far_ref, side_refs)
        image(2 * gp + 1, 1)
        return 0

    lax.fori_loop(2 * half, 2 * half + 2, pair, 0)


def subgrids(image_ref, rows_ref, cols_ref, out_ref):
    lane = lax.broadcasted_iota(jnp.int32, (256, 128), 1)
    lower = lane < 64
    image = image_ref[...]
    turned = dot(image, cols_ref[pl.ds(0, 256)]) + dot(image[:, :128], cols_ref[pl.ds(256, 128)])
    straight, crossed = [], []
    for k in range(2):
        even, odd = turned[k * 512 : k * 512 + 256], turned[k * 512 + 256 : k * 512 + 512]
        straight.append(jnp.where(lower, even, pltpu.roll(odd, 64, 1)))
        crossed.append(jnp.where(lower, pltpu.roll(even, 64, 1), odd))
    total = 0.0
    for part, pieces in enumerate((straight, crossed)):
        high, low = split(jnp.concatenate(pieces, axis=1))
        rows_high, rows_low = joined(rows_ref, 0, part), joined(rows_ref, 1, part)
        total += dot(rows_high, high) + dot(rows_high, low) + dot(rows_low, high)
    pieces = [
        total[b * 32 : b * 32 + 32, k * 128 : k * 128 + 128] for k in range(2) for b in range(4)
    ]
    group = lane[:32] // 8 % 8
    for bit in (1, 2, 4):
        clear = group & bit == 0
        for t in range(8):
            if t & bit == 0:
                x, y = pieces[t], pieces[t | bit]
                pieces[t] = jnp.where(clear, x, pltpu.roll(y, bit * 8, 1))
                pieces[t | bit] = jnp.where(clear, pltpu.roll(x, 128 - bit * 8, 1), y)
    for h in range(4):
        for l in range(4):
            both = [pieces[h * 2 + y][l * 8 : l * 8 + 8] for y in range(2)]
            out_ref[h * 4 + l] = jnp.concatenate(both, axis=0).astype(BF16)


def column_transform(grid, wide_ref, twist_ref, last_ref):
    high, low = split(grid)
    wide_high, wide_low = joined(wide_ref, 0), joined(wide_ref, 1)
    wide = dot(high, wide_high) + dot(low, wide_high) + dot(high, wide_low)
    real = wide[:SUB, :TILES] - wide[SUB:, TILES:]
    imag = wide[SUB:, :TILES] + wide[:SUB, TILES:]
    real, imag = cmul(real, imag, twist_ref[0], twist_ref[1])
    high, low = split(jnp.concatenate([real, imag], axis=0))
    return dot(last_ref[0], high) + dot(last_ref[0], low) + dot(last_ref[1], high)


def kernel(
    vis_hbm,
    off_hbm,
    freq_hbm,
    taper_hbm,
    owner_hbm,
    tile_hbm,
    rows_hbm,
    cols_hbm,
    wide_hbm,
    twist_hbm,
    last_hbm,
    out_ref,
    vis_ref,
    off_ref,
    freq_ref,
    taper_ref,
    owner_ref,
    tile_ref,
    rows_ref,
    cols_ref,
    wide_ref,
    twist_ref,
    last_ref,
    w_ref,
    place_ref,
    base_ref,
    far_ref,
    left_a_ref,
    right_a_ref,
    left_b_ref,
    right_b_ref,
    image_ref,
    zplace_ref,
    yplace_ref,
    zsend_ref,
    zgot_ref,
    turn_ref,
    ysend_ref,
    ygot_ref,
    onehot_ref,
    masked_ref,
    xsend_ref,
    xgot_ref,
    lsend_ref,
    lgot_ref,
    local_sem,
    zplace_send,
    zplace_recv,
    yplace_send,
    yplace_recv,
    z_send,
    z_recv,
    y_send,
    y_recv,
    x_send,
    x_recv,
    l_send,
    l_recv,
):
    loads = [
        pltpu.make_async_copy(source, target, local_sem.at[k])
        for k, (source, target) in enumerate(
            (
                (off_hbm, off_ref),
                (freq_hbm, freq_ref),
                (taper_hbm, taper_ref),
                (owner_hbm, owner_ref),
                (tile_hbm, tile_ref),
                (vis_hbm, vis_ref),
                (rows_hbm, rows_ref),
                (cols_hbm, cols_ref),
                (twist_hbm, twist_ref),
                (last_hbm, last_ref),
                (wide_hbm, wide_ref),
            )
        )
    ]
    for load in loads:
        load.start()

    bl, row, col = lax.axis_index("bl"), lax.axis_index("row"), lax.axis_index("col")
    high_z, low_z = bl // 4, bl % 4
    x, y_hi = row // 2, row % 2
    me = y_hi * 8 + col

    def along_z(slot):
        return (slot, row, col)

    def along_y(slot):
        return (bl, x * 2 + slot // 8, slot % 8)

    def along_x(step):
        return (bl, (x + step) % 4 * 2 + y_hi, col)

    def final(step):
        return ((high_z + step % 4) % 4 * 4 + low_z, x * 2 + (y_hi + step // 4) % 2, col)

    barrier = pltpu.get_barrier_semaphore()

    def greet(device):
        pl.semaphore_signal(barrier, inc=1, device_id=device, device_id_type=MESH)

    def greet_lines(step, _):
        greet(along_z((bl + step) % 16))
        greet(along_y((me + step) % 16))
        return 0

    lax.fori_loop(1, 16, greet_lines, 0)
    for step in range(1, 4):
        greet(along_x(step))
        greet(final(4 + step))

    for load in loads[:5]:
        load.wait()
    places(owner_ref, tile_ref, place_ref)
    phasors(off_ref, freq_ref, base_ref, far_ref)
    weights(taper_ref, w_ref)

    def remote(source, target, send_sem, recv_sem, device):
        return pltpu.make_async_remote_copy(
            src_ref=source,
            dst_ref=target,
            send_sem=send_sem,
            recv_sem=recv_sem,
            device_id=device,
            device_id_type=MESH,
        )

    def zplace_copy(slot):
        return remote(
            place_ref, zplace_ref.at[bl], zplace_send.at[slot], zplace_recv.at[bl], along_z(slot)
        )

    def yplace_copy(slot):
        return remote(
            zplace_ref, yplace_ref.at[me], yplace_send.at[slot], yplace_recv.at[me], along_y(slot)
        )

    def z_copy(half):
        return lambda slot: remote(
            zsend_ref.at[half, slot],
            zgot_ref.at[half, bl],
            z_send.at[half, slot],
            z_recv.at[half, bl],
            along_z(slot),
        )

    def y_copy(half):
        return lambda slot: remote(
            ysend_ref.at[half, slot],
            ygot_ref.at[half, me],
            y_send.at[half, slot],
            y_recv.at[half, me],
            along_y(slot),
        )

    def others(mine, act):
        def body(k, _):
            act((mine + 8 + k // 2 * (1 - k % 2 * 2)) % 16)
            return 0

        lax.fori_loop(1, 16, body, 0)

    def arrive(mine, buffer, sem):
        def wait(slot):
            pltpu.make_async_copy(buffer.at[slot], buffer.at[slot], sem.at[slot]).wait()

        others(mine, wait)

    for load in loads[5:8]:
        load.wait()
    side_refs = ((left_a_ref, right_a_ref), (left_b_ref, right_b_ref))
    sides(0, 0, vis_ref, base_ref, far_ref, side_refs)
    for half in range(2):
        images(half, vis_ref, w_ref, base_ref, far_ref, side_refs, image_ref)
        subgrids(image_ref, rows_ref, cols_ref, zsend_ref.at[half])
        if half == 0:
            pl.semaphore_wait(barrier, 36)
            others(bl, lambda slot: zplace_copy(slot).start())
            zplace_ref[bl] = place_ref[...]
        others(bl, lambda slot: z_copy(half)(slot).start())
        zgot_ref[half, bl] = zsend_ref[half, bl]
    arrive(bl, zplace_ref, zplace_recv)
    others(me, lambda slot: yplace_copy(slot).start())
    yplace_ref[me] = zplace_ref[...]

    def turn(half):
        arrive(bl, zgot_ref.at[half], z_recv.at[half])
        for slot in range(16):
            turn_ref[pl.ds(slot * 17, 16)] = zgot_ref[half, slot].astype(F32)
        for slot in range(16):
            ysend_ref[half, slot] = turn_ref[pl.ds(slot, 16, stride=17)].astype(BF16)
        others(me, lambda slot: y_copy(half)(slot).start())
        ygot_ref[half, me] = ysend_ref[half, me]

    turn(0)
    turn(1)

    arrive(me, yplace_ref, yplace_recv)
    place = yplace_ref[...].reshape(256, 128).astype(F32).T[:SUB].astype(jnp.int32)
    wanted = ((place // TILES - x * 8 + 32) % 32).astype(F32).astype(BF16)
    column = place % TILES
    columns = [
        jnp.where(column // 256 == k, column - k * 256, -1).astype(F32).astype(BF16)
        for k in range(2)
    ]
    tiles = lax.broadcasted_iota(jnp.int32, (256, 256), 0).astype(F32).astype(BF16)
    one, zero = jnp.ones((256, 256), BF16), jnp.zeros((256, 256), BF16)
    for n in range(SUB):
        for k in range(2):
            onehot_ref[n // 16, pl.ds(k * 256, 256), pl.ds(n % 16 * 256, 256)] = jnp.where(
                tiles == columns[k][n : n + 1], one, zero
            )

    step_down = (lax.broadcasted_iota(jnp.int32, (16, 256), 0) // 8).astype(F32).astype(BF16)
    placed = 0.0
    for half in range(2):
        arrive(me, ygot_ref.at[half], y_recv.at[half])
        data = ygot_ref[half].reshape(256, 128).astype(F32).T
        for j in range(16):
            values = data[j * 8 : j * 8 + 8]
            values = jnp.concatenate([values, values], axis=0).astype(BF16)
            row_of = wanted[half * 16 + j : half * 16 + j + 1]
            row_of = jnp.broadcast_to(row_of, (16, 256)) - step_down
            for k in range(16):
                masked_ref[half, pl.ds(k * 16, 16), pl.ds(j * 256, 256)] = jnp.where(
                    row_of == jnp.full((16, 256), 2.0 * k, BF16), values, zero[:16]
                )
        placed += dot_t(masked_ref[half], onehot_ref[half])

    def x_copy(step):
        return remote(
            xsend_ref.at[step - 1],
            xgot_ref.at[step - 1],
            x_send.at[step - 1],
            x_recv.at[step - 1],
            along_x(step),
        )

    for step in (2, 1, 3):
        xsend_ref[step - 1] = placed[step * 64 : step * 64 + 64].astype(BF16)
        x_copy(step).start()
    total = placed[:64]
    for step in (1, 3, 2):
        x_copy(step).wait_recv()
        total += xgot_ref[step - 1].astype(F32)

    mine = high_z * 2 + y_hi

    def l_copy(step):
        target = (y_hi + step // 4) % 2 * 4 + (high_z + step % 4) % 4
        return remote(
            lsend_ref.at[target], lgot_ref.at[mine], l_send.at[step], l_recv.at[mine], final(step)
        )

    for m in range(8):
        piece = total[m * 8 : m * 8 + 8]
        lsend_ref[m] = jnp.concatenate([piece[:, :256], piece[:, 256:]], axis=0).astype(BF16)
    for step in (2, 6, 1, 3, 5, 7, 4):
        l_copy(step).start()
    lgot_ref[mine] = lsend_ref[y_hi * 4 + high_z]

    others(bl, lambda slot: zplace_copy(slot).wait_send())
    others(me, lambda slot: yplace_copy(slot).wait_send())
    for half in range(2):
        others(bl, lambda slot: z_copy(half)(slot).wait_send())
        others(me, lambda slot: y_copy(half)(slot).wait_send())
    for step in range(1, 4):
        x_copy(step).wait_send()
    for load in loads[8:]:
        load.wait()

    for step in range(1, 8):
        source = (high_z + step % 4) % 4 * 2 + (y_hi + step // 4) % 2
        pltpu.make_async_copy(lgot_ref.at[source], lgot_ref.at[source], l_recv.at[source]).wait()
    upper = lax.broadcasted_iota(jnp.int32, (8, TILES), 0) < 4
    real, imag = [], []
    for h in range(4):
        even, odd = (
            jnp.concatenate([piece[:8], piece[8:]], axis=1)
            for piece in (lgot_ref[2 * h].astype(F32), lgot_ref[2 * h + 1].astype(F32))
        )
        real.append(jnp.where(upper, even, pltpu.roll(odd, 4, 0)))
        imag.append(jnp.where(upper, pltpu.roll(even, 4, 0), odd))
    grid = jnp.concatenate(real + imag, axis=0)
    result = column_transform(grid, wide_ref, twist_ref, last_ref)
    for part in range(2):
        for k in range(4):
            out_ref[pl.ds(k * 2 + part, SUB, stride=8), :] = result[
                part * 32 : part * 32 + 32, k * 128 : k * 128 + 128
            ]
    for step in range(1, 8):
        l_copy(step).wait_send()


def on_device(visibilities, offsets, frequencies, taper_curve, owner_index, tile_index):
    rows, cols, wide, twist, last = (jnp.asarray(table) for table in make_tables())
    operands = (
        visibilities,
        offsets.reshape(64, 64),
        frequencies.reshape(1, 16),
        taper_curve.reshape(1, SUB),
        owner_index.reshape(1, 32),
        tile_index.reshape(1, 32),
        rows,
        cols,
        wide,
        twist,
        last,
    )
    result = pl.pallas_call(
        kernel,
        out_shape=jax.ShapeDtypeStruct((256, 128), F32),
        in_specs=[pl.BlockSpec(memory_space=pl.ANY)] * len(operands),
        out_specs=pl.BlockSpec(memory_space=pltpu.VMEM),
        scratch_shapes=[pltpu.VMEM(operand.shape, operand.dtype) for operand in operands]
        + [
            pltpu.VMEM((2, 64, 128), F32),
            pltpu.VMEM((1, 128), jnp.int32),
            pltpu.VMEM((2, 8, 520, 128), F32),
            pltpu.VMEM((2, 2, 64, 1024), F32),
            pltpu.VMEM((256, 1024), BF16),
            pltpu.VMEM((256, 1024), BF16),
            pltpu.VMEM((256, 1024), BF16),
            pltpu.VMEM((256, 1024), BF16),
            pltpu.VMEM((1024, 256), BF16),
            pltpu.VMEM((16, 1, 128), jnp.int32),
            pltpu.VMEM((16, 16, 1, 128), jnp.int32),
            pltpu.VMEM((2, 16, 16, 128), BF16),
            pltpu.VMEM((2, 16, 16, 128), BF16),
            pltpu.VMEM((16 * 17, 128), F32),
            pltpu.VMEM((2, 16, 16, 128), BF16),
            pltpu.VMEM((2, 16, 16, 128), BF16),
            pltpu.VMEM((2, TILES, 4096), BF16),
            pltpu.VMEM((2, 256, 4096), BF16),
            pltpu.VMEM((3, 64, TILES), BF16),
            pltpu.VMEM((3, 64, TILES), BF16),
            pltpu.VMEM((8, 16, 256), BF16),
            pltpu.VMEM((8, 16, 256), BF16),
            pltpu.SemaphoreType.DMA((len(operands),)),
        ]
        + [pltpu.SemaphoreType.DMA((16,))] * 4
        + [pltpu.SemaphoreType.DMA((2, 16))] * 4
        + [pltpu.SemaphoreType.DMA((3,))] * 2
        + [pltpu.SemaphoreType.DMA((8,))] * 2,
        compiler_params=pltpu.CompilerParams(
            collective_id=0, has_side_effects=True, vmem_limit_bytes=60 * 1024 * 1024
        ),
    )(*operands)
    return result.reshape(128, 2, 128).transpose(1, 0, 2).reshape(1, 1, 2, GC)


def solution(mesh):
    in_specs = (
        P(("bl", "row", "col"), None, None),
        P(("bl", "row", "col"), None, None),
        P(),
        P(),
        P(("bl", "row", "col"), None),
        P(("bl", "row", "col")),
    )
    out_specs = P("row", ("bl", "col"), None, None)
    return jax.shard_map(
        on_device, mesh=mesh, in_specs=in_specs, out_specs=out_specs, check_vma=False
    )
```

```python
import math

import jax
import jax.numpy as jnp
import numpy as np
from jax import lax
from jax.experimental import pallas as pl
from jax.experimental.pallas import tpu as pltpu
from jax.sharding import PartitionSpec as P

MESH = pl.DeviceIdType.MESH
SUB = 32
GC = 16384
TILES = GC // SUB
F32 = jnp.float32
BF16 = jnp.bfloat16


def split_np(table):
    high = table.astype(BF16)
    low = (table - high.astype(np.float64)).astype(BF16)
    return np.stack([high, low])


def by_lanes(table):
    rows, lanes = table.shape[-2:]
    pieces = table.reshape(table.shape[:-1] + (lanes // 128, 128))
    return np.ascontiguousarray(np.moveaxis(pieces, -2, -3))


def joined(ref, *index):
    return jnp.concatenate([ref[(*index, k)] for k in range(ref.shape[-3])], axis=1)


def make_tables():
    index = np.arange(SUB)
    angle = 2.0 * np.pi * (index[:, None] * index[None, :] % SUB) / SUB
    cos, sin = np.cos(angle), np.sin(angle)
    order = pixel_order()
    cos_in, sin_in = cos[:, order], sin[:, order]
    rows = np.zeros((2, 4, SUB, 4, 2, SUB))
    for b in range(4):
        rows[0, b, :, b, 0], rows[0, b, :, b, 1] = cos_in, sin_in
        rows[1, b, :, b, 0], rows[1, b, :, b, 1] = sin_in, -cos_in
    rows = split_np(rows.reshape(2, 128, 256))
    cos_in, sin_in = cos[order], sin[order]
    straight = np.stack([[cos_in, -sin_in], [sin_in, cos_in]])
    crossed = np.stack([[-sin_in, -cos_in], [cos_in, -sin_in]])
    cols = np.stack([straight, crossed], axis=1)
    cols = cols.reshape(2, 2, 2, SUB, 8, 4).transpose(0, 3, 1, 4, 2, 5).reshape(64, 128)
    cols = split_np(np.tile(cols, (2, 1)))
    cols = np.concatenate([cols[0], cols[0], cols[1]])
    wide = np.arange(TILES)
    wide_angle = 2.0 * np.pi * (wide[:, None] * wide[None, :] % TILES) / TILES
    wide_table = np.concatenate([np.cos(wide_angle), np.sin(wide_angle)], axis=1)
    twist_angle = 2.0 * np.pi * (index[:, None] * wide[None, :]) / GC
    twist = (np.stack([np.cos(twist_angle), np.sin(twist_angle)]) / 128.0).astype(np.float32)
    last = np.block([[cos, -sin], [sin, cos]])
    return (
        by_lanes(rows),
        cols,
        by_lanes(split_np(wide_table)),
        twist,
        split_np(last),
    )


def dot(a, b):
    return lax.dot_general(a, b, (((1,), (0,)), ((), ())), preferred_element_type=F32)


def dot_t(a, b):
    return lax.dot_general(a, b, (((1,), (1,)), ((), ())), preferred_element_type=F32)


def split(x):
    high = x.astype(BF16)
    return high, (x - high.astype(F32)).astype(BF16)


def cmul(ar, ai, br, bi):
    return ar * br - ai * bi, ar * bi + ai * br


def three(x, rows):
    high = x.astype(BF16).astype(F32)
    middle = (x - high).astype(BF16).astype(F32)
    low = x - high - middle
    place = lax.broadcasted_iota(jnp.int32, (rows, x.shape[1]), 0)
    parts = jnp.where(place == 0, high, jnp.where(place == 1, middle, jnp.where(place == 2, low, 0.0)))
    return parts.astype(BF16)


def matches(shape, left, right):
    row, lane = lax.broadcasted_iota(jnp.int32, shape, 0), lax.broadcasted_iota(jnp.int32, shape, 1)
    return (left(row) == right(lane)).astype(F32).astype(BF16)


def pixel(k):
    slot = k % SUB
    return 16 + jnp.where(slot < 16, slot, jnp.where(slot == 16, -16, 16 - slot))


def weights(taper_ref, w_ref):
    parts = three(taper_ref[...], 16)
    along = dot(parts, matches((SUB, 128), lambda i: i, pixel))
    down = dot_t(matches((64, SUB), pixel, lambda k: k), parts)
    along, down = jnp.sum(along, axis=0, keepdims=True), jnp.sum(down, axis=1, keepdims=True)
    lane = lax.broadcasted_iota(jnp.int32, (64, 128), 1) // 64
    for half in range(2):
        w_ref[half] = jnp.where(lane == half, down * along * (1.0 / 1024.0), 0.0)


def place_order(lane):
    slot = lane % SUB
    return slot // 16 * 16 + slot // 4 % 2 * 8 + slot // 8 % 2 * 4 + slot % 4


def places(owner_ref, tile_ref):
    row = lax.broadcasted_iota(jnp.int32, (16, SUB), 0)
    parts = jnp.where(row == 0, owner_ref[...], jnp.where(row == 1, tile_ref[...], 0))
    order = matches((SUB, 128), lambda i: i, place_order)
    both = dot(parts.astype(F32).astype(BF16), order)
    lane = lax.broadcasted_iota(jnp.int32, (16, 128), 1)
    return jnp.where(lane < SUB, both[0:1], both[1:2]).astype(BF16)


def phasors(off_ref, freq_ref, base_ref, far_ref):
    spread = matches((64, 1024), lambda i: i, lambda k: k // 16)
    repeat = matches((16, 1024), lambda i: i, lambda k: k % 16)
    freq = jnp.sum(dot(three(freq_ref[...], 16), repeat), axis=0, keepdims=True)
    scaled = dot(off_ref[...], spread) * freq
    theta = scaled * (2.0 * math.pi / SUB)
    square = theta * theta
    cos = jnp.full_like(square, -1.0 / math.factorial(14))
    sin = jnp.full_like(square, -1.0 / math.factorial(15))
    for order in range(6, -1, -1):
        sign = 1.0 if order % 2 == 0 else -1.0
        cos = cos * square + sign / math.factorial(2 * order)
        sin = sin * square + sign / math.factorial(2 * order + 1)
    z = [(jnp.ones_like(cos), jnp.zeros_like(cos)), (cos, sin * theta)]
    for p in range(2, 8):
        z.append(cmul(*z[p // 2], *z[p - p // 2]))
    for p in range(8):
        for part in range(2):
            for k in range(8):
                base_ref[part, k, pl.ds(p * 65, 64)] = z[p][part][:, k * 128 : k * 128 + 128]
    z8 = cmul(*z[4], *z[4])
    for e, value in enumerate((z8, cmul(*z8, *z8))):
        for part in range(2):
            far_ref[e, part] = value[part]


def pixel_order():
    slot = np.arange(SUB)
    return 16 + np.where(slot < 16, slot, np.where(slot == 16, -16, 16 - slot))


def block_sides(block, slot, vis_ref, base_ref, far_ref, left_ref, right_ref):
    chunk = 256
    first = lax.broadcasted_iota(jnp.int32, (8, chunk), 0) == 0
    for start in range(0, 1024, chunk):
        lanes = pl.ds(start, chunk)
        for side, target in enumerate((left_ref, right_ref)):
            row = 2 * block + side
            low = [
                jnp.concatenate(
                    [
                        base_ref[part, start // 128 + k, pl.ds(row, 8, stride=65), :]
                        for k in range(chunk // 128)
                    ],
                    axis=1,
                )
                for part in (0, 1)
            ]
            far = [
                [jnp.broadcast_to(far_ref[e, part, pl.ds(row, 1), lanes], (8, chunk)) for part in (0, 1)]
                for e in (0, 1)
            ]
            near = (low, cmul(*low, *far[0]))
            if side == 0:
                vis = vis_ref[block, :, lanes].astype(F32)
                vr, vi = (jnp.broadcast_to(vis[k : k + 1], (8, chunk)) for k in (0, 1))
                products = [(vr * c, vi * s, vr * s, vi * c) for c, s in near]
                plus = [(a - b, d + e) for a, b, d, e in products]
                minus = [(a + b, e - d) for a, b, d, e in products]
                last = cmul(vr, vi, far[1][0], -far[1][1])
            else:
                plus, minus = near, [(c, -s) for c, s in near]
                last = (far[1][0], -far[1][1])
            minus[0] = tuple(jnp.where(first, x, y) for x, y in zip(last, minus[0]))
            for part in range(2):
                for k, pieces in enumerate((plus, minus)):
                    rows = pl.ds(slot * 64 + part * 32 + k * 16, 16)
                    target[rows, lanes] = jnp.concatenate(
                        [piece[part] for piece in pieces], axis=0
                    ).astype(BF16)


def sides(four, which, vis_ref, base_ref, far_ref, side_refs):
    for b in range(4):
        block_sides(four * 4 + b, b, vis_ref, base_ref, far_ref, *side_refs[which])


def images(vis_ref, w_ref, base_ref, far_ref, side_refs, image_ref):
    def image(four, which):
        left_ref, right_ref = side_refs[which]
        product = dot_t(left_ref[...], right_ref[...])
        for b in range(4):
            block = product[b * 64 : b * 64 + 64, b // 2 * 128 : b // 2 * 128 + 128] * w_ref[b % 2]
            high, low = split(block)
            rows = pl.ds(four * 256 + b * 64, 64)
            image_ref[rows, 0:128], image_ref[rows, 128:256] = high, low

    def pair(gp, _):
        sides(2 * gp + 1, 1, vis_ref, base_ref, far_ref, side_refs)
        image(2 * gp, 0)
        sides(jnp.minimum(2 * gp + 2, 7), 0, vis_ref, base_ref, far_ref, side_refs)
        image(2 * gp + 1, 1)
        return 0

    sides(0, 0, vis_ref, base_ref, far_ref, side_refs)
    lax.fori_loop(0, 4, pair, 0)


def subgrids(image, rows_ref, cols_ref, out_ref):
    lane = lax.broadcasted_iota(jnp.int32, (256, 128), 1)
    lower = lane < 64
    turned = dot(image, cols_ref[pl.ds(0, 256)]) + dot(image[:, :128], cols_ref[pl.ds(256, 128)])
    straight, crossed = [], []
    for k in range(2):
        even, odd = turned[k * 512 : k * 512 + 256], turned[k * 512 + 256 : k * 512 + 512]
        straight.append(jnp.where(lower, even, pltpu.roll(odd, 64, 1)))
        crossed.append(jnp.where(lower, pltpu.roll(even, 64, 1), odd))
    total = 0.0
    for part, pieces in enumerate((straight, crossed)):
        high, low = split(jnp.concatenate(pieces, axis=1))
        rows_high, rows_low = joined(rows_ref, 0, part), joined(rows_ref, 1, part)
        total += dot(rows_high, high) + dot(rows_high, low) + dot(rows_low, high)
    pieces = [
        total[b * 32 : b * 32 + 32, k * 128 : k * 128 + 128] for k in range(2) for b in range(4)
    ]
    group = lane[:32] // 8 % 8
    for bit in (1, 2, 4):
        clear = group & bit == 0
        for t in range(8):
            if t & bit == 0:
                x, y = pieces[t], pieces[t | bit]
                pieces[t] = jnp.where(clear, x, pltpu.roll(y, bit * 8, 1))
                pieces[t | bit] = jnp.where(clear, pltpu.roll(x, 128 - bit * 8, 1), y)
    for h in range(4):
        for l in range(4):
            both = [pieces[h * 2 + y][l * 8 : l * 8 + 8] for y in range(2)]
            out_ref[h * 4 + l, 0:16] = jnp.concatenate(both, axis=0).astype(BF16)


def column_transform(grid, wide_ref, twist_ref, last_ref):
    high, low = split(grid)
    wide_high, wide_low = joined(wide_ref, 0), joined(wide_ref, 1)
    wide = dot(high, wide_high) + dot(low, wide_high) + dot(high, wide_low)
    real = wide[:SUB, :TILES] - wide[SUB:, TILES:]
    imag = wide[SUB:, :TILES] + wide[:SUB, TILES:]
    real, imag = cmul(real, imag, twist_ref[0], twist_ref[1])
    high, low = split(jnp.concatenate([real, imag], axis=0))
    return dot(last_ref[0], high) + dot(last_ref[0], low) + dot(last_ref[1], high)


def kernel(
    vis_hbm,
    off_hbm,
    freq_hbm,
    taper_hbm,
    owner_hbm,
    tile_hbm,
    rows_hbm,
    cols_hbm,
    wide_hbm,
    twist_hbm,
    last_hbm,
    out_ref,
    vis_ref,
    off_ref,
    freq_ref,
    taper_ref,
    owner_ref,
    tile_ref,
    rows_ref,
    cols_ref,
    wide_ref,
    twist_ref,
    last_ref,
    w_ref,
    base_ref,
    far_ref,
    left_a_ref,
    right_a_ref,
    left_b_ref,
    right_b_ref,
    image_ref,
    zsend_ref,
    zgot_ref,
    turn_ref,
    ysend_ref,
    ygot_ref,
    onehot_ref,
    masked_ref,
    xsend_ref,
    xgot_ref,
    lsend_ref,
    lgot_ref,
    local_sem,
    z_send,
    z_recv,
    y_send,
    y_recv,
    x_send,
    x_recv,
    l_send,
    l_recv,
):
    loads = [
        pltpu.make_async_copy(source, target, local_sem.at[k])
        for k, (source, target) in enumerate(
            (
                (off_hbm, off_ref),
                (freq_hbm, freq_ref),
                (taper_hbm, taper_ref),
                (owner_hbm, owner_ref),
                (tile_hbm, tile_ref),
                (vis_hbm, vis_ref),
                (rows_hbm, rows_ref),
                (cols_hbm, cols_ref),
                (twist_hbm, twist_ref),
                (last_hbm, last_ref),
                (wide_hbm, wide_ref),
            )
        )
    ]
    for load in loads:
        load.start()

    bl, row, col = lax.axis_index("bl"), lax.axis_index("row"), lax.axis_index("col")
    high_z, low_z = bl // 4, bl % 4
    x, y_hi = row // 2, row % 2
    me = y_hi * 8 + col

    def along_z(slot):
        return (slot, row, col)

    def along_y(slot):
        return (bl, x * 2 + slot // 8, slot % 8)

    def along_x(step):
        return (bl, (x + step) % 4 * 2 + y_hi, col)

    def final(step):
        return ((high_z + step % 4) % 4 * 4 + low_z, x * 2 + (y_hi + step // 4) % 2, col)

    barrier = pltpu.get_barrier_semaphore()

    def greet(device):
        pl.semaphore_signal(barrier, inc=1, device_id=device, device_id_type=MESH)

    def others(mine, act):
        def body(k, _):
            act((mine + 8 + k // 2 * (1 - k % 2 * 2)) % 16)
            return 0

        lax.fori_loop(1, 16, body, 0)

    for step in (2, 1, 3):
        greet(final(4 + step))
    others(bl, lambda slot: greet(along_z(slot)))
    others(me, lambda slot: greet(along_y(slot)))
    for step in (2, 1, 3):
        greet(along_x(step))

    for load in loads[:5]:
        load.wait()
    phasors(off_ref, freq_ref, base_ref, far_ref)
    weights(taper_ref, w_ref)
    place_rows = places(owner_ref, tile_ref)
    for slot in range(16):
        zsend_ref[0, slot, 16:32] = place_rows

    def remote(source, target, send_sem, recv_sem, device):
        return pltpu.make_async_remote_copy(
            src_ref=source,
            dst_ref=target,
            send_sem=send_sem,
            recv_sem=recv_sem,
            device_id=device,
            device_id_type=MESH,
        )

    def part(ref, half, slot):
        return ref.at[half, slot, pl.ds(0, (32, 16)[half])]

    def z_copy(half, slot):
        source, target = part(zsend_ref, half, slot), part(zgot_ref, half, bl)
        return remote(source, target, z_send.at[half], z_recv.at[half], along_z(slot))

    def y_copy(half, slot):
        source, target = part(ysend_ref, half, slot), part(ygot_ref, half, me)
        return remote(source, target, y_send.at[half], y_recv.at[half], along_y(slot))

    def wait_all(ref, half, sem):
        arrived = ref.at[half, pl.ds(0, 15), pl.ds(0, (32, 16)[half])]
        pltpu.make_async_copy(arrived, arrived, sem.at[half]).wait()

    for load in loads[5:8]:
        load.wait()
    side_refs = ((left_a_ref, right_a_ref), (left_b_ref, right_b_ref))
    images(vis_ref, w_ref, base_ref, far_ref, side_refs, image_ref)
    for half in range(2):
        image = image_ref[half * 1024 : half * 1024 + 1024]
        subgrids(image, rows_ref, cols_ref, zsend_ref.at[half])
    pl.semaphore_wait(barrier, 36)
    for half in range(2):
        others(bl, lambda slot: z_copy(half, slot).start())
        rows = slice(0, (32, 16)[half])
        zgot_ref[half, bl, rows] = zsend_ref[half, bl, rows]

    row_of_slot = lax.broadcasted_iota(jnp.int32, (16, 128), 0)

    def turn(half):
        wait_all(zgot_ref, half, z_recv)
        for slot in range(16):
            turn_ref[pl.ds(slot * 17, 16)] = zgot_ref[half, slot, 0:16].astype(F32)
        for slot in range(16):
            ysend_ref[half, slot, 0:16] = turn_ref[pl.ds(slot, 16, stride=17)].astype(BF16)
        if half == 0:
            places_here = jnp.zeros((16, 128), F32)
            for slot in range(16):
                places_here = jnp.where(
                    row_of_slot == slot, zgot_ref[0, slot, 16:32].astype(F32), places_here
                )
            for slot in range(16):
                ysend_ref[0, slot, 16:32] = places_here.astype(BF16)
        others(me, lambda slot: y_copy(half, slot).start())
        rows = slice(0, (32, 16)[half])
        ygot_ref[half, me, rows] = ysend_ref[half, me, rows]

    turn(0)
    turn(1)

    wait_all(ygot_ref, 0, y_recv)
    place = ygot_ref[0, :, 16:32].reshape(256, 128).astype(F32).T.astype(jnp.int32)
    owner, tile = place[:SUB], place[SUB : 2 * SUB]
    wanted = (owner // 8 * 4 + tile // 64 - x * 8 + 32) % 32
    wanted = wanted.astype(F32).astype(BF16)
    column = owner % 8 * 64 + tile % 64
    columns = [
        jnp.where(column // 256 == k, column - k * 256, -1).astype(F32).astype(BF16)
        for k in range(2)
    ]
    tiles = lax.broadcasted_iota(jnp.int32, (256, 256), 0).astype(F32).astype(BF16)
    one, zero = jnp.ones((256, 256), BF16), jnp.zeros((256, 256), BF16)
    for n in range(SUB):
        for k in range(2):
            onehot_ref[n // 16, pl.ds(k * 256, 256), pl.ds(n % 16 * 256, 256)] = jnp.where(
                tiles == columns[k][n : n + 1], one, zero
            )

    step_down = (lax.broadcasted_iota(jnp.int32, (16, 256), 0) // 8).astype(F32).astype(BF16)
    placed = 0.0
    for half in range(2):
        if half == 1:
            wait_all(ygot_ref, 1, y_recv)
        data = ygot_ref[half, :, 0:16].reshape(256, 128).astype(F32).T
        for j in range(16):
            values = data[j * 8 : j * 8 + 8]
            values = jnp.concatenate([values, values], axis=0).astype(BF16)
            row_of = wanted[half * 16 + j : half * 16 + j + 1]
            row_of = jnp.broadcast_to(row_of, (16, 256)) - step_down
            for k in range(16):
                masked_ref[half, pl.ds(k * 16, 16), pl.ds(j * 256, 256)] = jnp.where(
                    row_of == jnp.full((16, 256), 2.0 * k, BF16), values, zero[:16]
                )
        placed += dot_t(masked_ref[half], onehot_ref[half])

    def x_copy(step):
        return remote(
            xsend_ref.at[step - 1],
            xgot_ref.at[step - 1],
            x_send.at[step - 1],
            x_recv.at[step - 1],
            along_x(step),
        )

    for step in (2, 1, 3):
        xsend_ref[step - 1] = placed[step * 64 : step * 64 + 64].astype(BF16)
        x_copy(step).start()
    total = placed[:64]
    for step in (1, 3, 2):
        x_copy(step).wait_recv()
        total += xgot_ref[step - 1].astype(F32)

    mine = high_z * 2 + y_hi

    def l_copy(step):
        target = (y_hi + step // 4) % 2 * 4 + (high_z + step % 4) % 4
        return remote(
            lsend_ref.at[target], lgot_ref.at[mine], l_send, l_recv, final(step)
        )

    for m in range(8):
        piece = total[m * 8 : m * 8 + 8]
        lsend_ref[m] = jnp.concatenate([piece[:, :256], piece[:, 256:]], axis=0).astype(BF16)
    for step in (2, 6, 1, 3, 5, 7, 4):
        l_copy(step).start()
    lgot_ref[mine] = lsend_ref[y_hi * 4 + high_z]

    for half in range(2):
        wait_all(zsend_ref, half, z_send)
        wait_all(ysend_ref, half, y_send)
    for step in range(1, 4):
        x_copy(step).wait_send()
    for load in loads[8:]:
        load.wait()

    seven = lgot_ref.at[pl.ds(0, 7)]
    pltpu.make_async_copy(seven, seven, l_recv).wait()
    upper = lax.broadcasted_iota(jnp.int32, (8, TILES), 0) < 4
    real, imag = [], []
    for h in range(4):
        even, odd = (
            jnp.concatenate([piece[:8], piece[8:]], axis=1)
            for piece in (lgot_ref[2 * h].astype(F32), lgot_ref[2 * h + 1].astype(F32))
        )
        real.append(jnp.where(upper, even, pltpu.roll(odd, 4, 0)))
        imag.append(jnp.where(upper, pltpu.roll(even, 4, 0), odd))
    grid = jnp.concatenate(real + imag, axis=0)
    result = column_transform(grid, wide_ref, twist_ref, last_ref)
    for part in range(2):
        for k in range(4):
            out_ref[pl.ds(k * 2 + part, SUB, stride=8), :] = result[
                part * 32 : part * 32 + 32, k * 128 : k * 128 + 128
            ]
    pltpu.make_async_copy(seven, seven, l_send).wait()


def on_device(visibilities, offsets, frequencies, taper_curve, owner_index, tile_index):
    rows, cols, wide, twist, last = (jnp.asarray(table) for table in make_tables())
    operands = (
        visibilities,
        offsets.reshape(64, 64),
        frequencies.reshape(1, 16),
        taper_curve.reshape(1, SUB),
        owner_index.reshape(1, 32),
        tile_index.reshape(1, 32),
        rows,
        cols,
        wide,
        twist,
        last,
    )
    result = pl.pallas_call(
        kernel,
        out_shape=jax.ShapeDtypeStruct((256, 128), F32),
        in_specs=[pl.BlockSpec(memory_space=pl.ANY)] * len(operands),
        out_specs=pl.BlockSpec(memory_space=pltpu.VMEM),
        scratch_shapes=[pltpu.VMEM(operand.shape, operand.dtype) for operand in operands]
        + [
            pltpu.VMEM((2, 64, 128), F32),
            pltpu.VMEM((2, 8, 520, 128), F32),
            pltpu.VMEM((2, 2, 64, 1024), F32),
            pltpu.VMEM((256, 1024), BF16),
            pltpu.VMEM((256, 1024), BF16),
            pltpu.VMEM((256, 1024), BF16),
            pltpu.VMEM((256, 1024), BF16),
            pltpu.VMEM((2048, 256), BF16),
            pltpu.VMEM((2, 16, 32, 128), BF16),
            pltpu.VMEM((2, 16, 32, 128), BF16),
            pltpu.VMEM((16 * 17, 128), F32),
            pltpu.VMEM((2, 16, 32, 128), BF16),
            pltpu.VMEM((2, 16, 32, 128), BF16),
            pltpu.VMEM((2, TILES, 4096), BF16),
            pltpu.VMEM((2, 256, 4096), BF16),
            pltpu.VMEM((3, 64, TILES), BF16),
            pltpu.VMEM((3, 64, TILES), BF16),
            pltpu.VMEM((8, 16, 256), BF16),
            pltpu.VMEM((8, 16, 256), BF16),
            pltpu.SemaphoreType.DMA((len(operands),)),
        ]
        + [pltpu.SemaphoreType.DMA((2,))] * 4
        + [pltpu.SemaphoreType.DMA((3,))] * 2
        + [pltpu.SemaphoreType.DMA] * 2,
        compiler_params=pltpu.CompilerParams(
            collective_id=0, has_side_effects=True, vmem_limit_bytes=60 * 1024 * 1024
        ),
    )(*operands)
    return result.reshape(128, 2, 128).transpose(1, 0, 2).reshape(1, 1, 2, GC)


def solution(mesh):
    in_specs = (
        P(("bl", "row", "col"), None, None),
        P(("bl", "row", "col"), None, None),
        P(),
        P(),
        P(("bl", "row", "col"), None),
        P(("bl", "row", "col")),
    )
    out_specs = P("row", ("bl", "col"), None, None)
    return jax.shard_map(
        on_device, mesh=mesh, in_specs=in_specs, out_specs=out_specs, check_vma=False
    )
```

```python
import math

import jax
import jax.numpy as jnp
import numpy as np
from jax import lax
from jax.experimental import pallas as pl
from jax.experimental.pallas import tpu as pltpu
from jax.sharding import PartitionSpec as P

MESH = pl.DeviceIdType.MESH
SUB = 32
GC = 16384
TILES = GC // SUB
F32 = jnp.float32
BF16 = jnp.bfloat16


def split_np(table):
    high = table.astype(BF16)
    low = (table - high.astype(np.float64)).astype(BF16)
    return np.stack([high, low])


def by_lanes(table):
    rows, lanes = table.shape[-2:]
    pieces = table.reshape(table.shape[:-1] + (lanes // 128, 128))
    return np.ascontiguousarray(np.moveaxis(pieces, -2, -3))


def joined(ref, *index):
    return jnp.concatenate([ref[(*index, k)] for k in range(ref.shape[-3])], axis=1)


def make_tables():
    index = np.arange(SUB)
    angle = 2.0 * np.pi * (index[:, None] * index[None, :] % SUB) / SUB
    cos, sin = np.cos(angle), np.sin(angle)
    order = pixel_order()
    cos_in, sin_in = cos[:, order], sin[:, order]
    rows = np.zeros((2, 4, SUB, 4, 2, SUB))
    for b in range(4):
        rows[0, b, :, b, 0], rows[0, b, :, b, 1] = cos_in, sin_in
        rows[1, b, :, b, 0], rows[1, b, :, b, 1] = sin_in, -cos_in
    rows = split_np(rows.reshape(2, 128, 256))
    cos_in, sin_in = cos[order], sin[order]
    straight = np.stack([[cos_in, -sin_in], [sin_in, cos_in]])
    crossed = np.stack([[-sin_in, -cos_in], [cos_in, -sin_in]])
    cols = np.stack([straight, crossed], axis=1)
    cols = cols.reshape(2, 2, 2, SUB, 8, 4).transpose(0, 3, 1, 4, 2, 5).reshape(64, 128)
    cols = split_np(np.tile(cols, (2, 1)))
    cols = np.concatenate([cols[0], cols[0], cols[1]])
    wide = np.arange(TILES)
    wide_angle = 2.0 * np.pi * (wide[:, None] * wide[None, :] % TILES) / TILES
    wide_table = np.concatenate([np.cos(wide_angle), np.sin(wide_angle)], axis=1)
    twist_angle = 2.0 * np.pi * (index[:, None] * wide[None, :]) / GC
    twist = (np.stack([np.cos(twist_angle), np.sin(twist_angle)]) / 128.0).astype(np.float32)
    last = np.block([[cos, -sin], [sin, cos]])
    return (
        by_lanes(rows),
        cols,
        by_lanes(split_np(wide_table)),
        twist,
        split_np(last),
    )


def dot(a, b):
    return lax.dot_general(a, b, (((1,), (0,)), ((), ())), preferred_element_type=F32)


def dot_t(a, b):
    return lax.dot_general(a, b, (((1,), (1,)), ((), ())), preferred_element_type=F32)


def split(x):
    high = x.astype(BF16)
    return high, (x - high.astype(F32)).astype(BF16)


def cmul(ar, ai, br, bi):
    return ar * br - ai * bi, ar * bi + ai * br


def three(x, rows):
    high = x.astype(BF16).astype(F32)
    middle = (x - high).astype(BF16).astype(F32)
    low = x - high - middle
    place = lax.broadcasted_iota(jnp.int32, (rows, x.shape[1]), 0)
    parts = jnp.where(place == 0, high, jnp.where(place == 1, middle, jnp.where(place == 2, low, 0.0)))
    return parts.astype(BF16)


def matches(shape, left, right):
    row, lane = lax.broadcasted_iota(jnp.int32, shape, 0), lax.broadcasted_iota(jnp.int32, shape, 1)
    return (left(row) == right(lane)).astype(F32).astype(BF16)


def pixel(k):
    slot = k % SUB
    return 16 + jnp.where(slot < 16, slot, jnp.where(slot == 16, -16, 16 - slot))


def weights(taper_ref, w_ref):
    parts = three(taper_ref[...], 16)
    along = dot(parts, matches((SUB, 128), lambda i: i, pixel))
    down = dot_t(matches((64, SUB), pixel, lambda k: k), parts)
    along, down = jnp.sum(along, axis=0, keepdims=True), jnp.sum(down, axis=1, keepdims=True)
    lane = lax.broadcasted_iota(jnp.int32, (64, 128), 1) // 64
    for half in range(2):
        w_ref[half] = jnp.where(lane == half, down * along * (1.0 / 1024.0), 0.0)


def place_order(lane):
    slot = lane % SUB
    return slot // 16 * 16 + slot // 4 % 2 * 8 + slot // 8 % 2 * 4 + slot % 4


def places(owner_ref, tile_ref):
    row = lax.broadcasted_iota(jnp.int32, (16, SUB), 0)
    parts = jnp.where(row == 0, owner_ref[...], jnp.where(row == 1, tile_ref[...], 0))
    order = matches((SUB, 128), lambda i: i, place_order)
    both = dot(parts.astype(F32).astype(BF16), order)
    lane = lax.broadcasted_iota(jnp.int32, (1, 128), 1)
    return jnp.where(lane < SUB, both[0:1], both[1:2])


def phasors(off_ref, freq_ref, base_ref, far_ref):
    spread = matches((64, 1024), lambda i: i, lambda k: k // 16)
    repeat = matches((16, 1024), lambda i: i, lambda k: k % 16)
    freq = jnp.sum(dot(three(freq_ref[...], 16), repeat), axis=0, keepdims=True)
    scaled = dot(off_ref[...], spread) * freq
    theta = scaled * (2.0 * math.pi / SUB)
    square = theta * theta
    cos = jnp.full_like(square, -1.0 / math.factorial(14))
    sin = jnp.full_like(square, -1.0 / math.factorial(15))
    for order in range(6, -1, -1):
        sign = 1.0 if order % 2 == 0 else -1.0
        cos = cos * square + sign / math.factorial(2 * order)
        sin = sin * square + sign / math.factorial(2 * order + 1)
    z = [(jnp.ones_like(cos), jnp.zeros_like(cos)), (cos, sin * theta)]
    for p in range(2, 8):
        z.append(cmul(*z[p // 2], *z[p - p // 2]))
    for p in range(8):
        for part in range(2):
            for k in range(8):
                base_ref[part, k, pl.ds(p * 65, 64)] = z[p][part][:, k * 128 : k * 128 + 128]
    z8 = cmul(*z[4], *z[4])
    for e, value in enumerate((z8, cmul(*z8, *z8))):
        for part in range(2):
            far_ref[e, part] = value[part]


def pixel_order():
    slot = np.arange(SUB)
    return 16 + np.where(slot < 16, slot, np.where(slot == 16, -16, 16 - slot))


def block_sides(block, slot, vis_ref, base_ref, far_ref, left_ref, right_ref):
    chunk = 256
    first = lax.broadcasted_iota(jnp.int32, (8, chunk), 0) == 0
    for start in range(0, 1024, chunk):
        lanes = pl.ds(start, chunk)
        for side, target in enumerate((left_ref, right_ref)):
            row = 2 * block + side
            low = [
                jnp.concatenate(
                    [
                        base_ref[part, start // 128 + k, pl.ds(row, 8, stride=65), :]
                        for k in range(chunk // 128)
                    ],
                    axis=1,
                )
                for part in (0, 1)
            ]
            far = [
                [jnp.broadcast_to(far_ref[e, part, pl.ds(row, 1), lanes], (8, chunk)) for part in (0, 1)]
                for e in (0, 1)
            ]
            near = (low, cmul(*low, *far[0]))
            if side == 0:
                vis = vis_ref[block, :, lanes].astype(F32)
                vr, vi = (jnp.broadcast_to(vis[k : k + 1], (8, chunk)) for k in (0, 1))
                products = [(vr * c, vi * s, vr * s, vi * c) for c, s in near]
                plus = [(a - b, d + e) for a, b, d, e in products]
                minus = [(a + b, e - d) for a, b, d, e in products]
                last = cmul(vr, vi, far[1][0], -far[1][1])
            else:
                plus, minus = near, [(c, -s) for c, s in near]
                last = (far[1][0], -far[1][1])
            minus[0] = tuple(jnp.where(first, x, y) for x, y in zip(last, minus[0]))
            for part in range(2):
                for k, pieces in enumerate((plus, minus)):
                    rows = pl.ds(slot * 64 + part * 32 + k * 16, 16)
                    target[rows, lanes] = jnp.concatenate(
                        [piece[part] for piece in pieces], axis=0
                    ).astype(BF16)


def sides(four, which, vis_ref, base_ref, far_ref, side_refs):
    for b in range(4):
        block_sides(four * 4 + b, b, vis_ref, base_ref, far_ref, *side_refs[which])


def images(vis_ref, w_ref, base_ref, far_ref, side_refs, image_ref):
    def image(four, which):
        left_ref, right_ref = side_refs[which]
        product = dot_t(left_ref[...], right_ref[...])
        for b in range(4):
            block = product[b * 64 : b * 64 + 64, b // 2 * 128 : b // 2 * 128 + 128] * w_ref[b % 2]
            high, low = split(block)
            rows = pl.ds(four * 256 + b * 64, 64)
            image_ref[rows, 0:128], image_ref[rows, 128:256] = high, low

    def pair(gp, _):
        sides(2 * gp + 1, 1, vis_ref, base_ref, far_ref, side_refs)
        image(2 * gp, 0)
        sides(jnp.minimum(2 * gp + 2, 7), 0, vis_ref, base_ref, far_ref, side_refs)
        image(2 * gp + 1, 1)
        return 0

    sides(0, 0, vis_ref, base_ref, far_ref, side_refs)
    lax.fori_loop(0, 4, pair, 0)


def subgrids(image, rows_ref, cols_ref, out_ref):
    lane = lax.broadcasted_iota(jnp.int32, (256, 128), 1)
    lower = lane < 64
    turned = dot(image, cols_ref[pl.ds(0, 256)]) + dot(image[:, :128], cols_ref[pl.ds(256, 128)])
    straight, crossed = [], []
    for k in range(2):
        even, odd = turned[k * 512 : k * 512 + 256], turned[k * 512 + 256 : k * 512 + 512]
        straight.append(jnp.where(lower, even, pltpu.roll(odd, 64, 1)))
        crossed.append(jnp.where(lower, pltpu.roll(even, 64, 1), odd))
    total = 0.0
    for part, pieces in enumerate((straight, crossed)):
        high, low = split(jnp.concatenate(pieces, axis=1))
        rows_high, rows_low = joined(rows_ref, 0, part), joined(rows_ref, 1, part)
        total += dot(rows_high, high) + dot(rows_high, low) + dot(rows_low, high)
    pieces = [
        total[b * 32 : b * 32 + 32, k * 128 : k * 128 + 128] for k in range(2) for b in range(4)
    ]
    group = lane[:32] // 8 % 8
    for bit in (1, 2, 4):
        clear = group & bit == 0
        for t in range(8):
            if t & bit == 0:
                x, y = pieces[t], pieces[t | bit]
                pieces[t] = jnp.where(clear, x, pltpu.roll(y, bit * 8, 1))
                pieces[t | bit] = jnp.where(clear, pltpu.roll(x, 128 - bit * 8, 1), y)
    for h in range(4):
        for l in range(4):
            both = [pieces[h * 2 + y][l * 8 : l * 8 + 8] for y in range(2)]
            out_ref[h * 4 + l] = jnp.concatenate(both, axis=0).astype(BF16)


def column_transform(grid, wide_ref, twist_ref, last_ref):
    high, low = split(grid)
    wide_high, wide_low = joined(wide_ref, 0), joined(wide_ref, 1)
    wide = dot(high, wide_high) + dot(low, wide_high) + dot(high, wide_low)
    real = wide[:SUB, :TILES] - wide[SUB:, TILES:]
    imag = wide[SUB:, :TILES] + wide[:SUB, TILES:]
    real, imag = cmul(real, imag, twist_ref[0], twist_ref[1])
    high, low = split(jnp.concatenate([real, imag], axis=0))
    return dot(last_ref[0], high) + dot(last_ref[0], low) + dot(last_ref[1], high)


def kernel(
    vis_hbm,
    off_hbm,
    freq_hbm,
    taper_hbm,
    owner_hbm,
    tile_hbm,
    rows_hbm,
    cols_hbm,
    wide_hbm,
    twist_hbm,
    last_hbm,
    out_ref,
    vis_ref,
    off_ref,
    freq_ref,
    taper_ref,
    owner_ref,
    tile_ref,
    rows_ref,
    cols_ref,
    wide_ref,
    twist_ref,
    last_ref,
    w_ref,
    base_ref,
    far_ref,
    left_a_ref,
    right_a_ref,
    left_b_ref,
    right_b_ref,
    image_ref,
    place_ref,
    zplace_ref,
    yplace_send_ref,
    yplace_ref,
    zsend_ref,
    zgot_ref,
    turn_ref,
    ysend_ref,
    ygot_ref,
    onehot_ref,
    masked_ref,
    xsend_ref,
    xgot_ref,
    lsend_ref,
    lgot_ref,
    local_sem,
    zplace_send,
    zplace_recv,
    yplace_send,
    yplace_recv,
    z_send,
    z_recv,
    y_send,
    y_recv,
    x_send,
    x_recv,
    l_send,
    l_recv,
):
    loads = [
        pltpu.make_async_copy(source, target, local_sem.at[k])
        for k, (source, target) in enumerate(
            (
                (off_hbm, off_ref),
                (freq_hbm, freq_ref),
                (taper_hbm, taper_ref),
                (owner_hbm, owner_ref),
                (tile_hbm, tile_ref),
                (vis_hbm, vis_ref),
                (rows_hbm, rows_ref),
                (cols_hbm, cols_ref),
                (twist_hbm, twist_ref),
                (last_hbm, last_ref),
                (wide_hbm, wide_ref),
            )
        )
    ]
    for load in loads:
        load.start()

    bl, row, col = lax.axis_index("bl"), lax.axis_index("row"), lax.axis_index("col")
    high_z, low_z = bl // 4, bl % 4
    x, y_hi = row // 2, row % 2
    me = y_hi * 8 + col

    def along_z(slot):
        return (slot, row, col)

    def along_y(slot):
        return (bl, x * 2 + slot // 8, slot % 8)

    def along_x(step):
        return (bl, (x + step) % 4 * 2 + y_hi, col)

    def final(step):
        return ((high_z + step % 4) % 4 * 4 + low_z, x * 2 + (y_hi + step // 4) % 2, col)

    barrier = pltpu.get_barrier_semaphore()

    def greet(device):
        pl.semaphore_signal(barrier, inc=1, device_id=device, device_id_type=MESH)

    def others(mine, act):
        def body(k, _):
            act((mine + 8 + k // 2 * (1 - k % 2 * 2)) % 16)
            return 0

        lax.fori_loop(1, 16, body, 0)

    for step in (2, 1, 3):
        greet(final(4 + step))
    others(bl, lambda slot: greet(along_z(slot)))
    others(me, lambda slot: greet(along_y(slot)))
    for step in (2, 1, 3):
        greet(along_x(step))

    for load in loads[:5]:
        load.wait()
    phasors(off_ref, freq_ref, base_ref, far_ref)
    weights(taper_ref, w_ref)
    place_ref[...] = places(owner_ref, tile_ref)

    def remote(source, target, send_sem, recv_sem, device):
        return pltpu.make_async_remote_copy(
            src_ref=source,
            dst_ref=target,
            send_sem=send_sem,
            recv_sem=recv_sem,
            device_id=device,
            device_id_type=MESH,
        )

    def zplace_copy(slot):
        return remote(place_ref, zplace_ref.at[bl], zplace_send, zplace_recv, along_z(slot))

    def yplace_copy(slot):
        return remote(yplace_send_ref, yplace_ref.at[me], yplace_send, yplace_recv, along_y(slot))

    def z_copy(half, slot):
        source, target = zsend_ref.at[half, slot], zgot_ref.at[half, bl]
        return remote(source, target, z_send.at[half], z_recv.at[half], along_z(slot))

    def y_copy(half, slot):
        source, target = ysend_ref.at[half, slot], ygot_ref.at[half, me]
        return remote(source, target, y_send.at[half], y_recv.at[half], along_y(slot))

    def wait_all(ref, sem):
        fifteen = ref.at[pl.ds(0, 15)]
        pltpu.make_async_copy(fifteen, fifteen, sem).wait()

    for load in loads[5:8]:
        load.wait()
    side_refs = ((left_a_ref, right_a_ref), (left_b_ref, right_b_ref))
    images(vis_ref, w_ref, base_ref, far_ref, side_refs, image_ref)
    for half in range(2):
        image = image_ref[half * 1024 : half * 1024 + 1024]
        subgrids(image, rows_ref, cols_ref, zsend_ref.at[half])
    pl.semaphore_wait(barrier, 36)
    others(bl, lambda slot: zplace_copy(slot).start())
    zplace_ref[bl] = place_ref[...]
    for half in range(2):
        others(bl, lambda slot: z_copy(half, slot).start())
        zgot_ref[half, bl] = zsend_ref[half, bl]
    wait_all(zplace_ref, zplace_recv)
    yplace_send_ref[...] = zplace_ref[...].reshape(16, 128).astype(BF16)
    others(me, lambda slot: yplace_copy(slot).start())
    yplace_ref[me] = yplace_send_ref[...]

    def turn(half):
        wait_all(zgot_ref.at[half], z_recv.at[half])
        for slot in range(16):
            turn_ref[pl.ds(slot * 17, 16)] = zgot_ref[half, slot].astype(F32)
        for slot in range(16):
            ysend_ref[half, slot] = turn_ref[pl.ds(slot, 16, stride=17)].astype(BF16)
        others(me, lambda slot: y_copy(half, slot).start())
        ygot_ref[half, me] = ysend_ref[half, me]

    turn(0)
    turn(1)

    wait_all(yplace_ref, yplace_recv)
    place = yplace_ref[...].reshape(256, 128).astype(F32).T.astype(jnp.int32)
    owner, tile = place[:SUB], place[SUB : 2 * SUB]
    pencil, down = owner // 8, tile // 64
    wanted = (pencil // 2 - x + 4) % 4 * 8 + (down - high_z + 4) % 4 * 2 + pencil % 2
    wanted = wanted.astype(F32).astype(BF16)
    column = owner % 8 * 64 + tile % 64
    columns = [
        jnp.where(column // 256 == k, column - k * 256, -1).astype(F32).astype(BF16)
        for k in range(2)
    ]
    tiles = lax.broadcasted_iota(jnp.int32, (256, 256), 0).astype(F32).astype(BF16)
    one, zero = jnp.ones((256, 256), BF16), jnp.zeros((256, 256), BF16)
    for n in range(SUB):
        for k in range(2):
            onehot_ref[n // 16, pl.ds(k * 256, 256), pl.ds(n % 16 * 256, 256)] = jnp.where(
                tiles == columns[k][n : n + 1], one, zero
            )

    step_down = (lax.broadcasted_iota(jnp.int32, (16, 256), 0) // 8).astype(F32).astype(BF16)
    placed = 0.0
    for half in range(2):
        wait_all(ygot_ref.at[half], y_recv.at[half])
        data = ygot_ref[half].reshape(256, 128).astype(F32).T
        for j in range(16):
            values = data[j * 8 : j * 8 + 8]
            values = jnp.concatenate([values, values], axis=0).astype(BF16)
            row_of = wanted[half * 16 + j : half * 16 + j + 1]
            row_of = jnp.broadcast_to(row_of, (16, 256)) - step_down
            for k in range(16):
                masked_ref[half, pl.ds(k * 16, 16), pl.ds(j * 256, 256)] = jnp.where(
                    row_of == jnp.full((16, 256), 2.0 * k, BF16), values, zero[:16]
                )
        placed += dot_t(masked_ref[half], onehot_ref[half])

    def x_copy(turns, step):
        return remote(
            xsend_ref.at[turns, step - 1],
            xgot_ref.at[turns, step - 1],
            x_send.at[turns, step - 1],
            x_recv.at[turns, step - 1],
            along_x(step),
        )

    mine = high_z * 2 + y_hi

    def l_copy(step):
        source = lsend_ref.at[step % 4, (y_hi + step // 4) % 2]
        return remote(source, lgot_ref.at[mine], l_send, l_recv, final(step))

    for turns in (2, 1, 3, 0):
        for step in (2, 1, 3):
            rows = slice(step * 64 + turns * 16, step * 64 + turns * 16 + 16)
            xsend_ref[turns, step - 1] = placed[rows].astype(BF16)
            x_copy(turns, step).start()
    for turns in (2, 1, 3, 0):
        total = placed[turns * 16 : turns * 16 + 16]
        for step in (1, 3, 2):
            x_copy(turns, step).wait_recv()
            total += xgot_ref[turns, step - 1].astype(F32)
        for y in range(2):
            piece = total[y * 8 : y * 8 + 8]
            lsend_ref[turns, y] = jnp.concatenate([piece[:, :256], piece[:, 256:]], axis=0).astype(
                BF16
            )
        for step in (turns + 4, turns):
            if step > 0:
                l_copy(step).start()
    lgot_ref[mine] = lsend_ref[0, y_hi]

    wait_all(zplace_ref, zplace_send)
    wait_all(yplace_ref, yplace_send)
    for half in range(2):
        wait_all(zsend_ref.at[half], z_send.at[half])
        wait_all(ysend_ref.at[half], y_send.at[half])
    for turns in range(4):
        for step in range(1, 4):
            x_copy(turns, step).wait_send()
    for load in loads[8:]:
        load.wait()

    seven = lgot_ref.at[pl.ds(0, 7)]
    pltpu.make_async_copy(seven, seven, l_recv).wait()
    upper = lax.broadcasted_iota(jnp.int32, (8, TILES), 0) < 4
    real, imag = [], []
    for h in range(4):
        even, odd = (
            jnp.concatenate([piece[:8], piece[8:]], axis=1)
            for piece in (lgot_ref[2 * h].astype(F32), lgot_ref[2 * h + 1].astype(F32))
        )
        real.append(jnp.where(upper, even, pltpu.roll(odd, 4, 0)))
        imag.append(jnp.where(upper, pltpu.roll(even, 4, 0), odd))
    grid = jnp.concatenate(real + imag, axis=0)
    result = column_transform(grid, wide_ref, twist_ref, last_ref)
    for part in range(2):
        for k in range(4):
            out_ref[pl.ds(k * 2 + part, SUB, stride=8), :] = result[
                part * 32 : part * 32 + 32, k * 128 : k * 128 + 128
            ]
    pltpu.make_async_copy(seven, seven, l_send).wait()


def on_device(visibilities, offsets, frequencies, taper_curve, owner_index, tile_index):
    rows, cols, wide, twist, last = (jnp.asarray(table) for table in make_tables())
    operands = (
        visibilities,
        offsets.reshape(64, 64),
        frequencies.reshape(1, 16),
        taper_curve.reshape(1, SUB),
        owner_index.reshape(1, 32),
        tile_index.reshape(1, 32),
        rows,
        cols,
        wide,
        twist,
        last,
    )
    result = pl.pallas_call(
        kernel,
        out_shape=jax.ShapeDtypeStruct((256, 128), F32),
        in_specs=[pl.BlockSpec(memory_space=pl.ANY)] * len(operands),
        out_specs=pl.BlockSpec(memory_space=pltpu.VMEM),
        scratch_shapes=[pltpu.VMEM(operand.shape, operand.dtype) for operand in operands]
        + [
            pltpu.VMEM((2, 64, 128), F32),
            pltpu.VMEM((2, 8, 520, 128), F32),
            pltpu.VMEM((2, 2, 64, 1024), F32),
            pltpu.VMEM((256, 1024), BF16),
            pltpu.VMEM((256, 1024), BF16),
            pltpu.VMEM((256, 1024), BF16),
            pltpu.VMEM((256, 1024), BF16),
            pltpu.VMEM((2048, 256), BF16),
            pltpu.VMEM((1, 128), F32),
            pltpu.VMEM((16, 1, 128), F32),
            pltpu.VMEM((16, 128), BF16),
            pltpu.VMEM((16, 16, 128), BF16),
            pltpu.VMEM((2, 16, 16, 128), BF16),
            pltpu.VMEM((2, 16, 16, 128), BF16),
            pltpu.VMEM((16 * 17, 128), F32),
            pltpu.VMEM((2, 16, 16, 128), BF16),
            pltpu.VMEM((2, 16, 16, 128), BF16),
            pltpu.VMEM((2, TILES, 4096), BF16),
            pltpu.VMEM((2, 256, 4096), BF16),
            pltpu.VMEM((4, 3, 16, TILES), BF16),
            pltpu.VMEM((4, 3, 16, TILES), BF16),
            pltpu.VMEM((4, 2, 16, 256), BF16),
            pltpu.VMEM((8, 16, 256), BF16),
            pltpu.SemaphoreType.DMA((len(operands),)),
        ]
        + [pltpu.SemaphoreType.DMA] * 4
        + [pltpu.SemaphoreType.DMA((2,))] * 4
        + [pltpu.SemaphoreType.DMA((4, 3))] * 2
        + [pltpu.SemaphoreType.DMA] * 2,
        compiler_params=pltpu.CompilerParams(
            collective_id=0, has_side_effects=True, vmem_limit_bytes=60 * 1024 * 1024
        ),
    )(*operands)
    return result.reshape(128, 2, 128).transpose(1, 0, 2).reshape(1, 1, 2, GC)


def solution(mesh):
    in_specs = (
        P(("bl", "row", "col"), None, None),
        P(("bl", "row", "col"), None, None),
        P(),
        P(),
        P(("bl", "row", "col"), None),
        P(("bl", "row", "col")),
    )
    out_specs = P("row", ("bl", "col"), None, None)
    return jax.shard_map(
        on_device, mesh=mesh, in_specs=in_specs, out_specs=out_specs, check_vma=False
    )
```

```python
import math

import jax
import jax.numpy as jnp
import numpy as np
from jax import lax
from jax.experimental import pallas as pl
from jax.experimental.pallas import tpu as pltpu
from jax.sharding import PartitionSpec as P

MESH = pl.DeviceIdType.MESH
SUB = 32
GC = 16384
TILES = GC // SUB
F32 = jnp.float32
BF16 = jnp.bfloat16


def split_np(table):
    high = table.astype(BF16)
    low = (table - high.astype(np.float64)).astype(BF16)
    return np.stack([high, low])


def by_lanes(table):
    rows, lanes = table.shape[-2:]
    pieces = table.reshape(table.shape[:-1] + (lanes // 128, 128))
    return np.ascontiguousarray(np.moveaxis(pieces, -2, -3))


def joined(ref, *index):
    return jnp.concatenate([ref[(*index, k)] for k in range(ref.shape[-3])], axis=1)


def make_tables():
    index = np.arange(SUB)
    angle = 2.0 * np.pi * (index[:, None] * index[None, :] % SUB) / SUB
    cos, sin = np.cos(angle), np.sin(angle)
    order = pixel_order()
    cos_in, sin_in = cos[:, order], sin[:, order]
    rows = np.zeros((2, 4, SUB, 4, 2, SUB))
    for b in range(4):
        rows[0, b, :, b, 0], rows[0, b, :, b, 1] = cos_in, sin_in
        rows[1, b, :, b, 0], rows[1, b, :, b, 1] = sin_in, -cos_in
    rows = split_np(rows.reshape(2, 128, 256))
    cos_in, sin_in = cos[order], sin[order]
    straight = np.stack([[cos_in, -sin_in], [sin_in, cos_in]])
    crossed = np.stack([[-sin_in, -cos_in], [cos_in, -sin_in]])
    cols = np.stack([straight, crossed], axis=1)
    cols = cols.reshape(2, 2, 2, SUB, 8, 4).transpose(0, 3, 1, 4, 2, 5).reshape(64, 128)
    cols = split_np(np.tile(cols, (2, 1)))
    cols = np.concatenate([cols[0], cols[0], cols[1]])
    wide = np.arange(TILES)
    wide_angle = 2.0 * np.pi * (wide[:, None] * wide[None, :] % TILES) / TILES
    wide_table = np.concatenate([np.cos(wide_angle), np.sin(wide_angle)], axis=1)
    twist_angle = 2.0 * np.pi * (index[:, None] * wide[None, :]) / GC
    twist = (np.stack([np.cos(twist_angle), np.sin(twist_angle)]) / 128.0).astype(np.float32)
    last = np.block([[cos, -sin], [sin, cos]])
    return (
        by_lanes(rows),
        cols,
        by_lanes(split_np(wide_table)),
        twist,
        split_np(last),
    )


def dot(a, b):
    return lax.dot_general(a, b, (((1,), (0,)), ((), ())), preferred_element_type=F32)


def dot_t(a, b):
    return lax.dot_general(a, b, (((1,), (1,)), ((), ())), preferred_element_type=F32)


def split(x):
    high = x.astype(BF16)
    return high, (x - high.astype(F32)).astype(BF16)


def cmul(ar, ai, br, bi):
    return ar * br - ai * bi, ar * bi + ai * br


def three(x, rows):
    high = x.astype(BF16).astype(F32)
    middle = (x - high).astype(BF16).astype(F32)
    low = x - high - middle
    place = lax.broadcasted_iota(jnp.int32, (rows, x.shape[1]), 0)
    parts = jnp.where(place == 0, high, jnp.where(place == 1, middle, jnp.where(place == 2, low, 0.0)))
    return parts.astype(BF16)


def matches(shape, left, right):
    row, lane = lax.broadcasted_iota(jnp.int32, shape, 0), lax.broadcasted_iota(jnp.int32, shape, 1)
    return (left(row) == right(lane)).astype(F32).astype(BF16)


def pixel(k):
    slot = k % SUB
    return 16 + jnp.where(slot < 16, slot, jnp.where(slot == 16, -16, 16 - slot))


def weights(taper_ref, w_ref):
    parts = three(taper_ref[...], 16)
    along = dot(parts, matches((SUB, 128), lambda i: i, pixel))
    down = dot_t(matches((64, SUB), pixel, lambda k: k), parts)
    along, down = jnp.sum(along, axis=0, keepdims=True), jnp.sum(down, axis=1, keepdims=True)
    lane = lax.broadcasted_iota(jnp.int32, (64, 128), 1) // 64
    for half in range(2):
        w_ref[half] = jnp.where(lane == half, down * along * (1.0 / 1024.0), 0.0)


def place_order(lane):
    slot = lane % SUB
    return slot // 16 * 16 + slot // 4 % 2 * 8 + slot // 8 % 2 * 4 + slot % 4


def places(owner_ref, tile_ref):
    row = lax.broadcasted_iota(jnp.int32, (16, SUB), 0)
    parts = jnp.where(row == 0, owner_ref[...], jnp.where(row == 1, tile_ref[...], 0))
    order = matches((SUB, 128), lambda i: i, place_order)
    both = dot(parts.astype(F32).astype(BF16), order)
    lane = lax.broadcasted_iota(jnp.int32, (1, 128), 1)
    return jnp.where(lane < SUB, both[0:1], both[1:2])


def phasors(off_ref, freq_ref, base_ref, far_ref):
    spread = matches((64, 1024), lambda i: i, lambda k: k // 16)
    repeat = matches((16, 1024), lambda i: i, lambda k: k % 16)
    freq = jnp.sum(dot(three(freq_ref[...], 16), repeat), axis=0, keepdims=True)
    scaled = dot(off_ref[...], spread) * freq
    theta = scaled * (2.0 * math.pi / SUB)
    square = theta * theta
    cos = jnp.full_like(square, -1.0 / math.factorial(14))
    sin = jnp.full_like(square, -1.0 / math.factorial(15))
    for order in range(6, -1, -1):
        sign = 1.0 if order % 2 == 0 else -1.0
        cos = cos * square + sign / math.factorial(2 * order)
        sin = sin * square + sign / math.factorial(2 * order + 1)
    z = [(jnp.ones_like(cos), jnp.zeros_like(cos)), (cos, sin * theta)]
    for p in range(2, 8):
        z.append(cmul(*z[p // 2], *z[p - p // 2]))
    for p in range(8):
        for part in range(2):
            for k in range(8):
                base_ref[part, k, pl.ds(p * 65, 64)] = z[p][part][:, k * 128 : k * 128 + 128]
    z8 = cmul(*z[4], *z[4])
    for e, value in enumerate((z8, cmul(*z8, *z8))):
        for part in range(2):
            far_ref[e, part] = value[part]


def pixel_order():
    slot = np.arange(SUB)
    return 16 + np.where(slot < 16, slot, np.where(slot == 16, -16, 16 - slot))


def block_sides(block, slot, vis_ref, base_ref, far_ref, left_ref, right_ref):
    chunk = 256
    first = lax.broadcasted_iota(jnp.int32, (8, chunk), 0) == 0
    for start in range(0, 1024, chunk):
        lanes = pl.ds(start, chunk)
        for side, target in enumerate((left_ref, right_ref)):
            row = 2 * block + side
            low = [
                jnp.concatenate(
                    [
                        base_ref[part, start // 128 + k, pl.ds(row, 8, stride=65), :]
                        for k in range(chunk // 128)
                    ],
                    axis=1,
                )
                for part in (0, 1)
            ]
            far = [
                [jnp.broadcast_to(far_ref[e, part, pl.ds(row, 1), lanes], (8, chunk)) for part in (0, 1)]
                for e in (0, 1)
            ]
            near = (low, cmul(*low, *far[0]))
            if side == 0:
                vis = vis_ref[block, :, lanes].astype(F32)
                vr, vi = (jnp.broadcast_to(vis[k : k + 1], (8, chunk)) for k in (0, 1))
                products = [(vr * c, vi * s, vr * s, vi * c) for c, s in near]
                plus = [(a - b, d + e) for a, b, d, e in products]
                minus = [(a + b, e - d) for a, b, d, e in products]
                last = cmul(vr, vi, far[1][0], -far[1][1])
            else:
                plus, minus = near, [(c, -s) for c, s in near]
                last = (far[1][0], -far[1][1])
            minus[0] = tuple(jnp.where(first, x, y) for x, y in zip(last, minus[0]))
            for part in range(2):
                for k, pieces in enumerate((plus, minus)):
                    rows = pl.ds(slot * 64 + part * 32 + k * 16, 16)
                    target[rows, lanes] = jnp.concatenate(
                        [piece[part] for piece in pieces], axis=0
                    ).astype(BF16)


def sides(four, which, vis_ref, base_ref, far_ref, side_refs):
    for b in range(4):
        block_sides(four * 4 + b, b, vis_ref, base_ref, far_ref, *side_refs[which])


def images(vis_ref, w_ref, base_ref, far_ref, side_refs, image_ref):
    def image(four, which):
        left_ref, right_ref = side_refs[which]
        product = dot_t(left_ref[...], right_ref[...])
        for b in range(4):
            block = product[b * 64 : b * 64 + 64, b // 2 * 128 : b // 2 * 128 + 128] * w_ref[b % 2]
            high, low = split(block)
            rows = pl.ds(four * 256 + b * 64, 64)
            image_ref[rows, 0:128], image_ref[rows, 128:256] = high, low

    def pair(gp, _):
        sides(2 * gp + 1, 1, vis_ref, base_ref, far_ref, side_refs)
        image(2 * gp, 0)
        sides(jnp.minimum(2 * gp + 2, 7), 0, vis_ref, base_ref, far_ref, side_refs)
        image(2 * gp + 1, 1)
        return 0

    sides(0, 0, vis_ref, base_ref, far_ref, side_refs)
    lax.fori_loop(0, 4, pair, 0)


def subgrids(image, rows_ref, cols_ref, out_ref):
    lane = lax.broadcasted_iota(jnp.int32, (256, 128), 1)
    lower = lane < 64
    turned = dot(image, cols_ref[pl.ds(0, 256)]) + dot(image[:, :128], cols_ref[pl.ds(256, 128)])
    straight, crossed = [], []
    for k in range(2):
        even, odd = turned[k * 512 : k * 512 + 256], turned[k * 512 + 256 : k * 512 + 512]
        straight.append(jnp.where(lower, even, pltpu.roll(odd, 64, 1)))
        crossed.append(jnp.where(lower, pltpu.roll(even, 64, 1), odd))
    total = 0.0
    for part, pieces in enumerate((straight, crossed)):
        high, low = split(jnp.concatenate(pieces, axis=1))
        rows_high, rows_low = joined(rows_ref, 0, part), joined(rows_ref, 1, part)
        total += dot(rows_high, high) + dot(rows_high, low) + dot(rows_low, high)
    pieces = [
        total[b * 32 : b * 32 + 32, k * 128 : k * 128 + 128] for k in range(2) for b in range(4)
    ]
    group = lane[:32] // 8 % 8
    for bit in (1, 2, 4):
        clear = group & bit == 0
        for t in range(8):
            if t & bit == 0:
                x, y = pieces[t], pieces[t | bit]
                pieces[t] = jnp.where(clear, x, pltpu.roll(y, bit * 8, 1))
                pieces[t | bit] = jnp.where(clear, pltpu.roll(x, 128 - bit * 8, 1), y)
    for h in range(4):
        for l in range(4):
            both = [pieces[h * 2 + y][l * 8 : l * 8 + 8] for y in range(2)]
            out_ref[h * 4 + l] = jnp.concatenate(both, axis=0).astype(BF16)


def column_transform(grid, wide_ref, twist_ref, last_ref):
    wide = dot(grid, joined(wide_ref, 0)) + dot(grid, joined(wide_ref, 1))
    real = wide[:SUB, :TILES] - wide[SUB:, TILES:]
    imag = wide[SUB:, :TILES] + wide[:SUB, TILES:]
    real, imag = cmul(real, imag, twist_ref[0], twist_ref[1])
    high, low = split(jnp.concatenate([real, imag], axis=0))
    return dot(last_ref[0], high) + dot(last_ref[0], low) + dot(last_ref[1], high)


def kernel(
    vis_hbm,
    off_hbm,
    freq_hbm,
    taper_hbm,
    owner_hbm,
    tile_hbm,
    rows_hbm,
    cols_hbm,
    wide_hbm,
    twist_hbm,
    last_hbm,
    out_ref,
    vis_ref,
    off_ref,
    freq_ref,
    taper_ref,
    owner_ref,
    tile_ref,
    rows_ref,
    cols_ref,
    wide_ref,
    twist_ref,
    last_ref,
    w_ref,
    base_ref,
    far_ref,
    left_a_ref,
    right_a_ref,
    left_b_ref,
    right_b_ref,
    image_ref,
    place_ref,
    zplace_ref,
    yplace_send_ref,
    yplace_ref,
    zsend_ref,
    zgot_ref,
    turn_ref,
    ysend_ref,
    ygot_ref,
    onehot_ref,
    masked_ref,
    xsend_ref,
    xgot_ref,
    lsend_ref,
    lgot_ref,
    local_sem,
    zplace_send,
    zplace_recv,
    yplace_send,
    yplace_recv,
    z_send,
    z_recv,
    y_send,
    y_recv,
    x_send,
    x_recv,
    l_send,
    l_recv,
):
    loads = [
        pltpu.make_async_copy(source, target, local_sem.at[k])
        for k, (source, target) in enumerate(
            (
                (off_hbm, off_ref),
                (freq_hbm, freq_ref),
                (taper_hbm, taper_ref),
                (owner_hbm, owner_ref),
                (tile_hbm, tile_ref),
                (vis_hbm, vis_ref),
                (rows_hbm, rows_ref),
                (cols_hbm, cols_ref),
                (twist_hbm, twist_ref),
                (last_hbm, last_ref),
                (wide_hbm, wide_ref),
            )
        )
    ]
    for load in loads:
        load.start()

    bl, row, col = lax.axis_index("bl"), lax.axis_index("row"), lax.axis_index("col")
    high_z, low_z = bl // 4, bl % 4
    x, y_hi = row // 2, row % 2
    me = y_hi * 8 + col

    def along_z(slot):
        return (slot, row, col)

    def along_y(slot):
        return (bl, x * 2 + slot // 8, slot % 8)

    def along_x(step):
        return (bl, (x + step) % 4 * 2 + y_hi, col)

    def final(step):
        return ((high_z + step % 4) % 4 * 4 + low_z, x * 2 + (y_hi + step // 4) % 2, col)

    barrier = pltpu.get_barrier_semaphore()

    def greet(device):
        pl.semaphore_signal(barrier, inc=1, device_id=device, device_id_type=MESH)

    def others(mine, act):
        def body(k, _):
            act((mine + 8 + k // 2 * (1 - k % 2 * 2)) % 16)
            return 0

        lax.fori_loop(1, 16, body, 0)

    others(bl, lambda slot: greet(along_z(slot)))
    others(me, lambda slot: greet(along_y(slot)))
    for step in (2, 1, 3):
        greet(along_x(step))

    for load in loads[:5]:
        load.wait()
    phasors(off_ref, freq_ref, base_ref, far_ref)
    weights(taper_ref, w_ref)
    place_ref[...] = places(owner_ref, tile_ref)

    def remote(source, target, send_sem, recv_sem, device):
        return pltpu.make_async_remote_copy(
            src_ref=source,
            dst_ref=target,
            send_sem=send_sem,
            recv_sem=recv_sem,
            device_id=device,
            device_id_type=MESH,
        )

    def zplace_copy(slot):
        return remote(place_ref, zplace_ref.at[bl], zplace_send, zplace_recv, along_z(slot))

    def yplace_copy(slot):
        return remote(yplace_send_ref, yplace_ref.at[me], yplace_send, yplace_recv, along_y(slot))

    def z_copy(half, slot):
        source, target = zsend_ref.at[half, slot], zgot_ref.at[half, bl]
        return remote(source, target, z_send.at[half], z_recv.at[half], along_z(slot))

    def y_copy(half, slot):
        source, target = ysend_ref.at[half, slot], ygot_ref.at[half, me]
        return remote(source, target, y_send.at[half], y_recv.at[half], along_y(slot))

    def wait_all(ref, sem):
        fifteen = ref.at[pl.ds(0, 15)]
        pltpu.make_async_copy(fifteen, fifteen, sem).wait()

    for load in loads[5:8]:
        load.wait()
    side_refs = ((left_a_ref, right_a_ref), (left_b_ref, right_b_ref))
    images(vis_ref, w_ref, base_ref, far_ref, side_refs, image_ref)
    for half in range(2):
        image = image_ref[half * 1024 : half * 1024 + 1024]
        subgrids(image, rows_ref, cols_ref, zsend_ref.at[half])
    pl.semaphore_wait(barrier, 33)
    others(bl, lambda slot: zplace_copy(slot).start())
    zplace_ref[bl] = place_ref[...]
    for half in range(2):
        others(bl, lambda slot: z_copy(half, slot).start())
        zgot_ref[half, bl] = zsend_ref[half, bl]
    wait_all(zplace_ref, zplace_recv)
    yplace_send_ref[...] = zplace_ref[...].reshape(16, 128).astype(BF16)
    others(me, lambda slot: yplace_copy(slot).start())
    yplace_ref[me] = yplace_send_ref[...]

    def turn(half):
        wait_all(zgot_ref.at[half], z_recv.at[half])
        for slot in range(16):
            turn_ref[pl.ds(slot * 17, 16)] = zgot_ref[half, slot].astype(F32)
        for slot in range(16):
            ysend_ref[half, slot] = turn_ref[pl.ds(slot, 16, stride=17)].astype(BF16)
        others(me, lambda slot: y_copy(half, slot).start())
        ygot_ref[half, me] = ysend_ref[half, me]

    turn(0)
    turn(1)

    wait_all(yplace_ref, yplace_recv)
    place = yplace_ref[...].reshape(256, 128).astype(F32).T.astype(jnp.int32)
    owner, tile = place[:SUB], place[SUB : 2 * SUB]
    pencil, down = owner // 8, tile // 64
    wanted = (pencil // 2 - x + 4) % 4 * 8 + (down - high_z + 4) % 4 * 2 + pencil % 2
    wanted = wanted.astype(F32).astype(BF16)
    column = owner % 8 * 64 + tile % 64
    columns = [
        jnp.where(column // 256 == k, column - k * 256, -1).astype(F32).astype(BF16)
        for k in range(2)
    ]
    tiles = lax.broadcasted_iota(jnp.int32, (256, 256), 0).astype(F32).astype(BF16)
    one, zero = jnp.ones((256, 256), BF16), jnp.zeros((256, 256), BF16)
    for n in range(SUB):
        for k in range(2):
            onehot_ref[n // 16, pl.ds(k * 256, 256), pl.ds(n % 16 * 256, 256)] = jnp.where(
                tiles == columns[k][n : n + 1], one, zero
            )

    step_down = (lax.broadcasted_iota(jnp.int32, (16, 256), 0) // 8).astype(F32).astype(BF16)
    placed = 0.0
    for half in range(2):
        wait_all(ygot_ref.at[half], y_recv.at[half])
        data = ygot_ref[half].reshape(256, 128).astype(F32).T
        for j in range(16):
            values = data[j * 8 : j * 8 + 8]
            values = jnp.concatenate([values, values], axis=0).astype(BF16)
            row_of = wanted[half * 16 + j : half * 16 + j + 1]
            row_of = jnp.broadcast_to(row_of, (16, 256)) - step_down
            for k in range(16):
                masked_ref[half, pl.ds(k * 16, 16), pl.ds(j * 256, 256)] = jnp.where(
                    row_of == jnp.full((16, 256), 2.0 * k, BF16), values, zero[:16]
                )
        placed += dot_t(masked_ref[half], onehot_ref[half])

    def x_copy(turns, step):
        return remote(
            xsend_ref.at[turns, step - 1],
            xgot_ref.at[turns, step - 1],
            x_send.at[turns, step - 1],
            x_recv.at[turns, step - 1],
            along_x(step),
        )

    mine = high_z * 2 + y_hi

    def l_copy(step):
        source = lsend_ref.at[step % 4, (y_hi + step // 4) % 2]
        return remote(source, lgot_ref.at[mine], l_send, l_recv, final(step))

    for turns in (2, 1, 3, 0):
        for step in (2, 1, 3):
            rows = slice(step * 64 + turns * 16, step * 64 + turns * 16 + 16)
            xsend_ref[turns, step - 1] = placed[rows].astype(BF16)
            x_copy(turns, step).start()
    for turns in (2, 1, 3, 0):
        total = placed[turns * 16 : turns * 16 + 16]
        for step in (1, 3, 2):
            x_copy(turns, step).wait_recv()
            total += xgot_ref[turns, step - 1].astype(F32)
        for y in range(2):
            piece = total[y * 8 : y * 8 + 8]
            lsend_ref[turns, y] = jnp.concatenate([piece[:, :256], piece[:, 256:]], axis=0).astype(
                BF16
            )
        for step in (turns + 4, turns):
            if step > 0:
                l_copy(step).start()
    lgot_ref[mine] = lsend_ref[0, y_hi]

    wait_all(zplace_ref, zplace_send)
    wait_all(yplace_ref, yplace_send)
    for half in range(2):
        wait_all(zsend_ref.at[half], z_send.at[half])
        wait_all(ysend_ref.at[half], y_send.at[half])
    for turns in range(4):
        for step in range(1, 4):
            x_copy(turns, step).wait_send()
    for load in loads[8:]:
        load.wait()

    seven = lgot_ref.at[pl.ds(0, 7)]
    pltpu.make_async_copy(seven, seven, l_recv).wait()
    upper = lax.broadcasted_iota(jnp.int32, (8, TILES), 0) < 4
    real, imag = [], []
    for h in range(4):
        even, odd = (
            jnp.concatenate([piece[:8], piece[8:]], axis=1)
            for piece in (lgot_ref[2 * h].astype(F32), lgot_ref[2 * h + 1].astype(F32))
        )
        real.append(jnp.where(upper, even, pltpu.roll(odd, 4, 0)))
        imag.append(jnp.where(upper, pltpu.roll(even, 4, 0), odd))
    grid = jnp.concatenate(real + imag, axis=0).astype(BF16)
    result = column_transform(grid, wide_ref, twist_ref, last_ref)
    for part in range(2):
        for k in range(4):
            out_ref[pl.ds(k * 2 + part, SUB, stride=8), :] = result[
                part * 32 : part * 32 + 32, k * 128 : k * 128 + 128
            ]
    pltpu.make_async_copy(seven, seven, l_send).wait()


def on_device(visibilities, offsets, frequencies, taper_curve, owner_index, tile_index):
    rows, cols, wide, twist, last = (jnp.asarray(table) for table in make_tables())
    operands = (
        visibilities,
        offsets.reshape(64, 64),
        frequencies.reshape(1, 16),
        taper_curve.reshape(1, SUB),
        owner_index.reshape(1, 32),
        tile_index.reshape(1, 32),
        rows,
        cols,
        wide,
        twist,
        last,
    )
    result = pl.pallas_call(
        kernel,
        out_shape=pltpu.VMEM((256, 128), F32),
        in_specs=[pl.BlockSpec(memory_space=pl.ANY)] * len(operands),
        out_specs=pl.BlockSpec(memory_space=pltpu.VMEM),
        scratch_shapes=[pltpu.VMEM(operand.shape, operand.dtype) for operand in operands]
        + [
            pltpu.VMEM((2, 64, 128), F32),
            pltpu.VMEM((2, 8, 520, 128), F32),
            pltpu.VMEM((2, 2, 64, 1024), F32),
            pltpu.VMEM((256, 1024), BF16),
            pltpu.VMEM((256, 1024), BF16),
            pltpu.VMEM((256, 1024), BF16),
            pltpu.VMEM((256, 1024), BF16),
            pltpu.VMEM((2048, 256), BF16),
            pltpu.VMEM((1, 128), F32),
            pltpu.VMEM((16, 1, 128), F32),
            pltpu.VMEM((16, 128), BF16),
            pltpu.VMEM((16, 16, 128), BF16),
            pltpu.VMEM((2, 16, 16, 128), BF16),
            pltpu.VMEM((2, 16, 16, 128), BF16),
            pltpu.VMEM((16 * 17, 128), F32),
            pltpu.VMEM((2, 16, 16, 128), BF16),
            pltpu.VMEM((2, 16, 16, 128), BF16),
            pltpu.VMEM((2, TILES, 4096), BF16),
            pltpu.VMEM((2, 256, 4096), BF16),
            pltpu.VMEM((4, 3, 16, TILES), BF16),
            pltpu.VMEM((4, 3, 16, TILES), BF16),
            pltpu.VMEM((4, 2, 16, 256), BF16),
            pltpu.VMEM((8, 16, 256), BF16),
            pltpu.SemaphoreType.DMA((len(operands),)),
        ]
        + [pltpu.SemaphoreType.DMA] * 4
        + [pltpu.SemaphoreType.DMA((2,))] * 4
        + [pltpu.SemaphoreType.DMA((4, 3))] * 2
        + [pltpu.SemaphoreType.DMA] * 2,
        compiler_params=pltpu.CompilerParams(
            collective_id=0, has_side_effects=True, vmem_limit_bytes=60 * 1024 * 1024
        ),
    )(*operands)
    return result.reshape(128, 2, 128).transpose(1, 0, 2).reshape(1, 1, 2, GC)


def solution(mesh):
    in_specs = (
        P(("bl", "row", "col"), None, None),
        P(("bl", "row", "col"), None, None),
        P(),
        P(),
        P(("bl", "row", "col"), None),
        P(("bl", "row", "col")),
    )
    out_specs = P("row", ("bl", "col"), None, None)
    return jax.shard_map(
        on_device, mesh=mesh, in_specs=in_specs, out_specs=out_specs, check_vma=False
    )
```

```python
import math

import jax
import jax.numpy as jnp
import numpy as np
from jax import lax
from jax.experimental import pallas as pl
from jax.experimental.pallas import tpu as pltpu
from jax.sharding import PartitionSpec as P

MESH = pl.DeviceIdType.MESH
SUB = 32
GC = 16384
TILES = GC // SUB
F32 = jnp.float32
BF16 = jnp.bfloat16


def split_np(table):
    high = table.astype(BF16)
    low = (table - high.astype(np.float64)).astype(BF16)
    return np.stack([high, low])


def by_lanes(table):
    rows, lanes = table.shape[-2:]
    pieces = table.reshape(table.shape[:-1] + (lanes // 128, 128))
    return np.ascontiguousarray(np.moveaxis(pieces, -2, -3))


def joined(ref, *index):
    return jnp.concatenate([ref[(*index, k)] for k in range(ref.shape[-3])], axis=1)


def make_tables():
    index = np.arange(SUB)
    angle = 2.0 * np.pi * (index[:, None] * index[None, :] % SUB) / SUB
    cos, sin = np.cos(angle), np.sin(angle)
    order = pixel_order()
    cos_in, sin_in = cos[:, order], sin[:, order]
    rows = np.zeros((2, 4, SUB, 4, 2, SUB))
    for b in range(4):
        rows[0, b, :, b, 0], rows[0, b, :, b, 1] = cos_in, sin_in
        rows[1, b, :, b, 0], rows[1, b, :, b, 1] = sin_in, -cos_in
    rows = split_np(rows.reshape(2, 128, 256))
    cos_in, sin_in = cos[order], sin[order]
    straight = np.stack([[cos_in, -sin_in], [sin_in, cos_in]])
    crossed = np.stack([[-sin_in, -cos_in], [cos_in, -sin_in]])
    cols = np.stack([straight, crossed], axis=1)
    cols = cols.reshape(2, 2, 2, SUB, 8, 4).transpose(0, 3, 1, 4, 2, 5).reshape(64, 128)
    cols = split_np(np.tile(cols, (2, 1)))
    cols = np.concatenate([cols[0], cols[0], cols[1]])
    wide = np.arange(TILES)
    wide_angle = 2.0 * np.pi * (wide[:, None] * wide[None, :] % TILES) / TILES
    wide_table = np.concatenate([np.cos(wide_angle), np.sin(wide_angle)], axis=1)
    twist_angle = 2.0 * np.pi * (index[:, None] * wide[None, :]) / GC
    twist = (np.stack([np.cos(twist_angle), np.sin(twist_angle)]) / 128.0).astype(np.float32)
    last = np.block([[cos, -sin], [sin, cos]])
    return (
        by_lanes(rows),
        cols,
        by_lanes(split_np(wide_table)),
        twist,
        split_np(last),
    )


def dot(a, b):
    return lax.dot_general(a, b, (((1,), (0,)), ((), ())), preferred_element_type=F32)


def dot_t(a, b):
    return lax.dot_general(a, b, (((1,), (1,)), ((), ())), preferred_element_type=F32)


def split(x):
    high = x.astype(BF16)
    return high, (x - high.astype(F32)).astype(BF16)


def cmul(ar, ai, br, bi):
    return ar * br - ai * bi, ar * bi + ai * br


def three(x, rows):
    high = x.astype(BF16).astype(F32)
    middle = (x - high).astype(BF16).astype(F32)
    low = x - high - middle
    place = lax.broadcasted_iota(jnp.int32, (rows, x.shape[1]), 0)
    parts = jnp.where(place == 0, high, jnp.where(place == 1, middle, jnp.where(place == 2, low, 0.0)))
    return parts.astype(BF16)


def matches(shape, left, right):
    row, lane = lax.broadcasted_iota(jnp.int32, shape, 0), lax.broadcasted_iota(jnp.int32, shape, 1)
    return (left(row) == right(lane)).astype(F32).astype(BF16)


def pixel(k):
    slot = k % SUB
    return 16 + jnp.where(slot < 16, slot, jnp.where(slot == 16, -16, 16 - slot))


def weights(taper_ref, w_ref):
    parts = three(taper_ref[...], 16)
    along = dot(parts, matches((SUB, 128), lambda i: i, pixel))
    down = dot_t(matches((64, SUB), pixel, lambda k: k), parts)
    along, down = jnp.sum(along, axis=0, keepdims=True), jnp.sum(down, axis=1, keepdims=True)
    lane = lax.broadcasted_iota(jnp.int32, (64, 128), 1) // 64
    for half in range(2):
        w_ref[half] = jnp.where(lane == half, down * along * (1.0 / 1024.0), 0.0)


def place_order(lane):
    slot = lane % SUB
    return slot // 16 * 16 + slot // 4 % 2 * 8 + slot // 8 % 2 * 4 + slot % 4


def places(owner_ref, tile_ref):
    row = lax.broadcasted_iota(jnp.int32, (16, SUB), 0)
    parts = jnp.where(row == 0, owner_ref[...], jnp.where(row == 1, tile_ref[...], 0))
    order = matches((SUB, 128), lambda i: i, place_order)
    both = dot(parts.astype(F32).astype(BF16), order)
    lane = lax.broadcasted_iota(jnp.int32, (1, 128), 1)
    return jnp.where(lane < SUB, both[0:1], both[1:2])


def phasors(off_ref, freq_ref, base_ref, far_ref):
    spread = matches((64, 1024), lambda i: i, lambda k: k // 16)
    repeat = matches((16, 1024), lambda i: i, lambda k: k % 16)
    freq = jnp.sum(dot(three(freq_ref[...], 16), repeat), axis=0, keepdims=True)
    scaled = dot(off_ref[...], spread) * freq
    theta = scaled * (2.0 * math.pi / SUB)
    square = theta * theta
    cos = jnp.full_like(square, -1.0 / math.factorial(14))
    sin = jnp.full_like(square, -1.0 / math.factorial(15))
    for order in range(6, -1, -1):
        sign = 1.0 if order % 2 == 0 else -1.0
        cos = cos * square + sign / math.factorial(2 * order)
        sin = sin * square + sign / math.factorial(2 * order + 1)
    z = [(jnp.ones_like(cos), jnp.zeros_like(cos)), (cos, sin * theta)]
    for p in range(2, 8):
        z.append(cmul(*z[p // 2], *z[p - p // 2]))
    for p in range(8):
        for part in range(2):
            for k in range(8):
                base_ref[part, k, pl.ds(p * 65, 64)] = z[p][part][:, k * 128 : k * 128 + 128]
    z8 = cmul(*z[4], *z[4])
    for e, value in enumerate((z8, cmul(*z8, *z8))):
        for part in range(2):
            far_ref[e, part] = value[part]


def pixel_order():
    slot = np.arange(SUB)
    return 16 + np.where(slot < 16, slot, np.where(slot == 16, -16, 16 - slot))


def block_sides(block, slot, vis_ref, base_ref, far_ref, left_ref, right_ref):
    chunk = 256
    first = lax.broadcasted_iota(jnp.int32, (8, chunk), 0) == 0
    for start in range(0, 1024, chunk):
        lanes = pl.ds(start, chunk)
        for side, target in enumerate((left_ref, right_ref)):
            row = 2 * block + side
            low = [
                jnp.concatenate(
                    [
                        base_ref[part, start // 128 + k, pl.ds(row, 8, stride=65), :]
                        for k in range(chunk // 128)
                    ],
                    axis=1,
                )
                for part in (0, 1)
            ]
            far = [
                [jnp.broadcast_to(far_ref[e, part, pl.ds(row, 1), lanes], (8, chunk)) for part in (0, 1)]
                for e in (0, 1)
            ]
            near = (low, cmul(*low, *far[0]))
            if side == 0:
                vis = vis_ref[block, :, lanes].astype(F32)
                vr, vi = (jnp.broadcast_to(vis[k : k + 1], (8, chunk)) for k in (0, 1))
                products = [(vr * c, vi * s, vr * s, vi * c) for c, s in near]
                plus = [(a - b, d + e) for a, b, d, e in products]
                minus = [(a + b, e - d) for a, b, d, e in products]
                last = cmul(vr, vi, far[1][0], -far[1][1])
            else:
                plus, minus = near, [(c, -s) for c, s in near]
                last = (far[1][0], -far[1][1])
            minus[0] = tuple(jnp.where(first, x, y) for x, y in zip(last, minus[0]))
            for part in range(2):
                for k, pieces in enumerate((plus, minus)):
                    rows = pl.ds(slot * 64 + part * 32 + k * 16, 16)
                    target[rows, lanes] = jnp.concatenate(
                        [piece[part] for piece in pieces], axis=0
                    ).astype(BF16)


def sides(four, which, vis_ref, base_ref, far_ref, side_refs):
    for b in range(4):
        block_sides(four * 4 + b, b, vis_ref, base_ref, far_ref, *side_refs[which])


def images(vis_ref, w_ref, base_ref, far_ref, side_refs, image_ref):
    def image(four, which):
        left_ref, right_ref = side_refs[which]
        product = dot_t(left_ref[...], right_ref[...])
        for b in range(4):
            block = product[b * 64 : b * 64 + 64, b // 2 * 128 : b // 2 * 128 + 128] * w_ref[b % 2]
            high, low = split(block)
            rows = pl.ds(four * 256 + b * 64, 64)
            image_ref[rows, 0:128], image_ref[rows, 128:256] = high, low

    def pair(gp, _):
        sides(2 * gp + 1, 1, vis_ref, base_ref, far_ref, side_refs)
        image(2 * gp, 0)
        sides(jnp.minimum(2 * gp + 2, 7), 0, vis_ref, base_ref, far_ref, side_refs)
        image(2 * gp + 1, 1)
        return 0

    sides(0, 0, vis_ref, base_ref, far_ref, side_refs)
    lax.fori_loop(0, 4, pair, 0)


def subgrids(image, rows_ref, cols_ref, out_ref):
    lane = lax.broadcasted_iota(jnp.int32, (256, 128), 1)
    lower = lane < 64
    turned = dot(image, cols_ref[pl.ds(0, 256)]) + dot(image[:, :128], cols_ref[pl.ds(256, 128)])
    straight, crossed = [], []
    for k in range(2):
        even, odd = turned[k * 512 : k * 512 + 256], turned[k * 512 + 256 : k * 512 + 512]
        straight.append(jnp.where(lower, even, pltpu.roll(odd, 64, 1)))
        crossed.append(jnp.where(lower, pltpu.roll(even, 64, 1), odd))
    total = 0.0
    for part, pieces in enumerate((straight, crossed)):
        high, low = split(jnp.concatenate(pieces, axis=1))
        rows_high, rows_low = joined(rows_ref, 0, part), joined(rows_ref, 1, part)
        total += dot(rows_high, high) + dot(rows_high, low) + dot(rows_low, high)
    pieces = [
        total[b * 32 : b * 32 + 32, k * 128 : k * 128 + 128] for k in range(2) for b in range(4)
    ]
    group = lane[:32] // 8 % 8
    for bit in (1, 2, 4):
        clear = group & bit == 0
        for t in range(8):
            if t & bit == 0:
                x, y = pieces[t], pieces[t | bit]
                pieces[t] = jnp.where(clear, x, pltpu.roll(y, bit * 8, 1))
                pieces[t | bit] = jnp.where(clear, pltpu.roll(x, 128 - bit * 8, 1), y)
    for h in range(4):
        for l in range(4):
            both = [pieces[h * 2 + y][l * 8 : l * 8 + 8] for y in range(2)]
            out_ref[h * 4 + l] = jnp.concatenate(both, axis=0).astype(BF16)


def column_transform(grid, wide_ref, twist_ref, last_ref):
    wide = dot(grid, joined(wide_ref, 0)) + dot(grid, joined(wide_ref, 1))
    real = wide[:SUB, :TILES] - wide[SUB:, TILES:]
    imag = wide[SUB:, :TILES] + wide[:SUB, TILES:]
    real, imag = cmul(real, imag, twist_ref[0], twist_ref[1])
    high, low = split(jnp.concatenate([real, imag], axis=0))
    return dot(last_ref[0], high) + dot(last_ref[0], low) + dot(last_ref[1], high)


def kernel(
    vis_hbm,
    off_hbm,
    freq_hbm,
    taper_hbm,
    owner_hbm,
    tile_hbm,
    rows_hbm,
    cols_hbm,
    wide_hbm,
    twist_hbm,
    last_hbm,
    out_ref,
    vis_ref,
    off_ref,
    freq_ref,
    taper_ref,
    owner_ref,
    tile_ref,
    rows_ref,
    cols_ref,
    wide_ref,
    twist_ref,
    last_ref,
    w_ref,
    base_ref,
    far_ref,
    left_a_ref,
    right_a_ref,
    left_b_ref,
    right_b_ref,
    image_ref,
    place_ref,
    zplace_ref,
    yplace_send_ref,
    yplace_ref,
    zsend_ref,
    zgot_ref,
    turn_ref,
    ysend_ref,
    ygot_ref,
    onehot_ref,
    masked_ref,
    xsend_ref,
    xgot_ref,
    lsend_ref,
    lgot_ref,
    local_sem,
    zplace_send,
    zplace_recv,
    yplace_send,
    yplace_recv,
    z_send,
    z_recv,
    y_send,
    y_recv,
    x_send,
    x_recv,
    l_send,
    l_recv,
):
    loads = [
        pltpu.make_async_copy(source, target, local_sem.at[k])
        for k, (source, target) in enumerate(
            (
                (off_hbm, off_ref),
                (freq_hbm, freq_ref),
                (taper_hbm, taper_ref),
                (owner_hbm, owner_ref),
                (tile_hbm, tile_ref),
                (vis_hbm, vis_ref),
                (rows_hbm, rows_ref),
                (cols_hbm, cols_ref),
                (twist_hbm, twist_ref),
                (last_hbm, last_ref),
                (wide_hbm, wide_ref),
            )
        )
    ]
    for load in loads:
        load.start()

    bl, row, col = lax.axis_index("bl"), lax.axis_index("row"), lax.axis_index("col")
    high_z, low_z = bl // 4, bl % 4
    x, y_hi = row // 2, row % 2
    me = y_hi * 8 + col

    def along_z(slot):
        return (slot, row, col)

    def along_y(slot):
        return (bl, x * 2 + slot // 8, slot % 8)

    def along_x(step):
        return (bl, (x + step) % 4 * 2 + y_hi, col)

    def final(step):
        return ((high_z + step % 4) % 4 * 4 + low_z, x * 2 + (y_hi + step // 4) % 2, col)

    barrier = pltpu.get_barrier_semaphore()

    def greet(device):
        pl.semaphore_signal(barrier, inc=1, device_id=device, device_id_type=MESH)

    def others(mine, act):
        def body(k, _):
            act((mine + 8 + k // 2 * (1 - k % 2 * 2)) % 16)
            return 0

        lax.fori_loop(1, 16, body, 0)

    for step in (2, 1, 3):
        greet(final(4 + step))
    others(bl, lambda slot: greet(along_z(slot)))
    others(me, lambda slot: greet(along_y(slot)))
    for step in (2, 1, 3):
        greet(along_x(step))

    for load in loads[:5]:
        load.wait()
    phasors(off_ref, freq_ref, base_ref, far_ref)
    weights(taper_ref, w_ref)
    place_ref[...] = places(owner_ref, tile_ref)

    def remote(source, target, send_sem, recv_sem, device):
        return pltpu.make_async_remote_copy(
            src_ref=source,
            dst_ref=target,
            send_sem=send_sem,
            recv_sem=recv_sem,
            device_id=device,
            device_id_type=MESH,
        )

    def zplace_copy(slot):
        return remote(place_ref, zplace_ref.at[bl], zplace_send, zplace_recv, along_z(slot))

    def yplace_copy(slot):
        return remote(yplace_send_ref, yplace_ref.at[me], yplace_send, yplace_recv, along_y(slot))

    def z_copy(half, slot):
        source, target = zsend_ref.at[half, slot], zgot_ref.at[half, bl]
        return remote(source, target, z_send.at[half], z_recv.at[half], along_z(slot))

    def y_copy(half, slot):
        source, target = ysend_ref.at[half, slot], ygot_ref.at[half, me]
        return remote(source, target, y_send.at[half], y_recv.at[half], along_y(slot))

    def wait_all(ref, sem):
        fifteen = ref.at[pl.ds(0, 15)]
        pltpu.make_async_copy(fifteen, fifteen, sem).wait()

    for load in loads[5:8]:
        load.wait()
    side_refs = ((left_a_ref, right_a_ref), (left_b_ref, right_b_ref))
    images(vis_ref, w_ref, base_ref, far_ref, side_refs, image_ref)
    for half in range(2):
        image = image_ref[half * 1024 : half * 1024 + 1024]
        subgrids(image, rows_ref, cols_ref, zsend_ref.at[half])
    pl.semaphore_wait(barrier, 36)
    others(bl, lambda slot: zplace_copy(slot).start())
    zplace_ref[bl] = place_ref[...]
    for half in range(2):
        others(bl, lambda slot: z_copy(half, slot).start())
        zgot_ref[half, bl] = zsend_ref[half, bl]
    wait_all(zplace_ref, zplace_recv)
    yplace_send_ref[...] = zplace_ref[...].reshape(16, 128).astype(BF16)
    others(me, lambda slot: yplace_copy(slot).start())
    yplace_ref[me] = yplace_send_ref[...]

    def turn(half):
        wait_all(zgot_ref.at[half], z_recv.at[half])
        for slot in range(16):
            turn_ref[pl.ds(slot * 17, 16)] = zgot_ref[half, slot].astype(F32)
        for slot in range(16):
            ysend_ref[half, slot] = turn_ref[pl.ds(slot, 16, stride=17)].astype(BF16)
        others(me, lambda slot: y_copy(half, slot).start())
        ygot_ref[half, me] = ysend_ref[half, me]

    turn(0)
    turn(1)

    wait_all(yplace_ref, yplace_recv)
    place = yplace_ref[...].reshape(256, 128).astype(F32).T.astype(jnp.int32)
    owner, tile = place[:SUB], place[SUB : 2 * SUB]
    pencil, down = owner // 8, tile // 64
    wanted = (pencil // 2 - x + 4) % 4 * 8 + (down - high_z + 4) % 4 * 2 + pencil % 2
    wanted = wanted.astype(F32).astype(BF16)
    column = owner % 8 * 64 + tile % 64
    columns = [
        jnp.where(column // 256 == k, column - k * 256, -1).astype(F32).astype(BF16)
        for k in range(2)
    ]
    tiles = lax.broadcasted_iota(jnp.int32, (256, 256), 0).astype(F32).astype(BF16)
    one, zero = jnp.ones((256, 256), BF16), jnp.zeros((256, 256), BF16)
    for n in range(SUB):
        for k in range(2):
            onehot_ref[n // 16, pl.ds(k * 256, 256), pl.ds(n % 16 * 256, 256)] = jnp.where(
                tiles == columns[k][n : n + 1], one, zero
            )

    step_down = (lax.broadcasted_iota(jnp.int32, (16, 256), 0) // 8).astype(F32).astype(BF16)
    placed = 0.0
    for half in range(2):
        wait_all(ygot_ref.at[half], y_recv.at[half])
        data = ygot_ref[half].reshape(256, 128).astype(F32).T
        for j in range(16):
            values = data[j * 8 : j * 8 + 8]
            values = jnp.concatenate([values, values], axis=0).astype(BF16)
            row_of = wanted[half * 16 + j : half * 16 + j + 1]
            row_of = jnp.broadcast_to(row_of, (16, 256)) - step_down
            for k in range(16):
                masked_ref[half, pl.ds(k * 16, 16), pl.ds(j * 256, 256)] = jnp.where(
                    row_of == jnp.full((16, 256), 2.0 * k, BF16), values, zero[:16]
                )
        placed += dot_t(masked_ref[half], onehot_ref[half])

    def x_copy(turns, step):
        return remote(
            xsend_ref.at[turns, step - 1],
            xgot_ref.at[turns, step - 1],
            x_send.at[turns, step - 1],
            x_recv.at[turns, step - 1],
            along_x(step),
        )

    mine = high_z * 2 + y_hi

    def l_copy(step):
        source = lsend_ref.at[step % 4, (y_hi + step // 4) % 2]
        return remote(source, lgot_ref.at[mine], l_send, l_recv, final(step))

    for turns in (2, 1, 3, 0):
        for step in (2, 1, 3):
            rows = slice(step * 64 + turns * 16, step * 64 + turns * 16 + 16)
            xsend_ref[turns, step - 1] = placed[rows].astype(BF16)
            x_copy(turns, step).start()
    for turns in (2, 1, 3, 0):
        total = placed[turns * 16 : turns * 16 + 16]
        for step in (1, 3, 2):
            x_copy(turns, step).wait_recv()
            total += xgot_ref[turns, step - 1].astype(F32)
        for y in range(2):
            piece = total[y * 8 : y * 8 + 8]
            lsend_ref[turns, y] = jnp.concatenate([piece[:, :256], piece[:, 256:]], axis=0).astype(
                BF16
            )
        for step in (turns + 4, turns):
            if step > 0:
                l_copy(step).start()
    lgot_ref[mine] = lsend_ref[0, y_hi]

    wait_all(zplace_ref, zplace_send)
    wait_all(yplace_ref, yplace_send)
    for half in range(2):
        wait_all(zsend_ref.at[half], z_send.at[half])
        wait_all(ysend_ref.at[half], y_send.at[half])
    for turns in range(4):
        for step in range(1, 4):
            x_copy(turns, step).wait_send()
    for load in loads[8:]:
        load.wait()

    seven = lgot_ref.at[pl.ds(0, 7)]
    pltpu.make_async_copy(seven, seven, l_recv).wait()
    upper = lax.broadcasted_iota(jnp.int32, (8, TILES), 0) < 4
    real, imag = [], []
    for h in range(4):
        even, odd = (
            jnp.concatenate([piece[:8], piece[8:]], axis=1)
            for piece in (lgot_ref[2 * h].astype(F32), lgot_ref[2 * h + 1].astype(F32))
        )
        real.append(jnp.where(upper, even, pltpu.roll(odd, 4, 0)))
        imag.append(jnp.where(upper, pltpu.roll(even, 4, 0), odd))
    grid = jnp.concatenate(real + imag, axis=0).astype(BF16)
    result = column_transform(grid, wide_ref, twist_ref, last_ref)
    for part in range(2):
        for k in range(4):
            out_ref[pl.ds(k * 2 + part, SUB, stride=8), :] = result[
                part * 32 : part * 32 + 32, k * 128 : k * 128 + 128
            ]
    pltpu.make_async_copy(seven, seven, l_send).wait()


def on_device(visibilities, offsets, frequencies, taper_curve, owner_index, tile_index):
    rows, cols, wide, twist, last = (jnp.asarray(table) for table in make_tables())
    operands = (
        visibilities,
        offsets.reshape(64, 64),
        frequencies.reshape(1, 16),
        taper_curve.reshape(1, SUB),
        owner_index.reshape(1, 32),
        tile_index.reshape(1, 32),
        rows,
        cols,
        wide,
        twist,
        last,
    )
    result = pl.pallas_call(
        kernel,
        out_shape=pltpu.VMEM((256, 128), F32),
        in_specs=[pl.BlockSpec(memory_space=pl.ANY)] * len(operands),
        out_specs=pl.BlockSpec(memory_space=pltpu.VMEM),
        scratch_shapes=[pltpu.VMEM(operand.shape, operand.dtype) for operand in operands]
        + [
            pltpu.VMEM((2, 64, 128), F32),
            pltpu.VMEM((2, 8, 584, 128), F32),
            pltpu.VMEM((2, 2, 64, 1024), F32),
            pltpu.VMEM((256, 1024), BF16),
            pltpu.VMEM((256, 1024), BF16),
            pltpu.VMEM((256, 1024), BF16),
            pltpu.VMEM((256, 1024), BF16),
            pltpu.VMEM((2048, 256), BF16),
            pltpu.VMEM((1, 128), F32),
            pltpu.VMEM((16, 1, 128), F32),
            pltpu.VMEM((16, 128), BF16),
            pltpu.VMEM((16, 16, 128), BF16),
            pltpu.VMEM((2, 16, 16, 128), BF16),
            pltpu.VMEM((2, 16, 16, 128), BF16),
            pltpu.VMEM((16 * 17, 128), F32),
            pltpu.VMEM((2, 16, 16, 128), BF16),
            pltpu.VMEM((2, 16, 16, 128), BF16),
            pltpu.VMEM((2, TILES, 4096), BF16),
            pltpu.VMEM((2, 256, 4096), BF16),
            pltpu.VMEM((4, 3, 16, TILES), BF16),
            pltpu.VMEM((4, 3, 16, TILES), BF16),
            pltpu.VMEM((4, 2, 16, 256), BF16),
            pltpu.VMEM((8, 16, 256), BF16),
            pltpu.SemaphoreType.DMA((len(operands),)),
        ]
        + [pltpu.SemaphoreType.DMA] * 4
        + [pltpu.SemaphoreType.DMA((2,))] * 4
        + [pltpu.SemaphoreType.DMA((4, 3))] * 2
        + [pltpu.SemaphoreType.DMA] * 2,
        compiler_params=pltpu.CompilerParams(
            collective_id=0, has_side_effects=True, vmem_limit_bytes=60 * 1024 * 1024
        ),
    )(*operands)
    return result.reshape(128, 2, 128).transpose(1, 0, 2).reshape(1, 1, 2, GC)


def solution(mesh):
    in_specs = (
        P(("bl", "row", "col"), None, None),
        P(("bl", "row", "col"), None, None),
        P(),
        P(),
        P(("bl", "row", "col"), None),
        P(("bl", "row", "col")),
    )
    out_specs = P("row", ("bl", "col"), None, None)
    return jax.shard_map(
        on_device, mesh=mesh, in_specs=in_specs, out_specs=out_specs, check_vma=False
    )
```
